32 devices in a mesh: grp: 4 (over y, core), wide: 8 (over z, x).
Axes of the slice: x: 2, y: 2, z: 4, core: 2. Of those that a mesh axis runs over, the one named last changes fastest.
Arguments:
- tokens: bfloat16 [256, 256, 128], P(('grp', 'wide')), may hold values from -6 to 6
- episode_length: int32 [256], P(('grp', 'wide')), may hold values from 1 to 2048, as said below
- window_start: int32 [256], P(('grp', 'wide')), may hold values from 0 to 1792, as said below
- attn_gain: bfloat16 [128], P('wide'), may hold values from 0.5 to 1.5
- attn_shift: bfloat16 [128], P('wide'), may hold values from -3 to 3
- qkv_weight: bfloat16 [128, 384], P('wide'), may hold values from -0.5 to 0.5
- query_bias: bfloat16 [128], P('wide'), may hold values from -3 to 3
- value_bias: bfloat16 [128], P('wide'), may hold values from -3 to 3
- out_weight: bfloat16 [128, 128], P('wide'), may hold values from -2 to 2
- out_bias: bfloat16 [128], P('wide'), may hold values from -3 to 3
- mlp_gain: bfloat16 [128], P('wide'), may hold values from 0.5 to 1.5
- mlp_shift: bfloat16 [128], P('wide'), may hold values from -3 to 3
- up_weight: bfloat16 [128, 512], P('wide'), may hold values from -0.5 to 0.5
- up_bias: bfloat16 [512], P('wide'), may hold values from -3 to 3
- down_weight: bfloat16 [512, 128], P('wide'), may hold values from -0.25 to 0.25
- down_bias: bfloat16 [128], P('wide'), may hold values from -3 to 3
- cotangent: bfloat16 [256, 256, 128], P(('grp', 'wide')), may hold values from -6 to 6
Outputs:
- layer_out: float32 [256, 256, 128], P(('grp', 'wide'))
- tokens_grad: float32 [256, 256, 128], P(('grp', 'wide'))
- attn_gain_grad: float32 [128], P('wide')
- attn_shift_grad: float32 [128], P('wide')
- qkv_weight_grad: float32 [128, 384], P('wide')
- query_bias_grad: float32 [128], P('wide')
- value_bias_grad: float32 [128], P('wide')
- out_weight_grad: float32 [128, 128], P('wide')
- out_bias_grad: float32 [128], P('wide')
- mlp_gain_grad: float32 [128], P('wide')
- mlp_shift_grad: float32 [128], P('wide')
- up_weight_grad: float32 [128, 512], P('wide')
- up_bias_grad: float32 [512], P('wide')
- down_weight_grad: float32 [512, 128], P('wide')
- down_bias_grad: float32 [128], P('wide')
The draws below stay inside these ranges and needn't reach their ends.
Inputs may be any that keep to these rules, and one draw needn't show every extreme that they name: `episode_length`: the number of steps of the episode from which each window is cut. `window_start`: a multiple of 256 below the episode_length of the same window.
All inputs are finite; a program needn't handle non-finite values.
Results may differ from the reference program's by a relative error of at most 0.012.
Values may be sent and summed in bfloat16 or wider, within the bound.
No kernel may reach another device: no remote copies, remote signals or barrier semaphores. Data moves between devices by JAX's collectives and lax.ppermute only.
A program may use at most 64 MiB of HBM per device.

```python
import math
import jax
import jax.numpy as jnp
from jax import lax

D = 128
HEADS = 4
FF = 512
SPAN = 256
WINDOWS = 256


def window_layout(key):
    first_key, second_key = jax.random.split(jax.random.fold_in(key, 17))
    lengths = jax.random.randint(first_key, (WINDOWS,), 1, 8 * SPAN + 1)
    lengths = lengths.at[0].set(8 * SPAN).at[1].set(1)
    window_count = (lengths + SPAN - 1) // SPAN
    picks = jax.random.randint(second_key, (WINDOWS,), 0, 1 << 20) % window_count
    picks = picks.at[0].set(7).at[1].set(0)
    return (lengths.astype(jnp.int32), (picks * SPAN).astype(jnp.int32))


def draw_episode_length(key, part):
    lengths, starts = window_layout(key)
    return lengths


def draw_window_start(key, part):
    lengths, starts = window_layout(key)
    return starts


def level_of(stream_key, shape, cuts, smallest, high):
    factor_of = 1.0
    for axis_at, shards_of in cuts:
        draws = jax.random.uniform(jax.random.fold_in(jax.random.fold_in(stream_key, 6), axis_at), (shards_of,), jnp.float32, smallest / len(cuts), high / len(cuts))
        factor_of = factor_of * jnp.repeat(jnp.exp(draws), shape[axis_at] // shards_of).reshape((-1,) + (1,) * (len(shape) - 1 - axis_at))
    return factor_of


def normal_values(stream_key, extent, width, reach, shards=(), held_as=jnp.bfloat16):
    level = level_of(stream_key, extent, shards, -0.22, 0.18) if shards else 1.0
    values = jax.random.normal(stream_key, extent, jnp.float32) * width * level
    return jnp.minimum(jnp.maximum(values, -reach), reach).astype(held_as)


def setup_inputs(seed: int = 0) -> dict:
    key_of = jax.random.split(jax.random.key(seed), 18)
    tokens = normal_values(key_of[0], (WINDOWS, SPAN, D), 1.0, 6.0, ((0, 32),))
    episode_length = draw_episode_length(jax.random.fold_in(key_of[17], 71), 0)
    window_start = draw_window_start(jax.random.fold_in(key_of[17], 71), 0)
    attn_gain = jnp.clip(1.0 + 0.1 * jax.random.normal(key_of[3], (D,), jnp.float32), 0.5, 1.5).astype(jnp.bfloat16)
    attn_shift = normal_values(key_of[4], (D,), 0.3, 3.0, ((0, 8),))
    qkv_weight = normal_values(key_of[5], (D, 3 * D), D ** -0.5, 0.5, ((0, 8),))
    query_bias = normal_values(key_of[6], (D,), 0.3, 3.0, ((0, 8),))
    value_bias = normal_values(key_of[7], (D,), 0.3, 3.0, ((0, 8),))
    out_weight = normal_values(key_of[8], (D, D), (D // 16) ** -0.5, 2.0, ((0, 8),))
    out_bias = normal_values(key_of[9], (D,), 0.3, 3.0, ((0, 8),))
    mlp_gain = jnp.clip(1.0 + 0.1 * jax.random.normal(key_of[10], (D,), jnp.float32), 0.5, 1.5).astype(jnp.bfloat16)
    mlp_shift = normal_values(key_of[11], (D,), 0.3, 3.0, ((0, 8),))
    up_weight = normal_values(key_of[12], (D, FF), D ** -0.5, 0.5, ((0, 8),))
    up_bias = normal_values(key_of[13], (FF,), 0.3, 3.0, ((0, 8),))
    down_weight = normal_values(key_of[14], (FF, D), FF ** -0.5, 0.25, ((0, 8),))
    down_bias = normal_values(key_of[15], (D,), 0.3, 3.0, ((0, 8),))
    cotangent = normal_values(key_of[16], (WINDOWS, SPAN, D), 1.0, 6.0, ((0, 32),))
    return {"tokens": tokens, "episode_length": episode_length, "window_start": window_start, "attn_gain": attn_gain, "attn_shift": attn_shift, "qkv_weight": qkv_weight, "query_bias": query_bias, "value_bias": value_bias, "out_weight": out_weight, "out_bias": out_bias, "mlp_gain": mlp_gain, "mlp_shift": mlp_shift, "up_weight": up_weight, "up_bias": up_bias, "down_weight": down_weight, "down_bias": down_bias, "cotangent": cotangent}


@jax.custom_vjp
def low(v):
    return lax.optimization_barrier(v.astype(jnp.bfloat16)).astype(jnp.float32)

@jax.custom_vjp
def low_back(v):
    return v

def low_keep(v):
    return (low(v), None)

def low_pass(kept, grad):
    return (grad,)

def back_keep(v):
    return (v, None)

def back_low(kept, grad):
    return (low(grad),)
low.defvjp(low_keep, low_pass)
low_back.defvjp(back_keep, back_low)
EPS = 1e-05
CUBIC = 0.044715
TANH_SCALE = math.sqrt(2.0 / math.pi)
NEG_FILL = -1e+30
HIGH = lax.Precision.HIGHEST

def gelu_tanh(values):
    return 0.5 * values * (1.0 + jnp.tanh(TANH_SCALE * (values + CUBIC * values * values * values)))

def norm_rows(values, norm_gain, norm_shift):
    center = lax.optimization_barrier(jnp.mean(values, axis=-1, keepdims=True))
    offset = values - center
    spread = lax.optimization_barrier(jnp.mean(offset * offset, axis=-1, keepdims=True))
    return offset * lax.rsqrt(spread + EPS) * norm_gain + norm_shift

def layer_pass(inputs, valid_count, params):
    attn_gain, attn_shift, qkv_weight, query_bias, value_bias, out_weight, out_bias, mlp_gain, mlp_shift, up_weight, up_bias, down_weight, down_bias = params
    windows_now = inputs.shape[0]
    head_size = D // HEADS
    positions = jnp.arange(SPAN)
    causal = positions[None, :] <= positions[:, None]
    allowed = causal[None, None, :, :] & (positions[None, None, None, :] < valid_count[:, None, None, None])
    attn_normed = low(norm_rows(inputs, attn_gain, attn_shift))
    bias_all = jnp.concatenate([query_bias, jnp.zeros((D,), jnp.float32), value_bias])
    projected = low(low_back(jnp.einsum('wtd,df->wtf', attn_normed, qkv_weight, precision=HIGH) + bias_all))
    heads_view = projected.reshape(windows_now, SPAN, 3, HEADS, head_size)
    query_heads = heads_view[:, :, 0]
    key_heads = heads_view[:, :, 1]
    value_heads = heads_view[:, :, 2]
    scores = low_back(jnp.einsum('wqhe,wkhe->whqk', query_heads, key_heads, precision=HIGH) * head_size ** (-0.5))
    masked = jnp.where(allowed, scores, NEG_FILL)
    row_max = lax.optimization_barrier(jnp.max(masked, axis=-1, keepdims=True))
    log_total = row_max + jnp.log(lax.optimization_barrier(jnp.sum(jnp.exp(masked - row_max), axis=-1, keepdims=True)))
    probs = low(jnp.exp(masked - log_total))
    attended = jnp.einsum('whqk,wkhe->wqhe', probs, value_heads, precision=HIGH)
    attended = low(low_back(attended.reshape(windows_now, SPAN, D)))
    mid = inputs + low_back(jnp.einsum('wtd,df->wtf', attended, out_weight, precision=HIGH) + out_bias)
    mlp_normed = low(norm_rows(mid, mlp_gain, mlp_shift))
    hidden = low_back(jnp.einsum('wtd,df->wtf', mlp_normed, up_weight, precision=HIGH) + up_bias)
    activated = low(gelu_tanh(hidden))
    return mid + low_back(jnp.einsum('wtf,fd->wtd', activated, down_weight, precision=HIGH) + down_bias)

def add_pair(running, extra):
    return running + extra

def reference(tokens, episode_length, window_start, attn_gain, attn_shift, qkv_weight, query_bias, value_bias, out_weight, out_bias, mlp_gain, mlp_shift, up_weight, up_bias, down_weight, down_bias, cotangent):
    valid_count = jnp.clip(episode_length - window_start, 1, SPAN).astype(jnp.int32)
    params = tuple((weight.astype(jnp.float32) for weight in (attn_gain, attn_shift, qkv_weight, query_bias, value_bias, out_weight, out_bias, mlp_gain, mlp_shift, up_weight, up_bias, down_weight, down_bias)))
    positions = jnp.arange(SPAN)
    live_rows = (positions[None, :] < valid_count[:, None]).astype(jnp.float32)
    upstream = cotangent.astype(jnp.float32) * live_rows[:, :, None]
    group_size = math.gcd(WINDOWS, 16)
    group_count = WINDOWS // group_size
    inputs = tokens.astype(jnp.float32).reshape(group_count, group_size, SPAN, D)
    counts = valid_count.reshape(group_count, group_size)
    seeds = upstream.reshape(group_count, group_size, SPAN, D)

    def advance(totals, batch_item):
        block_in, block_count, block_seed = batch_item

        def forward(values, weights):
            return layer_pass(values, block_count, weights)
        block_out, pull = jax.vjp(forward, block_in, params)
        block_grad, weight_grads = pull(block_seed)
        totals = jax.tree.map(add_pair, totals, weight_grads)
        return (totals, (block_out, block_grad))
    zeros = tuple((jnp.zeros_like(weight) for weight in params))
    totals, (outs_all, grads_all) = lax.scan(advance, zeros, (inputs, counts, seeds))
    grad_attn_gain, grad_attn_shift, grad_qkv, grad_query_bias, grad_value_bias, grad_out_weight, grad_out_bias, grad_mlp_gain, grad_mlp_shift, grad_up_weight, grad_up_bias, grad_down_weight, grad_down_bias = totals
    return (outs_all.reshape(WINDOWS, SPAN, D), grads_all.reshape(WINDOWS, SPAN, D), grad_attn_gain, grad_attn_shift, grad_qkv, grad_query_bias, grad_value_bias, grad_out_weight, grad_out_bias, grad_mlp_gain, grad_mlp_shift, grad_up_weight, grad_up_bias, grad_down_weight, grad_down_bias)
```

```python
import math
import functools

import jax
import jax.numpy as jnp
from jax import lax
from jax.experimental import pallas as pl
from jax.experimental.pallas import tpu as pltpu
from jax.sharding import PartitionSpec as P

HEADS = 4
EPS = 1e-05
CUBIC = 0.044715
TANH_SCALE = math.sqrt(2.0 / math.pi)
NEG_FILL = -1e30
LOG2E = math.log2(math.e)
f32, bf16 = jnp.float32, jnp.bfloat16
PIECES = 8
PIECE_ROWS = 208
GRAD_ROWS = 224

def nn(a, b):
    return lax.dot_general(a, b, (((1,), (0,)), ((), ())), preferred_element_type=f32)

def nt(a, b):
    return lax.dot_general(a, b, (((1,), (1,)), ((), ())), preferred_element_type=f32)

def norm(v):
    d = v.shape[0]
    off = v - jnp.sum(v, axis=0, keepdims=True) * (1.0 / d)
    r = lax.rsqrt(jnp.sum(off * off, axis=0, keepdims=True) * (1.0 / d) + EPS)
    return off * r, r

def norm_back(dy, gain, n, r):
    d = dy.shape[0]
    g = dy * gain
    mg = jnp.sum(g, axis=0, keepdims=True) * (1.0 / d)
    mgn = jnp.sum(g * n, axis=0, keepdims=True) * (1.0 / d)
    return r * (g - mg - n * mgn)

def layer_kernel(where_ref, len_ref, start_ref, wg_ref, x_ref, ct_ref,
                 lo_ref, tg_ref, keep_ref, send_ref,
                 wqkv, wqkvT, wo, woT, wup, wupT, wd, wdT, cols, dbias,
                 aqkv, ao, aup, ad, alng, bias0, bias1, *, wps, steps):
    step = pl.program_id(0)
    me, core = where_ref[0], where_ref[1]
    T, D = x_ref.shape[1], x_ref.shape[2]
    H = T // 2
    E = D // HEADS
    FF = wup.shape[1]
    scale = E ** -0.5

    @pl.when(step == 0)
    def _():
        vec = jnp.zeros((16, D), f32)
        for o in range(PIECES):
            s = jnp.bitwise_xor(me, o)
            rows = slice(16 * o, 16 * o + 16)
            for b in range(3):
                wqkv[rows, D * b:D * b + D] = wg_ref[s, 16 * b:16 * b + 16, :]
            wo[rows, :] = wg_ref[s, 48:64, :]
            for b in range(4):
                wup[rows, D * b:D * b + D] = wg_ref[s, 64 + 16 * b:80 + 16 * b, :]
            wd[64 * o:64 * o + 64, :] = wg_ref[s, 128:192, :]
            vec = vec + wg_ref[s, 192:208, :].astype(f32)
        dbias[...] = jnp.broadcast_to(vec[7:8, :], (8, D))
        vecT = jnp.concatenate([vec, jnp.zeros((D - 16, D), f32)], 0).T
        lane = lax.broadcasted_iota(jnp.int32, (D, 16), 1)
        def col(k):
            return jnp.where(lane == k, vecT[:, 0:16], 0.0).astype(bf16)
        def full(k):
            return jnp.broadcast_to(vecT[:, k:k + 1], (D, T))
        for b in range(3):
            wqkvT[D * b:D * b + D, 0:D] = wqkv[:, D * b:D * b + D].T
        wqkvT[0:D, D:D + 16] = col(2)
        wqkvT[D:2 * D, D:D + 16] = jnp.zeros((D, 16), bf16)
        wqkvT[2 * D:3 * D, D:D + 16] = col(3)
        woT[:, 0:D] = wo[...].T
        woT[:, D:D + 16] = col(4)
        for b in range(4):
            wupT[D * b:D * b + D, 0:D] = wup[:, D * b:D * b + D].T
            wupT[D * b:D * b + D, D:D + 16] = col(8 + b)
            wdT[:, D * b:D * b + D] = wd[D * b:D * b + D, :].T
        cols[0] = full(0)
        cols[1] = full(1)
        cols[2] = full(5)
        cols[3] = full(6)
        for ref in (aqkv, ao, aup, ad, alng):
            ref[...] = jnp.zeros(ref.shape, f32)

    ones = jnp.ones((16, T), bf16)
    gs = []
    for w in range(wps):
        idx = step * wps + w
        valid = jnp.clip(len_ref[idx] - start_ref[idx], 1, T)
        j0 = lax.broadcasted_iota(jnp.int32, (H, H), 0)
        i0 = lax.broadcasted_iota(jnp.int32, (H, H), 1)
        bias0[w] = jnp.where((j0 <= i0) & (j0 < valid), 0.0, NEG_FILL)
        bias1[w, 0:H] = jnp.where(j0 < valid, 0.0, NEG_FILL)
        bias1[w, H:T] = jnp.where((j0 <= i0) & (j0 + H < valid), 0.0, NEG_FILL)
        xT = x_ref[w].astype(f32).T
        n1, r1 = norm(xT)
        a1 = (n1 * cols[0] + cols[1]).astype(bf16)
        a1g = jnp.concatenate([a1, ones], 0)
        pT = nn(wqkvT[...], a1g).astype(bf16)
        qT, kT, vT = pT[0:D], pT[D:2 * D], pT[2 * D:3 * D]
        krow, vrow = kT.T, vT.T

        def spread(m, h):
            parts = []
            if h > 0:
                parts.append(jnp.zeros((E * h, T), bf16))
            parts.append(m[E * h:E * h + E])
            if h < HEADS - 1:
                parts.append(jnp.zeros((E * (HEADS - 1 - h), T), bf16))
            return jnp.concatenate(parts, 0)

        probs, probs_low, att = [], [], []
        c = scale * LOG2E
        for h in range(HEADS):
            S = nn(krow, spread(qT, h))
            ps = []
            for t in (S[0:H, 0:H] * c + bias0[w], S[:, H:T] * c + bias1[w]):
                e = jnp.exp2(t - jnp.max(t, axis=0, keepdims=True))
                ps.append(e * (1.0 / jnp.sum(e, axis=0, keepdims=True)))
            low0 = jnp.concatenate([ps[0].astype(bf16), jnp.zeros((H, H), bf16)], 0)
            low = jnp.concatenate([low0, ps[1].astype(bf16)], 1)
            probs.append(ps)
            probs_low.append(low)
            att.append(nn(vT[E * h:E * h + E], low))
        attT = jnp.concatenate(att, 0).astype(bf16)
        attg = jnp.concatenate([attT, ones], 0)
        mid = xT + nn(woT[...], attg)
        n2, r2 = norm(mid)
        a2 = (n2 * cols[2] + cols[3]).astype(bf16)
        a2g = jnp.concatenate([a2, ones], 0)
        live = (lax.broadcasted_iota(jnp.int32, (1, T), 1) < valid).astype(f32)
        upT = ct_ref[w].astype(f32).T * live
        upb = upT.astype(bf16)
        acts, hgs = [], []
        for b in range(FF // D):
            blk = slice(D * b, D * b + D)
            hid = nn(wupT[blk, :], a2g)
            v2 = hid * hid
            s = 0.5 * jnp.tanh(hid * (TANH_SCALE + (TANH_SCALE * CUBIC) * v2)) + 0.5
            act = hid * s
            acts.append(act.astype(bf16))
            gp = s + act * (1.0 - s) * (2 * TANH_SCALE + (6 * TANH_SCALE * CUBIC) * v2)
            hgs.append((nn(wd[blk, :], upb) * gp).astype(bf16))
        act = jnp.concatenate(acts, 0)
        hg = jnp.concatenate(hgs, 0)
        lo_ref[w] = (mid + nn(wdT[...], act)).T + dbias[0:1, :]
        dn2 = nn(wup[...], hg)
        alng[0] += dn2 * n2
        alng[1] += dn2
        midg = upT + norm_back(dn2, cols[2], n2, r2)
        bg = midg.astype(bf16)
        daT = nn(wo[...], bg).astype(bf16)
        dq, dk, dv = [], [], []
        for h in range(HEADS):
            blk = slice(E * h, E * h + E)
            dP = nn(vrow, spread(daT, h))
            ds = []
            for p, g in zip(probs[h], (dP[0:H, 0:H], dP[:, H:T])):
                inner = jnp.sum(p * g, axis=0, keepdims=True)
                ds.append((p * (g - inner)).astype(bf16))
            ds0 = jnp.concatenate([ds[0], jnp.zeros((H, H), bf16)], 0)
            dS = jnp.concatenate([ds0, ds[1]], 1)
            dq.append(nn(kT[blk], dS) * scale)
            dk.append(nt(qT[blk], dS) * scale)
            dv.append(nt(daT[blk], probs_low[h]))
        pg = jnp.concatenate(dq + dk + dv, 0).astype(bf16)
        dn1 = nn(wqkv[...], pg)
        alng[2] += dn1 * n1
        alng[3] += dn1
        tg_ref[w] = (midg + norm_back(dn1, cols[0], n1, r1)).T
        gs.append((a1g, pg, attg, bg, a2g, hg, jnp.concatenate([act, ones], 0), upb))
    cat = [jnp.concatenate([g[k] for g in gs], 1) if wps > 1 else gs[0][k] for k in range(8)]
    aqkv[...] += nt(cat[0], cat[1])
    ao[...] += nt(cat[2], cat[3])
    aup[...] += nt(cat[4], cat[5])
    ad[...] += nt(cat[6], cat[7])

    @pl.when(step == steps - 1)
    def _():
        def row(k):
            a = alng[k]
            a = a[:, 0:H] + a[:, H:T]
            return jnp.sum(a.T, axis=0, keepdims=True)
        vec = jnp.concatenate(
            [row(2), row(3), aqkv[D:D + 1, 0:D], aqkv[D:D + 1, 2 * D:3 * D], ao[D:D + 1, :],
             row(0), row(1), ad[FF:FF + 1, :]]
            + [aup[D:D + 1, D * b:D * b + D] for b in range(4)] + [jnp.zeros((4, D), f32)], 0)
        high = vec.astype(bf16)
        low = (vec - high.astype(f32)).astype(bf16)
        for k in range(PIECES // 2):
            for ref, half in ((keep_ref, core), (send_ref, 1 - core)):
                o = jnp.bitwise_xor(me, half * (PIECES // 2) + k)
                r16 = pl.ds(pl.multiple_of(o * 16, 16), 16)
                for b in range(3):
                    ref[k, 16 * b:16 * b + 16, :] = aqkv[r16, D * b:D * b + D].astype(bf16)
                ref[k, 48:64, :] = ao[r16, :].astype(bf16)
                for b in range(4):
                    ref[k, 64 + 16 * b:80 + 16 * b, :] = aup[r16, D * b:D * b + D].astype(bf16)
                ref[k, 128:192, :] = ad[pl.ds(pl.multiple_of(o * 64, 64), 64), :].astype(bf16)
                ref[k, 192:208, :] = high
                ref[k, 208:224, :] = low

def layer(where, lens, starts, wg, x, ct, wps=2):

    nw, T, D = x.shape
    FF = 512
    steps = nw // wps
    vm = lambda s, d: pltpu.VMEM(s, d)
    smem = pl.BlockSpec(memory_space=pltpu.SMEM)
    win = pl.BlockSpec((wps, T, D), lambda i: (i, 0, 0))
    whole = lambda s: pl.BlockSpec(s, lambda i: (0,) * len(s))
    half = (PIECES // 2, GRAD_ROWS, D)
    return pl.pallas_call(
        functools.partial(layer_kernel, wps=wps, steps=steps),
        grid=(steps,),
        in_specs=[smem, smem, smem, whole(wg.shape), win, win],
        out_specs=[win, win, whole(half), whole(half)],
        out_shape=[jax.ShapeDtypeStruct(x.shape, f32)] * 2 + [jax.ShapeDtypeStruct(half, bf16)] * 2,
        scratch_shapes=[
            vm((D, 3 * D), bf16), vm((3 * D, D + 16), bf16), vm((D, D), bf16), vm((D, D + 16), bf16),
            vm((D, FF), bf16), vm((FF, D + 16), bf16), vm((FF, D), bf16), vm((D, FF), bf16),
            vm((4, D, T), f32), vm((8, D), f32),
            vm((D + 16, 3 * D), f32), vm((D + 16, D), f32), vm((D + 16, FF), f32), vm((FF + 16, D), f32),
            vm((4, D, T), f32), vm((wps, T // 2, T // 2), f32), vm((wps, T, T // 2), f32)],
        compiler_params=pltpu.CompilerParams(vmem_limit_bytes=48 << 20, dimension_semantics=("arbitrary",)),
        name="layer",
    )(where, lens, starts, wg, x, ct)


VMEM = pl.BlockSpec(memory_space=pltpu.VMEM)
SMEM = pl.BlockSpec(memory_space=pltpu.SMEM)
SMALL = pltpu.CompilerParams(vmem_limit_bytes=16 << 20)


def pack_kernel(where_ref, gain_a, shift_a, qkv, query, value, outw, outb, gain_m, shift_m, upw, upb, downw, downb, out_ref):
    me = where_ref[0]
    D = out_ref.shape[1]
    for b in range(3):
        out_ref[16 * b:16 * b + 16, :] = qkv[:, D * b:D * b + D]
    out_ref[48:64, :] = outw[...]
    for b in range(4):
        out_ref[64 + 16 * b:80 + 16 * b, :] = upw[:, D * b:D * b + D]
    out_ref[128:192, :] = downw[...]
    total = jnp.zeros((16, D), f32)
    row = lax.broadcasted_iota(jnp.int32, (16, D), 0)
    lane16 = lax.broadcasted_iota(jnp.int32, (16, D), 1)
    spot16 = (lane16 == row + 16 * me).astype(bf16)
    r64 = lax.broadcasted_iota(jnp.int32, (64, D), 0)
    l64 = lax.broadcasted_iota(jnp.int32, (64, D), 1)
    spot64 = (l64 == r64 + 64 * jnp.bitwise_and(me, 1)).astype(bf16)
    for k, ref in enumerate((gain_a, shift_a, query, value, outb, gain_m, shift_m, downb)):
        v = jnp.broadcast_to(ref[...].astype(f32).reshape(1, 16), (16, 16)).astype(bf16)
        total = total + jnp.where(row == k, nn(v, spot16), 0.0)
    v = jnp.broadcast_to(upb[...].astype(f32).reshape(1, 64), (16, 64)).astype(bf16)
    total = total + jnp.where(row == 8 + lax.shift_right_logical(me, 1), nn(v, spot64), 0.0)
    out_ref[192:208, :] = total.astype(bf16)


def split_add(parts):
    total = parts[0].astype(f32)
    for p in parts[1:]:
        total = total + p.astype(f32)
    vec = total[192:208] + total[208:224]
    high = vec.astype(bf16)
    low = (vec - high.astype(f32)).astype(bf16)
    return total[0:192], vec, high, low


def pair_kernel(keep_ref, got_ref, *out_refs):
    for k, ref in enumerate(out_refs):
        main, vec, high, low = split_add([keep_ref[k], got_ref[k]])
        ref[0:192, :] = main.astype(bf16)
        ref[192:208, :] = high
        ref[208:224, :] = low


def merge_kernel(where_ref, own_ref, r0, r1, r2, r3, out_ref):
    first = jnp.where(where_ref[1] == 0, own_ref[...].astype(f32), r0[...].astype(f32))
    main, vec, high, low = split_add([first, r1[...], r2[...], r3[...]])
    out_ref[0:192, :] = main.astype(bf16)
    out_ref[192:208, :] = high
    out_ref[208:224, :] = low


def finish_kernel(where_ref, all_ref, gain_a, shift_a, qkv, query, value, outw, outb, gain_m, shift_m, upw, upb, downw, downb):
    me = where_ref[0]
    D = all_ref.shape[2]
    main, vec, high, low = split_add([all_ref[k] for k in range(all_ref.shape[0])])
    for b in range(3):
        qkv[:, D * b:D * b + D] = main[16 * b:16 * b + 16]
    outw[...] = main[48:64]
    for b in range(4):
        upw[:, D * b:D * b + D] = main[64 + 16 * b:80 + 16 * b]
    downw[...] = main[128:192]
    turned = pltpu.roll(vec, jnp.bitwise_and(D - 16 * me, D - 1), 1)
    for k, ref in enumerate((gain_a, shift_a, query, value, outb, gain_m, shift_m, downb)):
        ref[...] = turned[k:k + 1, 0:16].reshape(16)
    row = lax.broadcasted_iota(jnp.int32, (16, D), 0)
    half = jnp.sum(jnp.where(row == 8 + lax.shift_right_logical(me, 1), vec, 0.0), axis=0, keepdims=True)
    half = jnp.where(jnp.bitwise_and(me, 1) == 0, half[:, 0:64], half[:, 64:128])
    upb[...] = half.reshape(64)


def per_device(tokens, episode_length, window_start, *rest):
    params, cotangent = rest[:13], rest[13]
    D = tokens.shape[2]
    grp, wide = lax.axis_size("grp"), lax.axis_size("wide")
    me = lax.axis_index("wide").astype(jnp.int32)
    core = jnp.bitwise_and(lax.axis_index("grp").astype(jnp.int32), 1)
    where = jnp.stack([me, core])
    axes = ("grp", "wide")

    def across(core_slots):
        pairs = []
        for g in range(grp):
            s = core_slots[g % 2]
            if s:
                pairs += [(g * wide + i, g * wide + (i ^ s)) for i in range(wide)]
        return pairs

    swap = [(g * wide + i, (g ^ 1) * wide + i) for g in range(grp) for i in range(wide)]
    upward = [(g * wide + i, (g ^ 1) * wide + i) for g in range(1, grp, 2) for i in range(wide)]
    piece = pl.pallas_call(
        pack_kernel, in_specs=[SMEM] + [VMEM] * 13, out_specs=VMEM,
        out_shape=jax.ShapeDtypeStruct((PIECE_ROWS, D), bf16), compiler_params=SMALL, name="pack",
    )(where, *params)
    hops = [across((k, 4 + k)) for k in range(4)]
    direct = [lax.ppermute(piece, axes, hops[k]) for k in range(4)]
    other = [lax.ppermute(direct[0], axes, upward)] + [lax.ppermute(direct[k], axes, swap) for k in (1, 2, 3)]
    mine = jnp.stack([jnp.where(core == 0, piece, direct[0])] + direct[1:])
    theirs = jnp.stack([jnp.where(core == 0, other[0], piece)] + other[1:])
    low_half = jnp.where(core == 0, mine, theirs)
    high_half = jnp.where(core == 0, theirs, mine)
    slots = jnp.concatenate([low_half, high_half], 0)
    layer_out, tokens_grad, keep, send = layer(where, episode_length, window_start, slots, tokens, cotangent)
    got = lax.ppermute(send, axes, swap)
    shape = jax.ShapeDtypeStruct((GRAD_ROWS, D), bf16)
    pairs = pl.pallas_call(
        pair_kernel, in_specs=[VMEM] * 2, out_specs=[VMEM] * 4, out_shape=[shape] * 4, compiler_params=SMALL, name="pair",
    )(keep, got)
    came = [lax.ppermute(pairs[k], axes, hops[k]) for k in range(4)]
    merged = pl.pallas_call(
        merge_kernel, in_specs=[SMEM] + [VMEM] * 5, out_specs=VMEM, out_shape=shape, compiler_params=SMALL, name="merge",
    )(where, pairs[0], *came)
    every = lax.all_gather(merged, "grp", axis=0, tiled=False)
    grads = pl.pallas_call(
        finish_kernel, in_specs=[SMEM, VMEM], out_specs=[VMEM] * 13,
        out_shape=[jax.ShapeDtypeStruct(p.shape, f32) for p in params], compiler_params=SMALL, name="finish",
    )(where, every)
    return (layer_out, tokens_grad, *grads)


def gathered(tokens, episode_length, window_start, *rest):
    params, cotangent = rest[:13], rest[13]
    D = tokens.shape[2]
    full = [lax.all_gather(p, "wide", axis=0, tiled=True) for p in params]
    gain_a, shift_a, qkv, query, value, outw, outb, gain_m, shift_m, upw, upb, downw, downb = full
    FF = upw.shape[1]
    lanes = jnp.arange(D) // (D // PIECES)
    spots = (lanes[None, :] == jnp.arange(PIECES)[:, None]).astype(bf16)
    vectors = jnp.stack([gain_a, shift_a, query, value, outb, gain_m, shift_m, downb])[None] * spots[:, None, :]
    where_up = (jnp.arange(FF) // (FF // PIECES))[None, :] == jnp.arange(PIECES)[:, None]
    ups = (upb[None] * where_up.astype(bf16)).reshape(PIECES, FF // D, D)

    def blocks(weight):
        cut = weight.reshape(PIECES, weight.shape[0] // PIECES, weight.shape[1] // D, D)
        return cut.transpose(0, 2, 1, 3).reshape(PIECES, -1, D)

    slots = jnp.concatenate(
        [blocks(qkv), blocks(outw), blocks(upw), blocks(downw), vectors, ups, jnp.zeros((PIECES, 4, D), bf16)], 1
    )
    where = jnp.zeros((2,), jnp.int32)
    layer_out, tokens_grad, keep, send = layer(where, episode_length, window_start, slots, tokens, cotangent)
    pieces = jnp.concatenate([keep, send], 0).astype(f32)
    vec = pieces[0, 192:208] + pieces[0, 208:224]

    def rebuilt(first, last, weight):
        cut = pieces[:, first:last].reshape(PIECES, weight.shape[1] // D, weight.shape[0] // PIECES, D)
        return cut.transpose(0, 2, 1, 3).reshape(weight.shape)

    grads = (
        vec[0], vec[1], rebuilt(0, 48, qkv), vec[2], vec[3], rebuilt(48, 64, outw), vec[4], vec[5], vec[6],
        rebuilt(64, 128, upw), vec[8:12].reshape(FF), rebuilt(128, 192, downw), vec[7],
    )
    grads = [lax.psum_scatter(g, "wide", scatter_dimension=0, tiled=True) for g in grads]
    return (layer_out, tokens_grad, *lax.psum(grads, "grp"))


def solution(mesh):
    rows = P(("grp", "wide"), None, None)
    flat = P(("grp", "wide"))
    one, two = P("wide"), P("wide", None)
    params = (one, one, two, one, one, two, one, one, one, two, one, two, one)
    fits = mesh.shape["wide"] == PIECES and mesh.shape["grp"] % 2 == 0
    return jax.shard_map(
        per_device if fits else gathered, mesh=mesh, in_specs=(rows, flat, flat, *params, rows), out_specs=(rows, rows, *params), check_vma=False
    )
```

```python
import math
import functools

import jax
import jax.numpy as jnp
from jax import lax
from jax.experimental import pallas as pl
from jax.experimental.pallas import tpu as pltpu
from jax.sharding import PartitionSpec as P

HEADS = 4
EPS = 1e-05
CUBIC = 0.044715
TANH_SCALE = math.sqrt(2.0 / math.pi)
NEG_FILL = -1e30
LOG2E = math.log2(math.e)
f32, bf16 = jnp.float32, jnp.bfloat16
PIECES = 8
PIECE_ROWS = 208
GRAD_ROWS = 224
SLOTS = ((0, 6, 5, 1), (4, 7, 2, 3))

def place():
    return lax.axis_index("wide").astype(jnp.int32), jnp.bitwise_and(lax.axis_index("grp").astype(jnp.int32), 1)


def slot_of(core, k):
    return jnp.where(core == 0, SLOTS[0][k], SLOTS[1][k])


def nn(a, b):
    return lax.dot_general(a, b, (((1,), (0,)), ((), ())), preferred_element_type=f32)

def nt(a, b):
    return lax.dot_general(a, b, (((1,), (1,)), ((), ())), preferred_element_type=f32)

def norm(v):
    d = v.shape[0]
    off = v - jnp.sum(v, axis=0, keepdims=True) * (1.0 / d)
    r = lax.rsqrt(jnp.sum(off * off, axis=0, keepdims=True) * (1.0 / d) + EPS)
    return off * r, r

def norm_back(dy, gain, n, r):
    d = dy.shape[0]
    g = dy * gain
    mg = jnp.sum(g, axis=0, keepdims=True) * (1.0 / d)
    mgn = jnp.sum(g * n, axis=0, keepdims=True) * (1.0 / d)
    return r * (g - mg - n * mgn)

def prepare_kernel(len_ref, start_ref, x_in, ct_in, x_ref, n_ref, r_ref, up_ref, mask_ref):
    count, T, D = x_in.shape
    H = T // 2
    for w in range(count):
        valid = jnp.clip(len_ref[w] - start_ref[w], 1, T)
        xT = x_in[w].astype(f32).T
        n, r = norm(xT)
        x_ref[w] = xT
        n_ref[w] = n
        r_ref[w] = jnp.broadcast_to(r, (8, T))
        live = (lax.broadcasted_iota(jnp.int32, (1, T), 1) < valid).astype(f32)
        up_ref[w] = ct_in[w].astype(f32).T * live
        j = lax.broadcasted_iota(jnp.int32, (H, H), 0)
        tri = j <= lax.broadcasted_iota(jnp.int32, (H, H), 1)
        for k, seen in enumerate((tri & (j < valid), j < valid, tri & (j + H < valid))):
            mask_ref[w, H * k:H * k + H] = jnp.where(seen, 0.0, NEG_FILL).astype(bf16)


def layer_kernel(w0, d0, d1, d2, d3, others, x_ref, n_ref, r_ref, up_ref, mask_ref,
                 lo_ref, tg_ref, keep_ref, send_ref,
                 wqkv, wqkvT, wo, woT, wup, wupT, wd, wdT, cols,
                 aqkv, ao, aup, ad, alng, *, wps, steps, group, skew, spread_out):
    step = pl.program_id(0)
    me, core = place() if spread_out else (jnp.int32(0), jnp.int32(0))
    D, T = x_ref.shape[1], x_ref.shape[2]
    H = T // 2
    E = D // HEADS
    FF = wup.shape[1]
    scale = E ** -0.5

    @pl.when(step == 0)
    def _():
        vec = jnp.zeros((16, D), f32)
        places = [(0, w0, 0), (SLOTS[1][0], d0, 0)]
        for k in (1, 2, 3):
            places += [(slot_of(core, k), (d1, d2, d3)[k - 1], 0), (slot_of(1 - core, k), others, PIECE_ROWS * k)]
        for slot, ref, at in places:
            o = jnp.bitwise_xor(me, slot)
            r16 = pl.ds(pl.multiple_of(o * 16, 16), 16)
            get = lambda first, last: ref[at + first:at + last, :]
            if ref is d0:
                get = lambda first, last: d0[first:last, :] + others[first:last, :]
            for b in range(3):
                wqkv[r16, D * b:D * b + D] = get(16 * b, 16 * b + 16)
            wo[r16, :] = get(48, 64)
            for b in range(4):
                wup[r16, D * b:D * b + D] = get(64 + 16 * b, 80 + 16 * b)
            wd[pl.ds(pl.multiple_of(o * 64, 64), 64), :] = get(128, 192)
            vec = vec + get(192, 208).astype(f32)
        vecT = jnp.concatenate([vec, jnp.zeros((D - 16, D), f32)], 0).T
        lane = lax.broadcasted_iota(jnp.int32, (D, 16), 1)
        def col(k):
            return jnp.where(lane == k, vecT[:, 0:16], 0.0).astype(bf16)
        def full(k):
            return jnp.broadcast_to(vecT[:, k:k + 1], (D, T))
        for b in range(3):
            wqkvT[D * b:D * b + D, 0:D] = wqkv[:, D * b:D * b + D].T
        wqkvT[0:D, D:D + 16] = col(2)
        wqkvT[D:2 * D, D:D + 16] = jnp.zeros((D, 16), bf16)
        wqkvT[2 * D:3 * D, D:D + 16] = col(3)
        woT[:, 0:D] = wo[...].T
        woT[:, D:D + 16] = col(4)
        for b in range(4):
            wupT[D * b:D * b + D, 0:D] = wup[:, D * b:D * b + D].T
            wupT[D * b:D * b + D, D:D + 16] = col(8 + b)
            wdT[:, D * b:D * b + D] = wd[D * b:D * b + D, :].T
        wdT[:, FF:FF + 16] = col(7)
        cols[0] = full(0)
        cols[1] = full(1)
        cols[2] = full(5)
        cols[3] = full(6)
        for ref in (aqkv, ao, aup, ad, alng):
            ref[...] = jnp.zeros(ref.shape, f32)

    ones = jnp.ones((16, T), bf16)
    eye2 = (lax.broadcasted_iota(jnp.int32, (H, T), 0) == jnp.bitwise_and(lax.broadcasted_iota(jnp.int32, (H, T), 1), H - 1)).astype(f32).astype(bf16)

    def spread(m, h):
        parts = []
        if h > 0:
            parts.append(jnp.zeros((E * h, m.shape[1]), bf16))
        parts.append(m)
        if h < HEADS - 1:
            parts.append(jnp.zeros((E * (HEADS - 1 - h), m.shape[1]), bf16))
        return jnp.concatenate(parts, 0)

    def window(w):
        idx = step * wps + w
        n1, r1 = n_ref[idx], r_ref[idx, 0:1]
        a1 = (n1 * cols[0] + cols[1]).astype(bf16)
        a1g = jnp.concatenate([a1, ones], 0)
        yield
        qT = (nn(wqkvT[0:D, :], a1g) * (scale * LOG2E)).astype(bf16)
        kT = nn(wqkvT[D:2 * D, :], a1g).astype(bf16)
        vT = nn(wqkvT[2 * D:3 * D, :], a1g).astype(bf16)
        yield
        krow, vrow = kT.T, vT.T
        left = (jnp.concatenate([krow[0:H], mask_ref[idx, 0:H]], 1), jnp.concatenate([krow, mask_ref[idx, H:H + T]], 1))
        vrow1 = jnp.concatenate([vrow, jnp.ones((T, 16), bf16)], 1)
        yield
        exps, lows, att, invs = [], [], [], []
        for h in range(0, HEADS, 2):
            strips = []
            for k in range(2):
                cut = slice(H * k, H * k + H)
                right = jnp.concatenate([spread(qT[E * g:E * g + E, cut], g) for g in (h, h + 1)], 1)
                S = nn(left[k], jnp.concatenate([right, eye2], 0))
                strips.append(jnp.exp2(S - jnp.max(S, axis=0, keepdims=True)))
                yield
            exps.append(strips)
            packed = [v.astype(bf16) for v in strips]
            for g in (0, 1):
                cut = slice(H * g, H * g + H)
                low0 = jnp.concatenate([packed[0][:, cut], jnp.zeros((H, H), bf16)], 0)
                low = jnp.concatenate([low0, packed[1][:, cut]], 1)
                lows.append(low)
                sums = nn(jnp.concatenate([vT[E * (h + g):E * (h + g) + E], ones], 0), low)
                inv = 1.0 / sums[E:E + 1]
                att.append(sums[0:E] * inv)
                invs.append(inv)
            yield
        attT = jnp.concatenate(att, 0)
        attg = jnp.concatenate([attT.astype(bf16), ones], 0)
        mid = x_ref[idx] + nn(woT[...], attg)
        yield
        n2, r2 = norm(mid)
        a2 = (n2 * cols[2] + cols[3]).astype(bf16)
        a2g = jnp.concatenate([a2, ones], 0)
        upT = up_ref[idx]
        upb = upT.astype(bf16)
        yield
        acts, hgs = [], []
        for b in range(FF // D):
            blk = slice(D * b, D * b + D)
            hid = nn(wupT[blk, :], a2g)
            v2 = hid * hid
            s = 0.5 * jnp.tanh(hid * (TANH_SCALE + (TANH_SCALE * CUBIC) * v2)) + 0.5
            act = hid * s
            acts.append(act.astype(bf16))
            gp = s + act * (1.0 - s) * (2 * TANH_SCALE + (6 * TANH_SCALE * CUBIC) * v2)
            hgs.append((nn(wd[blk, :], upb) * gp).astype(bf16))
            yield
        actg = jnp.concatenate(acts + [ones], 0)
        hg = jnp.concatenate(hgs, 0)
        lo_ref[w] = (mid + nn(wdT[...], actg)).T
        yield
        yield (3, actg, upb)
        dn2 = nn(wup[...], hg)
        yield (2, a2g, hg)
        alng[0] += dn2 * n2
        midg = upT + norm_back(dn2, cols[2], n2, r2)
        bg = midg.astype(bf16)
        yield
        yield (1, attg, bg)
        daT = nn(wo[...], bg)
        yield
        dq, dk, dv = [], [], []
        das, rows = [], []
        for h in range(HEADS):
            blk = slice(E * h, E * h + E)
            da = (daT[blk] * invs[h]).astype(bf16)
            inner = -jnp.sum(da.astype(f32) * att[h], axis=0, keepdims=True)
            hi = inner.astype(bf16).astype(f32)
            mi = (inner - hi).astype(bf16).astype(f32)
            lo = inner - hi - mi
            das.append(da)
            rows.append(jnp.concatenate([hi, mi, lo, jnp.zeros((13, T), f32)], 0).astype(bf16))
        yield
        for h in range(0, HEADS, 2):
            low = []
            for k in range(2):
                cut = slice(H * k, H * k + H)
                right = jnp.concatenate(
                    [jnp.concatenate([spread(das[g][:, cut], g), rows[g][:, cut]], 0) for g in (h, h + 1)], 1)
                dP = nn(vrow1[0:H] if k == 0 else vrow1, right)
                low.append((exps[h // 2][k] * dP).astype(bf16))
                yield
            for g in (0, 1):
                blk = slice(E * (h + g), E * (h + g) + E)
                cut = slice(H * g, H * g + H)
                ds0 = jnp.concatenate([low[0][:, cut], jnp.zeros((H, H), bf16)], 0)
                dS = jnp.concatenate([ds0, low[1][:, cut]], 1)
                dq.append(nn(kT[blk], dS) * scale)
                dk.append(nt(qT[blk], dS) * (1.0 / LOG2E))
                dv.append(nt(das[h + g], lows[h + g]))
            yield
        pg = jnp.concatenate(dq + dk + dv, 0).astype(bf16)
        dn1 = nn(wqkv[...], pg)
        yield (0, a1g, pg)
        alng[1] += dn1 * n1
        tg_ref[w] = (midg + norm_back(dn1, cols[0], n1, r1)).T

    accs = (aqkv, ao, aup, ad)
    held = [[] for _ in accs]
    live_windows = [(w * skew, window(w)) for w in range(wps)]
    tick = 0
    while live_windows:
        still = []
        for start, gen in live_windows:
            if tick < start:
                still.append((start, gen))
                continue
            try:
                item = next(gen)
            except StopIteration:
                continue
            still.append((start, gen))
            if item is not None:
                held[item[0]].append(item[1:])
                if len(held[item[0]]) == group:
                    pairs = held[item[0]]
                    held[item[0]] = []
                    join = lambda k: pairs[0][k] if group == 1 else jnp.concatenate([p[k] for p in pairs], 1)
                    accs[item[0]][...] += nt(join(0), join(1))
        live_windows = still
        tick += 1

    @pl.when(step == steps - 1)
    def _():
        def row(k):
            a = alng[k]
            a = a[:, 0:H] + a[:, H:T]
            return jnp.sum(a.T, axis=0, keepdims=True)

        def shift(sums, weight):
            hi = sums.astype(bf16).astype(f32)
            mi = (sums - hi).astype(bf16).astype(f32)
            parts = jnp.concatenate([hi, mi, sums - hi - mi, jnp.zeros((13, sums.shape[1]), f32)], 0)
            return jnp.sum(nt(parts.astype(bf16), weight), axis=0, keepdims=True)

        vec = jnp.concatenate(
            [row(1), shift(aqkv[D:D + 1, :], wqkv[...]), aqkv[D:D + 1, 0:D], aqkv[D:D + 1, 2 * D:3 * D], ao[D:D + 1, :],
             row(0), shift(aup[D:D + 1, :], wup[...]), ad[FF:FF + 1, :]]
            + [aup[D:D + 1, D * b:D * b + D] for b in range(4)] + [jnp.zeros((4, D), f32)], 0)
        high = vec.astype(bf16)
        low = (vec - high.astype(f32)).astype(bf16)
        for k in range(PIECES // 2):
            for ref, half in ((keep_ref, core), (send_ref, 1 - core)):
                o = jnp.bitwise_xor(me, slot_of(half, k))
                r16 = pl.ds(pl.multiple_of(o * 16, 16), 16)
                for b in range(3):
                    ref[k, 16 * b:16 * b + 16, :] = aqkv[r16, D * b:D * b + D].astype(bf16)
                ref[k, 48:64, :] = ao[r16, :].astype(bf16)
                for b in range(4):
                    ref[k, 64 + 16 * b:80 + 16 * b, :] = aup[r16, D * b:D * b + D].astype(bf16)
                ref[k, 128:192, :] = ad[pl.ds(pl.multiple_of(o * 64, 64), 64), :].astype(bf16)
                ref[k, 192:208, :] = high
                ref[k, 208:224, :] = low

def prepare(lens, starts, x, ct):
    count, T, D = x.shape
    smem, vmem = pl.BlockSpec(memory_space=pltpu.SMEM), pl.BlockSpec(memory_space=pltpu.VMEM)
    turned = jax.ShapeDtypeStruct((count, D, T), f32)
    return pl.pallas_call(
        prepare_kernel,
        in_specs=[smem, smem, vmem, vmem],
        out_specs=[vmem] * 5,
        out_shape=[turned, turned, jax.ShapeDtypeStruct((count, 8, T), f32), turned,
                   jax.ShapeDtypeStruct((count, T + T // 2, T // 2), bf16)],
        compiler_params=pltpu.CompilerParams(vmem_limit_bytes=16 << 20),
        cost_estimate=pl.CostEstimate(flops=count * T * D * 40, bytes_accessed=count * T * D * 20, transcendentals=0),
        name="prepare",
    )(lens, starts, x, ct)


def layer(slots, ready, wps=4, group=4, skew=0, spread_out=True):
    count, D, T = ready[0].shape
    FF = 512
    steps = count // wps
    vm = lambda s, d: pltpu.VMEM(s, d)
    vmem = pl.BlockSpec(memory_space=pltpu.VMEM)
    win = pl.BlockSpec((wps, T, D), lambda i: (i, 0, 0))
    whole = lambda s: pl.BlockSpec(s, lambda i: (0,) * len(s))
    half = (PIECES // 2, GRAD_ROWS, D)
    return pl.pallas_call(
        functools.partial(layer_kernel, wps=wps, steps=steps, group=group, skew=skew, spread_out=spread_out),
        grid=(steps,),
        in_specs=[vmem] * 11,
        out_specs=[win, win, whole(half), whole(half)],
        out_shape=[jax.ShapeDtypeStruct((count, T, D), f32)] * 2 + [jax.ShapeDtypeStruct(half, bf16)] * 2,
        scratch_shapes=[
            vm((D, 3 * D), bf16), vm((3 * D, D + 16), bf16), vm((D, D), bf16), vm((D, D + 16), bf16),
            vm((D, FF), bf16), vm((FF, D + 16), bf16), vm((FF, D), bf16), vm((D, FF + 16), bf16),
            vm((4, D, T), f32),
            vm((D + 16, 3 * D), f32), vm((D + 16, D), f32), vm((D + 16, FF), f32), vm((FF + 16, D), f32),
            vm((2, D, T), f32)],
        compiler_params=pltpu.CompilerParams(vmem_limit_bytes=30 << 20, dimension_semantics=("arbitrary",)),
        name="layer",
    )(*slots, *ready)


VMEM = pl.BlockSpec(memory_space=pltpu.VMEM)
SMEM = pl.BlockSpec(memory_space=pltpu.SMEM)
HBM = pl.BlockSpec(memory_space=pltpu.HBM)
SMALL = pltpu.CompilerParams(vmem_limit_bytes=16 << 20)
ALONE = pltpu.CompilerParams(vmem_limit_bytes=60 << 20)


def pack_kernel(*refs):
    hbm, out_ref, held, sems = refs[:13], refs[13], refs[14:27], refs[27]
    copies = [pltpu.make_async_copy(src, dst, sems.at[k]) for k, (src, dst) in enumerate(zip(hbm, held))]
    for copy in copies:
        copy.start()
    gain_a, shift_a, qkv, query, value, outw, outb, gain_m, shift_m, upw, upb, downw, downb = held
    me, core = place()
    D = out_ref.shape[1]
    row = lax.broadcasted_iota(jnp.int32, (16, D), 0)
    lane16 = lax.broadcasted_iota(jnp.int32, (16, D), 1)
    spot16 = (lane16 == row + 16 * me).astype(bf16)
    r64 = lax.broadcasted_iota(jnp.int32, (64, D), 0)
    l64 = lax.broadcasted_iota(jnp.int32, (64, D), 1)
    spot64 = (l64 == r64 + 64 * jnp.bitwise_and(me, 1)).astype(bf16)
    for copy in copies:
        copy.wait()
    for b in range(3):
        out_ref[16 * b:16 * b + 16, :] = qkv[:, D * b:D * b + D]
    out_ref[48:64, :] = outw[...]
    for b in range(4):
        out_ref[64 + 16 * b:80 + 16 * b, :] = upw[:, D * b:D * b + D]
    out_ref[128:192, :] = downw[...]
    total = jnp.zeros((16, D), f32)
    for k, ref in enumerate((gain_a, shift_a, query, value, outb, gain_m, shift_m, downb)):
        v = jnp.broadcast_to(ref[...].astype(f32).reshape(1, 16), (16, 16)).astype(bf16)
        total = total + jnp.where(row == k, nn(v, spot16), 0.0)
    v = jnp.broadcast_to(upb[...].astype(f32).reshape(1, 64), (16, 64)).astype(bf16)
    total = total + jnp.where(row == 8 + lax.shift_right_logical(me, 1), nn(v, spot64), 0.0)
    out_ref[192:208, :] = total.astype(bf16)


def split_add(parts):
    total = parts[0].astype(f32)
    for p in parts[1:]:
        total = total + p.astype(f32)
    vec = total[192:208] + total[208:224]
    high = vec.astype(bf16)
    low = (vec - high.astype(f32)).astype(bf16)
    return total[0:192], vec, high, low


def pair_kernel(keep_ref, got_ref, *out_refs):
    for k, ref in enumerate(out_refs):
        main, vec, high, low = split_add([keep_ref[k], got_ref[k]])
        ref[0:192, :] = main.astype(bf16)
        ref[192:208, :] = high
        ref[208:224, :] = low


def merge_kernel(own_ref, r0, r1, r2, r3, out_ref):
    first = jnp.where(place()[1] == 0, own_ref[...].astype(f32), r0[...].astype(f32))
    main, vec, high, low = split_add([first, r1[...], r2[...], r3[...]])
    out_ref[0:192, :] = main.astype(bf16)
    out_ref[192:208, :] = high
    out_ref[208:224, :] = low


def finish_kernel(m0, m1, m2, m3, gain_a, shift_a, qkv, query, value, outw, outb, gain_m, shift_m, upw, upb, downw, downb):
    me, core = place()
    D = m0.shape[1]
    main, vec, high, low = split_add([m0[...], m1[...], m2[...], m3[...]])
    for b in range(3):
        qkv[:, D * b:D * b + D] = main[16 * b:16 * b + 16]
    outw[...] = main[48:64]
    for b in range(4):
        upw[:, D * b:D * b + D] = main[64 + 16 * b:80 + 16 * b]
    downw[...] = main[128:192]
    turned = pltpu.roll(vec, jnp.bitwise_and(D - 16 * me, D - 1), 1)
    for k, ref in enumerate((gain_a, shift_a, query, value, outb, gain_m, shift_m, downb)):
        ref[...] = turned[k:k + 1, 0:16].reshape(16)
    row = lax.broadcasted_iota(jnp.int32, (16, D), 0)
    half = jnp.sum(jnp.where(row == 8 + lax.shift_right_logical(me, 1), vec, 0.0), axis=0, keepdims=True)
    half = jnp.where(jnp.bitwise_and(me, 1) == 0, half[:, 0:64], half[:, 64:128])
    upb[...] = half.reshape(64)


def per_device(tokens, episode_length, window_start, *rest):
    params, cotangent = rest[:13], rest[13]
    D = tokens.shape[2]
    grp, wide = lax.axis_size("grp"), lax.axis_size("wide")
    axes = ("grp", "wide")

    def across(core_slots):
        pairs = []
        for g in range(grp):
            s = core_slots[g % 2]
            if s:
                pairs += [(g * wide + i, g * wide + (i ^ s)) for i in range(wide)]
        return pairs

    swap = [(g * wide + i, (g ^ 1) * wide + i) for g in range(grp) for i in range(wide)]
    piece = pl.pallas_call(
        pack_kernel, in_specs=[HBM] * 13, out_specs=VMEM,
        out_shape=jax.ShapeDtypeStruct((PIECE_ROWS, D), bf16), compiler_params=ALONE, name="pack",
        scratch_shapes=[pltpu.VMEM(p.shape, bf16) for p in params] + [pltpu.SemaphoreType.DMA((13,))],
    )(*params)
    hops = [across((SLOTS[0][k], SLOTS[1][k])) for k in range(4)]
    direct = [lax.ppermute(piece, axes, hops[k]) for k in range(4)]
    others = lax.ppermute(jnp.concatenate(direct, 0), axes, swap)
    ready = prepare(episode_length, window_start, tokens, cotangent)
    layer_out, tokens_grad, keep, send = layer([piece, *direct, others], ready)
    got = lax.ppermute(send, axes, swap)
    shape = jax.ShapeDtypeStruct((GRAD_ROWS, D), bf16)
    pairs = pl.pallas_call(
        pair_kernel, in_specs=[VMEM] * 2, out_specs=[VMEM] * 4, out_shape=[shape] * 4, compiler_params=SMALL, name="pair",
    )(keep, got)
    came = [lax.ppermute(pairs[k], axes, hops[k]) for k in range(4)]
    merged = pl.pallas_call(
        merge_kernel, in_specs=[VMEM] * 5, out_specs=VMEM, out_shape=shape, compiler_params=SMALL, name="merge",
    )(pairs[0], *came)
    around = [[(g * wide + i, (g ^ m) * wide + i) for g in range(grp) for i in range(wide)] for m in range(1, grp)]
    every = [merged] + [lax.ppermute(merged, axes, pairs_of) for pairs_of in around]
    grads = pl.pallas_call(
        finish_kernel, in_specs=[VMEM] * grp, out_specs=[VMEM] * 13,
        out_shape=[jax.ShapeDtypeStruct(p.shape, f32) for p in params], compiler_params=SMALL, name="finish",
    )(*every)
    return (layer_out, tokens_grad, *grads)


def gathered(tokens, episode_length, window_start, *rest):
    params, cotangent = rest[:13], rest[13]
    D = tokens.shape[2]
    full = [lax.all_gather(p, "wide", axis=0, tiled=True) for p in params]
    gain_a, shift_a, qkv, query, value, outw, outb, gain_m, shift_m, upw, upb, downw, downb = full
    FF = upw.shape[1]
    lanes = jnp.arange(D) // (D // PIECES)
    spots = (lanes[None, :] == jnp.arange(PIECES)[:, None]).astype(bf16)
    vectors = jnp.stack([gain_a, shift_a, query, value, outb, gain_m, shift_m, downb])[None] * spots[:, None, :]
    where_up = (jnp.arange(FF) // (FF // PIECES))[None, :] == jnp.arange(PIECES)[:, None]
    ups = (upb[None] * where_up.astype(bf16)).reshape(PIECES, FF // D, D)

    def blocks(weight):
        cut = weight.reshape(PIECES, weight.shape[0] // PIECES, weight.shape[1] // D, D)
        return cut.transpose(0, 2, 1, 3).reshape(PIECES, -1, D)

    slots = jnp.concatenate(
        [blocks(qkv), blocks(outw), blocks(upw), blocks(downw), vectors, ups, jnp.zeros((PIECES, 4, D), bf16)], 1
    )
    direct = [slots[SLOTS[1][0]]] + [slots[SLOTS[0][k]] for k in (1, 2, 3)]
    others = jnp.concatenate([jnp.zeros_like(slots[0])] + [slots[SLOTS[1][k]] for k in (1, 2, 3)], 0)
    ready = prepare(episode_length, window_start, tokens, cotangent)
    layer_out, tokens_grad, keep, send = layer([slots[0], *direct, others], ready, spread_out=False)
    order = [0] * PIECES
    for half in (0, 1):
        for k in range(4):
            order[SLOTS[half][k]] = 4 * half + k
    pieces = jnp.concatenate([keep, send], 0)[jnp.array(order)].astype(f32)
    vec = pieces[0, 192:208] + pieces[0, 208:224]

    def rebuilt(first, last, weight):
        cut = pieces[:, first:last].reshape(PIECES, weight.shape[1] // D, weight.shape[0] // PIECES, D)
        return cut.transpose(0, 2, 1, 3).reshape(weight.shape)

    grads = (
        vec[0], vec[1], rebuilt(0, 48, qkv), vec[2], vec[3], rebuilt(48, 64, outw), vec[4], vec[5], vec[6],
        rebuilt(64, 128, upw), vec[8:12].reshape(FF), rebuilt(128, 192, downw), vec[7],
    )
    grads = [lax.psum_scatter(g, "wide", scatter_dimension=0, tiled=True) for g in grads]
    return (layer_out, tokens_grad, *lax.psum(grads, "grp"))


def solution(mesh):
    rows = P(("grp", "wide"), None, None)
    flat = P(("grp", "wide"))
    one, two = P("wide"), P("wide", None)
    params = (one, one, two, one, one, two, one, one, one, two, one, two, one)
    fits = mesh.shape["wide"] == PIECES and mesh.shape["grp"] == 4
    return jax.shard_map(
        per_device if fits else gathered, mesh=mesh, in_specs=(rows, flat, flat, *params, rows), out_specs=(rows, rows, *params), check_vma=False
    )
```

```python
import math
import functools

import jax
import jax.numpy as jnp
from jax import lax
from jax.experimental import pallas as pl
from jax.experimental.pallas import tpu as pltpu
from jax.sharding import PartitionSpec as P

HEADS = 4
EPS = 1e-05
CUBIC = 0.044715
TANH_SCALE = math.sqrt(2.0 / math.pi)
NEG_FILL = -1e30
LOG2E = math.log2(math.e)
f32, bf16 = jnp.float32, jnp.bfloat16
PIECES = 8
PIECE_ROWS = 208
GRAD_ROWS = 224
SLOTS = ((0, 1, 5, 6), (3, 2, 4, 7))
BACK = ((0, 6, 5, 1), (3, 7, 4, 2))

TILES = ((1, (0, 1)), (1, (2, 3)), (0, (0, 2)), (0, (1, 3)))
EARLY = (0, 2, 1, 3)


def place():
    return lax.axis_index("wide").astype(jnp.int32), jnp.bitwise_and(lax.axis_index("grp").astype(jnp.int32), 1)


def slot_of(core, k, table=SLOTS):
    return jnp.where(core == 0, table[0][k], table[1][k])


def nn(a, b):
    return lax.dot_general(a, b, (((1,), (0,)), ((), ())), preferred_element_type=f32)

def nt(a, b):
    return lax.dot_general(a, b, (((1,), (1,)), ((), ())), preferred_element_type=f32)

def norm(v):
    d = v.shape[0]
    off = v - jnp.sum(v, axis=0, keepdims=True) * (1.0 / d)
    r = lax.rsqrt(jnp.sum(off * off, axis=0, keepdims=True) * (1.0 / d) + EPS)
    return off * r, r

def norm_back(dy, gain, n, r):
    d = dy.shape[0]
    g = dy * gain
    mg = jnp.sum(g, axis=0, keepdims=True) * (1.0 / d)
    mgn = jnp.sum(g * n, axis=0, keepdims=True) * (1.0 / d)
    return r * (g - mg - n * mgn)

def tokens_kernel(x_in, x_ref, n_ref, r_ref):
    count, T, D = x_in.shape
    for w in range(count):
        xT = x_in[w].astype(f32).T
        n, r = norm(xT)
        x_ref[w] = xT
        n_ref[w] = n
        r_ref[w] = jnp.broadcast_to(r, (8, T))


def cotangent_kernel(len_ref, start_ref, ct_in, up_ref, mask_ref):
    count, T, D = ct_in.shape
    H = T // 2
    for w in range(count):
        valid = jnp.clip(len_ref[w] - start_ref[w], 1, T)
        live = (lax.broadcasted_iota(jnp.int32, (1, T), 1) < valid).astype(f32)
        up_ref[w] = ct_in[w].astype(f32).T * live
        j = lax.broadcasted_iota(jnp.int32, (H, H), 0)
        tri = j <= lax.broadcasted_iota(jnp.int32, (H, H), 1)
        for k, seen in enumerate((tri & (j < valid), j < valid, tri & (j + H < valid))):
            mask_ref[w, H * k:H * k + H] = jnp.where(seen, 0.0, NEG_FILL).astype(bf16)


def layer_kernel(w0, d0, d1, d2, d3, others, x_ref, n_ref, r_ref, up_ref, mask_ref,
                 lo_ref, tg_ref, keep_ref, send_ref,
                 wqkv, wqkvT, wo, woT, wup, wupT, wd, wdT, cols,
                 aqkv, ao, aup, ad, alng, *, wps, steps, group, skew, spread_out):
    step = pl.program_id(0)
    me, core = place() if spread_out else (jnp.int32(0), jnp.int32(0))
    D, T = x_ref.shape[1], x_ref.shape[2]
    H = T // 2
    E = D // HEADS
    FF = wup.shape[1]
    scale = E ** -0.5

    @pl.when(step == 0)
    def _():
        vec = jnp.zeros((16, D), f32)
        places = [(0, w0, 0), (SLOTS[1][0], d0, 0)]
        for k in (1, 2, 3):
            places += [(slot_of(core, k), (d1, d2, d3)[k - 1], 0), (slot_of(1 - core, k), others, PIECE_ROWS * k)]
        for slot, ref, at in places:
            o = jnp.bitwise_xor(me, slot)
            r16 = pl.ds(pl.multiple_of(o * 16, 16), 16)
            get = lambda first, last: ref[at + first:at + last, :]
            if ref is d0:
                get = lambda first, last: d0[first:last, :] + others[first:last, :]
            for b in range(3):
                wqkv[r16, D * b:D * b + D] = get(16 * b, 16 * b + 16)
            wo[r16, :] = get(48, 64)
            for b in range(4):
                wup[r16, D * b:D * b + D] = get(64 + 16 * b, 80 + 16 * b)
            wd[pl.ds(pl.multiple_of(o * 64, 64), 64), :] = get(128, 192)
            vec = vec + get(192, 208).astype(f32)
        vecT = jnp.concatenate([vec, jnp.zeros((D - 16, D), f32)], 0).T
        lane = lax.broadcasted_iota(jnp.int32, (D, 16), 1)
        def col(k):
            return jnp.where(lane == k, vecT[:, 0:16], 0.0).astype(bf16)
        def full(k):
            return jnp.broadcast_to(vecT[:, k:k + 1], (D, T))
        for b in range(3):
            wqkvT[D * b:D * b + D, 0:D] = wqkv[:, D * b:D * b + D].T
        wqkvT[0:D, D:D + 16] = col(2)
        wqkvT[D:2 * D, D:D + 16] = jnp.zeros((D, 16), bf16)
        wqkvT[2 * D:3 * D, D:D + 16] = col(3)
        woT[:, 0:D] = wo[...].T
        woT[:, D:D + 16] = col(4)
        for b in range(4):
            wupT[D * b:D * b + D, 0:D] = wup[:, D * b:D * b + D].T
            wupT[D * b:D * b + D, D:D + 16] = col(8 + b)
            wdT[:, D * b:D * b + D] = wd[D * b:D * b + D, :].T
        wdT[:, FF:FF + 16] = col(7)
        cols[0] = full(0)
        cols[1] = full(1)
        cols[2] = full(5)
        cols[3] = full(6)
        for ref in (aqkv, ao, aup, ad, alng):
            ref[...] = jnp.zeros(ref.shape, f32)

    ones = jnp.ones((16, T), bf16)
    eye2 = (lax.broadcasted_iota(jnp.int32, (H, T), 0) == jnp.bitwise_and(lax.broadcasted_iota(jnp.int32, (H, T), 1), H - 1)).astype(f32).astype(bf16)

    def spread(m, h):
        parts = []
        if h > 0:
            parts.append(jnp.zeros((E * h, m.shape[1]), bf16))
        parts.append(m)
        if h < HEADS - 1:
            parts.append(jnp.zeros((E * (HEADS - 1 - h), m.shape[1]), bf16))
        return jnp.concatenate(parts, 0)

    none = jnp.zeros((16, H), bf16)
    blank = jnp.zeros((E, H), bf16)

    def beside(m, g, first, put):
        part = m[E * g:E * g + E, H * first:H * first + H]
        return jnp.concatenate([part, blank] if put == 0 else [blank, part], 1)

    def stack_keys(m):
        return jnp.concatenate([beside(m, g, 0, g % 2) for g in EARLY], 0)

    def stack_early(m):
        return jnp.concatenate([beside(m, g, 0, g // 2) for g in EARLY], 0)

    def stack_late(m, p):
        return jnp.concatenate([beside(m, 2 * p, 1, 0), beside(m, 2 * p + 1, 1, 1)], 0)

    def window(w):
        idx = step * wps + w
        n1, r1 = n_ref[idx], r_ref[idx, 0:1]
        a1 = (n1 * cols[0] + cols[1]).astype(bf16)
        a1g = jnp.concatenate([a1, ones], 0)
        yield
        qT = (nn(wqkvT[0:D, :], a1g) * (scale * LOG2E)).astype(bf16)
        kT = nn(wqkvT[D:2 * D, :], a1g).astype(bf16)
        vT = nn(wqkvT[2 * D:3 * D, :], a1g).astype(bf16)
        yield
        krow, vrow = kT.T, vT.T
        left = (jnp.concatenate([krow[0:H], mask_ref[idx, 0:H]], 1), jnp.concatenate([krow, mask_ref[idx, H:H + T]], 1))
        vrow1 = jnp.concatenate([vrow, jnp.ones((T, 16), bf16)], 1)
        yield
        exps = []
        for k, pair in TILES:
            cut = slice(H * k, H * k + H)
            right = jnp.concatenate([spread(qT[E * g:E * g + E, cut], g) for g in pair], 1)
            S = nn(left[k], jnp.concatenate([right, eye2], 0))
            exps.append(jnp.exp2(S - jnp.max(S, axis=0, keepdims=True)))
            yield
        lows = [exps[0].astype(bf16), exps[1].astype(bf16), jnp.concatenate([exps[2].astype(bf16), exps[3].astype(bf16)], 0)]
        tops = [nn(jnp.concatenate([vT[E * 2 * p:E * 2 * p + 2 * E], ones], 0), lows[p]) for p in (0, 1)]
        yield
        early = nn(jnp.concatenate([stack_keys(vT), jnp.concatenate([ones[:, 0:H], none], 1), jnp.concatenate([none, ones[:, 0:H]], 1)], 0), lows[2])
        att, invs = [], []
        for g in range(HEADS):
            top, low = tops[g // 2], early[4 * E + 16 * (g % 2):4 * E + 16 * (g % 2) + 1]
            cut, at = slice(H * (g % 2), H * (g % 2) + H), slice(H * (g // 2), H * (g // 2) + H)
            inv = 1.0 / jnp.concatenate([low[:, at], top[2 * E:2 * E + 1, cut]], 1)
            invs.append(inv)
            row = E * EARLY.index(g)
            att.append(jnp.concatenate([early[row:row + E, at], top[E * (g % 2):E * (g % 2) + E, cut]], 1) * inv)
        yield
        attT = jnp.concatenate(att, 0)
        attg = jnp.concatenate([attT.astype(bf16), ones], 0)
        mid = x_ref[idx] + nn(woT[...], attg)
        yield
        n2, r2 = norm(mid)
        a2 = (n2 * cols[2] + cols[3]).astype(bf16)
        a2g = jnp.concatenate([a2, ones], 0)
        upT = up_ref[idx]
        upb = upT.astype(bf16)
        yield
        acts, hgs = [], []
        for b in range(FF // D):
            blk = slice(D * b, D * b + D)
            hid = nn(wupT[blk, :], a2g)
            v2 = hid * hid
            s = 0.5 * jnp.tanh(hid * (TANH_SCALE + (TANH_SCALE * CUBIC) * v2)) + 0.5
            act = hid * s
            acts.append(act.astype(bf16))
            gp = s + act * (1.0 - s) * (2 * TANH_SCALE + (6 * TANH_SCALE * CUBIC) * v2)
            hgs.append((nn(wd[blk, :], upb) * gp).astype(bf16))
            yield
        actg = jnp.concatenate(acts + [ones], 0)
        hg = jnp.concatenate(hgs, 0)
        lo_ref[w] = (mid + nn(wdT[...], actg)).T
        yield
        yield (3, actg, upb)
        dn2 = nn(wup[...], hg)
        yield (2, a2g, hg)
        alng[0] += dn2 * n2
        midg = upT + norm_back(dn2, cols[2], n2, r2)
        bg = midg.astype(bf16)
        yield
        yield (1, attg, bg)
        daT = nn(wo[...], bg)
        yield
        dq, dk, dv = [], [], []
        das, rows = [], []
        for h in range(HEADS):
            blk = slice(E * h, E * h + E)
            da = (daT[blk] * invs[h]).astype(bf16)
            inner = -jnp.sum(da.astype(f32) * att[h], axis=0, keepdims=True)
            hi = inner.astype(bf16).astype(f32)
            mi = (inner - hi).astype(bf16).astype(f32)
            lo = inner - hi - mi
            das.append(da)
            rows.append(jnp.concatenate([hi, mi, lo, jnp.zeros((13, T), f32)], 0).astype(bf16))
        yield
        daT2 = jnp.concatenate(das, 0)
        tiles = []
        for (k, pair), e in zip(TILES, exps):
            cut = slice(H * k, H * k + H)
            right = jnp.concatenate(
                [jnp.concatenate([spread(das[g][:, cut], g), rows[g][:, cut]], 0) for g in pair], 1)
            dP = nn(vrow1[0:H] if k == 0 else vrow1, right)
            tiles.append((e * dP).astype(bf16))
            yield
        tiles = [tiles[0], tiles[1], jnp.concatenate([tiles[2], tiles[3]], 0)]

        def by_query(m, tiles):
            tops = [nn(m[2 * E * p:2 * E * p + 2 * E], tiles[p]) for p in (0, 1)]
            low = nn(stack_keys(m), tiles[2])
            out = []
            for g in range(HEADS):
                at, cut, row = slice(H * (g // 2), H * (g // 2) + H), slice(H * (g % 2), H * (g % 2) + H), E * EARLY.index(g)
                out.append(jnp.concatenate([low[row:row + E, at], tops[g // 2][E * (g % 2):E * (g % 2) + E, cut]], 1))
            return out

        def by_key(m, tiles):
            tops = [nt(stack_late(m, p), tiles[p]) for p in (0, 1)]
            low = nt(stack_early(m), tiles[2])
            out = []
            for g in range(HEADS):
                at, row = slice(H * (g % 2), H * (g % 2) + H), E * EARLY.index(g)
                top = tops[g // 2][E * (g % 2):E * (g % 2) + E]
                out.append(jnp.concatenate([top[:, 0:H] + low[row:row + E, at], top[:, H:T]], 1))
            return out

        dq = [v * scale for v in by_query(kT, tiles)]
        yield
        dk = [v * (1.0 / LOG2E) for v in by_key(qT, tiles)]
        yield
        dv = by_key(daT2, lows)
        yield
        pg = jnp.concatenate(dq + dk + dv, 0).astype(bf16)
        dn1 = nn(wqkv[...], pg)
        yield (0, a1g, pg)
        alng[1] += dn1 * n1
        tg_ref[w] = (midg + norm_back(dn1, cols[0], n1, r1)).T

    accs = (aqkv, ao, aup, ad)
    held = [[] for _ in accs]
    live_windows = [(w // group * skew, window(w)) for w in range(wps)]
    tick = 0
    while live_windows:
        still = []
        for start, gen in live_windows:
            if tick < start:
                still.append((start, gen))
                continue
            try:
                item = next(gen)
            except StopIteration:
                continue
            still.append((start, gen))
            if item is not None:
                held[item[0]].append(item[1:])
                if len(held[item[0]]) == group:
                    pairs = held[item[0]]
                    held[item[0]] = []
                    join = lambda k: pairs[0][k] if group == 1 else jnp.concatenate([p[k] for p in pairs], 1)
                    accs[item[0]][...] += nt(join(0), join(1))
        live_windows = still
        tick += 1

    @pl.when(step == steps - 1)
    def _():
        def row(k):
            a = alng[k]
            a = a[:, 0:H] + a[:, H:T]
            return jnp.sum(a.T, axis=0, keepdims=True)

        def shift(sums, weight):
            hi = sums.astype(bf16).astype(f32)
            mi = (sums - hi).astype(bf16).astype(f32)
            parts = jnp.concatenate([hi, mi, sums - hi - mi, jnp.zeros((13, sums.shape[1]), f32)], 0)
            return jnp.sum(nt(parts.astype(bf16), weight), axis=0, keepdims=True)

        vec = jnp.concatenate(
            [row(1), shift(aqkv[D:D + 1, :], wqkv[...]), aqkv[D:D + 1, 0:D], aqkv[D:D + 1, 2 * D:3 * D], ao[D:D + 1, :],
             row(0), shift(aup[D:D + 1, :], wup[...]), ad[FF:FF + 1, :]]
            + [aup[D:D + 1, D * b:D * b + D] for b in range(4)] + [jnp.zeros((4, D), f32)], 0)
        high = vec.astype(bf16)
        low = (vec - high.astype(f32)).astype(bf16)
        for k in range(PIECES // 2):
            for ref, half in ((keep_ref, core), (send_ref, 1 - core)):
                o = jnp.bitwise_xor(me, slot_of(half, k, BACK))
                r16 = pl.ds(pl.multiple_of(o * 16, 16), 16)
                for b in range(3):
                    ref[k, 16 * b:16 * b + 16, :] = aqkv[r16, D * b:D * b + D].astype(bf16)
                ref[k, 48:64, :] = ao[r16, :].astype(bf16)
                for b in range(4):
                    ref[k, 64 + 16 * b:80 + 16 * b, :] = aup[r16, D * b:D * b + D].astype(bf16)
                ref[k, 128:192, :] = ad[pl.ds(pl.multiple_of(o * 64, 64), 64), :].astype(bf16)
                ref[k, 192:208, :] = high
                ref[k, 208:224, :] = low

def prepare_tokens(x):
    count, T, D = x.shape
    vmem = pl.BlockSpec(memory_space=pltpu.VMEM)
    turned = jax.ShapeDtypeStruct((count, D, T), f32)
    return pl.pallas_call(
        tokens_kernel,
        in_specs=[vmem],
        out_specs=[vmem] * 3,
        out_shape=[turned, turned, jax.ShapeDtypeStruct((count, 8, T), f32)],
        compiler_params=pltpu.CompilerParams(vmem_limit_bytes=16 << 20),
        cost_estimate=pl.CostEstimate(flops=0, bytes_accessed=count * T * D * 40, transcendentals=0),
        name="prepare_tokens",
    )(x)


def prepare_cotangent(lens, starts, ct):
    count, T, D = ct.shape
    smem, vmem = pl.BlockSpec(memory_space=pltpu.SMEM), pl.BlockSpec(memory_space=pltpu.VMEM)
    return pl.pallas_call(
        cotangent_kernel,
        in_specs=[smem, smem, vmem],
        out_specs=[vmem] * 2,
        out_shape=[jax.ShapeDtypeStruct((count, D, T), f32), jax.ShapeDtypeStruct((count, T + T // 2, T // 2), bf16)],
        compiler_params=pltpu.CompilerParams(vmem_limit_bytes=16 << 20),
        cost_estimate=pl.CostEstimate(flops=0, bytes_accessed=count * T * D * 20, transcendentals=0),
        name="prepare_cotangent",
    )(lens, starts, ct)


def layer(slots, ready, wps=8, group=4, skew=13, spread_out=True):
    count, D, T = ready[0].shape
    FF = 512
    steps = count // wps
    vm = lambda s, d: pltpu.VMEM(s, d)
    vmem = pl.BlockSpec(memory_space=pltpu.VMEM)
    win = pl.BlockSpec((wps, T, D), lambda i: (i, 0, 0))
    whole = lambda s: pl.BlockSpec(s, lambda i: (0,) * len(s))
    half = (PIECES // 2, GRAD_ROWS, D)
    return pl.pallas_call(
        functools.partial(layer_kernel, wps=wps, steps=steps, group=group, skew=skew, spread_out=spread_out),
        grid=(steps,),
        in_specs=[vmem] * 11,
        out_specs=[win, win, whole(half), whole(half)],
        out_shape=[jax.ShapeDtypeStruct((count, T, D), f32)] * 2 + [jax.ShapeDtypeStruct(half, bf16)] * 2,
        scratch_shapes=[
            vm((D, 3 * D), bf16), vm((3 * D, D + 16), bf16), vm((D, D), bf16), vm((D, D + 16), bf16),
            vm((D, FF), bf16), vm((FF, D + 16), bf16), vm((FF, D), bf16), vm((D, FF + 16), bf16),
            vm((4, D, T), f32),
            vm((D + 16, 3 * D), f32), vm((D + 16, D), f32), vm((D + 16, FF), f32), vm((FF + 16, D), f32),
            vm((2, D, T), f32)],
        compiler_params=pltpu.CompilerParams(vmem_limit_bytes=30 << 20, dimension_semantics=("arbitrary",)),
        name="layer",
    )(*slots, *ready)


VMEM = pl.BlockSpec(memory_space=pltpu.VMEM)
SMEM = pl.BlockSpec(memory_space=pltpu.SMEM)
HBM = pl.BlockSpec(memory_space=pltpu.HBM)
SMALL = pltpu.CompilerParams(vmem_limit_bytes=16 << 20)
ALONE = pltpu.CompilerParams(vmem_limit_bytes=60 << 20)


def pack_kernel(*refs):
    hbm, out_ref, held, sems = refs[:13], refs[13], refs[14:27], refs[27]
    copies = [pltpu.make_async_copy(src, dst, sems.at[k]) for k, (src, dst) in enumerate(zip(hbm, held))]
    for copy in copies:
        copy.start()
    gain_a, shift_a, qkv, query, value, outw, outb, gain_m, shift_m, upw, upb, downw, downb = held
    me, core = place()
    D = out_ref.shape[1]
    row = lax.broadcasted_iota(jnp.int32, (16, D), 0)
    lane16 = lax.broadcasted_iota(jnp.int32, (16, D), 1)
    spot16 = (lane16 == row + 16 * me).astype(bf16)
    r64 = lax.broadcasted_iota(jnp.int32, (64, D), 0)
    l64 = lax.broadcasted_iota(jnp.int32, (64, D), 1)
    spot64 = (l64 == r64 + 64 * jnp.bitwise_and(me, 1)).astype(bf16)
    for copy in copies:
        copy.wait()
    for b in range(3):
        out_ref[16 * b:16 * b + 16, :] = qkv[:, D * b:D * b + D]
    out_ref[48:64, :] = outw[...]
    for b in range(4):
        out_ref[64 + 16 * b:80 + 16 * b, :] = upw[:, D * b:D * b + D]
    out_ref[128:192, :] = downw[...]
    total = jnp.zeros((16, D), f32)
    for k, ref in enumerate((gain_a, shift_a, query, value, outb, gain_m, shift_m, downb)):
        v = jnp.broadcast_to(ref[...].astype(f32).reshape(1, 16), (16, 16)).astype(bf16)
        total = total + jnp.where(row == k, nn(v, spot16), 0.0)
    v = jnp.broadcast_to(upb[...].astype(f32).reshape(1, 64), (16, 64)).astype(bf16)
    total = total + jnp.where(row == 8 + lax.shift_right_logical(me, 1), nn(v, spot64), 0.0)
    out_ref[192:208, :] = total.astype(bf16)


def split_add(parts):
    total = parts[0].astype(f32)
    for p in parts[1:]:
        total = total + p.astype(f32)
    vec = total[192:208] + total[208:224]
    high = vec.astype(bf16)
    low = (vec - high.astype(f32)).astype(bf16)
    return total[0:192], vec, high, low


def pair_kernel(keep_ref, got_ref, *out_refs):
    for k, ref in enumerate(out_refs):
        main, vec, high, low = split_add([keep_ref[k], got_ref[k]])
        ref[0:192, :] = main.astype(bf16)
        ref[192:208, :] = high
        ref[208:224, :] = low


def merge_kernel(own_ref, r0, r1, r2, r3, out_ref):
    first = jnp.where(place()[1] == 0, own_ref[...].astype(f32), r0[...].astype(f32))
    main, vec, high, low = split_add([first, r1[...], r2[...], r3[...]])
    out_ref[0:192, :] = main.astype(bf16)
    out_ref[192:208, :] = high
    out_ref[208:224, :] = low


def chip_kernel(own_ref, got_ref, out_ref):
    main, vec, high, low = split_add([own_ref[...], got_ref[...]])
    out_ref[0:192, :] = main.astype(bf16)
    out_ref[192:208, :] = high
    out_ref[208:224, :] = low


def finish_kernel(m0, m1, gain_a, shift_a, qkv, query, value, outw, outb, gain_m, shift_m, upw, upb, downw, downb):
    me, core = place()
    D = m0.shape[1]
    main, vec, high, low = split_add([m0[...], m1[...]])
    for b in range(3):
        qkv[:, D * b:D * b + D] = main[16 * b:16 * b + 16]
    outw[...] = main[48:64]
    for b in range(4):
        upw[:, D * b:D * b + D] = main[64 + 16 * b:80 + 16 * b]
    downw[...] = main[128:192]
    turned = pltpu.roll(vec, jnp.bitwise_and(D - 16 * me, D - 1), 1)
    for k, ref in enumerate((gain_a, shift_a, query, value, outb, gain_m, shift_m, downb)):
        ref[...] = turned[k:k + 1, 0:16].reshape(16)
    row = lax.broadcasted_iota(jnp.int32, (16, D), 0)
    half = jnp.sum(jnp.where(row == 8 + lax.shift_right_logical(me, 1), vec, 0.0), axis=0, keepdims=True)
    half = jnp.where(jnp.bitwise_and(me, 1) == 0, half[:, 0:64], half[:, 64:128])
    upb[...] = half.reshape(64)


def per_device(tokens, episode_length, window_start, *rest):
    params, cotangent = rest[:13], rest[13]
    D = tokens.shape[2]
    grp, wide = lax.axis_size("grp"), lax.axis_size("wide")
    axes = ("grp", "wide")

    def across(core_slots):
        pairs = []
        for g in range(grp):
            s = core_slots[g % 2]
            if s:
                pairs += [(g * wide + i, g * wide + (i ^ s)) for i in range(wide)]
        return pairs

    swap = [(g * wide + i, (g ^ 1) * wide + i) for g in range(grp) for i in range(wide)]
    piece = pl.pallas_call(
        pack_kernel, in_specs=[HBM] * 13, out_specs=VMEM,
        out_shape=jax.ShapeDtypeStruct((PIECE_ROWS, D), bf16), compiler_params=ALONE, name="pack",
        cost_estimate=pl.CostEstimate(flops=0, bytes_accessed=40 << 20, transcendentals=0),
        scratch_shapes=[pltpu.VMEM(p.shape, bf16) for p in params] + [pltpu.SemaphoreType.DMA((13,))],
    )(*params)
    hops = [across((SLOTS[0][k], SLOTS[1][k])) for k in range(4)]
    direct = [lax.ppermute(piece, axes, hops[k]) for k in range(4)]
    ready = prepare_tokens(tokens)
    joined, ready = lax.optimization_barrier((jnp.concatenate(direct, 0), ready))
    others = lax.ppermute(joined, axes, swap)
    ready = [*ready, *prepare_cotangent(episode_length, window_start, cotangent)]
    layer_out, tokens_grad, keep, send = layer([piece, *direct, others], ready)
    got = lax.ppermute(send, axes, swap)
    shape = jax.ShapeDtypeStruct((GRAD_ROWS, D), bf16)
    pairs = pl.pallas_call(
        pair_kernel, in_specs=[VMEM] * 2, out_specs=[VMEM] * 4, out_shape=[shape] * 4, compiler_params=SMALL, name="pair",
    )(keep, got)
    back = [across((BACK[0][k], BACK[1][k])) for k in range(4)]
    came = [lax.ppermute(pairs[k], axes, back[k]) for k in range(4)]
    merged = pl.pallas_call(
        merge_kernel, in_specs=[VMEM] * 5, out_specs=VMEM, out_shape=shape, compiler_params=SMALL, name="merge",
    )(pairs[0], *came)
    beside = lax.ppermute(merged, axes, swap)
    chip = pl.pallas_call(
        chip_kernel, in_specs=[VMEM] * 2, out_specs=VMEM, out_shape=shape, compiler_params=SMALL, name="chip",
    )(merged, beside)
    over = [(g * wide + i, (g ^ 2) * wide + i) for g in range(grp) for i in range(wide)]
    every = [chip, lax.ppermute(chip, axes, over)]
    grads = pl.pallas_call(
        finish_kernel, in_specs=[VMEM] * 2, out_specs=[VMEM] * 13,
        out_shape=[jax.ShapeDtypeStruct(p.shape, f32) for p in params], compiler_params=SMALL, name="finish",
    )(*every)
    return (layer_out, tokens_grad, *grads)


def gathered(tokens, episode_length, window_start, *rest):
    params, cotangent = rest[:13], rest[13]
    D = tokens.shape[2]
    full = [lax.all_gather(p, "wide", axis=0, tiled=True) for p in params]
    gain_a, shift_a, qkv, query, value, outw, outb, gain_m, shift_m, upw, upb, downw, downb = full
    FF = upw.shape[1]
    lanes = jnp.arange(D) // (D // PIECES)
    spots = (lanes[None, :] == jnp.arange(PIECES)[:, None]).astype(bf16)
    vectors = jnp.stack([gain_a, shift_a, query, value, outb, gain_m, shift_m, downb])[None] * spots[:, None, :]
    where_up = (jnp.arange(FF) // (FF // PIECES))[None, :] == jnp.arange(PIECES)[:, None]
    ups = (upb[None] * where_up.astype(bf16)).reshape(PIECES, FF // D, D)

    def blocks(weight):
        cut = weight.reshape(PIECES, weight.shape[0] // PIECES, weight.shape[1] // D, D)
        return cut.transpose(0, 2, 1, 3).reshape(PIECES, -1, D)

    slots = jnp.concatenate(
        [blocks(qkv), blocks(outw), blocks(upw), blocks(downw), vectors, ups, jnp.zeros((PIECES, 4, D), bf16)], 1
    )
    direct = [slots[SLOTS[1][0]]] + [slots[SLOTS[0][k]] for k in (1, 2, 3)]
    others = jnp.concatenate([jnp.zeros_like(slots[0])] + [slots[SLOTS[1][k]] for k in (1, 2, 3)], 0)
    ready = [*prepare_tokens(tokens), *prepare_cotangent(episode_length, window_start, cotangent)]
    layer_out, tokens_grad, keep, send = layer([slots[0], *direct, others], ready, spread_out=False)
    order = [0] * PIECES
    for half in (0, 1):
        for k in range(4):
            order[BACK[half][k]] = 4 * half + k
    pieces = jnp.concatenate([keep, send], 0)[jnp.array(order)].astype(f32)
    vec = pieces[0, 192:208] + pieces[0, 208:224]

    def rebuilt(first, last, weight):
        cut = pieces[:, first:last].reshape(PIECES, weight.shape[1] // D, weight.shape[0] // PIECES, D)
        return cut.transpose(0, 2, 1, 3).reshape(weight.shape)

    grads = (
        vec[0], vec[1], rebuilt(0, 48, qkv), vec[2], vec[3], rebuilt(48, 64, outw), vec[4], vec[5], vec[6],
        rebuilt(64, 128, upw), vec[8:12].reshape(FF), rebuilt(128, 192, downw), vec[7],
    )
    grads = [lax.psum_scatter(g, "wide", scatter_dimension=0, tiled=True) for g in grads]
    return (layer_out, tokens_grad, *lax.psum(grads, "grp"))


def solution(mesh):
    rows = P(("grp", "wide"), None, None)
    flat = P(("grp", "wide"))
    one, two = P("wide"), P("wide", None)
    params = (one, one, two, one, one, two, one, one, one, two, one, two, one)
    fits = mesh.shape["wide"] == PIECES and mesh.shape["grp"] == 4
    return jax.shard_map(
        per_device if fits else gathered, mesh=mesh, in_specs=(rows, flat, flat, *params, rows), out_specs=(rows, rows, *params), check_vma=False
    )
```

```python
import math
import functools

import jax
import jax.numpy as jnp
from jax import lax
from jax.experimental import pallas as pl
from jax.experimental.pallas import tpu as pltpu
from jax.sharding import PartitionSpec as P

HEADS = 4
EPS = 1e-05
CUBIC = 0.044715
TANH_SCALE = math.sqrt(2.0 / math.pi)
NEG_FILL = -1e30
LOG2E = math.log2(math.e)
f32, bf16 = jnp.float32, jnp.bfloat16
PIECES = 8
PIECE_ROWS = 208
GRAD_ROWS = 224
SLOTS = ((0, 4, 5, 6), (1, 2, 3, 7))
BACK = ((0, 6, 5, 4), (1, 7, 3, 2))

TILES = ((1, (0, 1)), (1, (2, 3)), (0, (0, 2)), (0, (1, 3)))
EARLY = (0, 2, 1, 3)


def place():
    return lax.axis_index("wide").astype(jnp.int32), jnp.bitwise_and(lax.axis_index("grp").astype(jnp.int32), 1)


def slot_of(core, k, table=SLOTS):
    return jnp.where(core == 0, table[0][k], table[1][k])


def nn(a, b):
    return lax.dot_general(a, b, (((1,), (0,)), ((), ())), preferred_element_type=f32)

def nt(a, b):
    return lax.dot_general(a, b, (((1,), (1,)), ((), ())), preferred_element_type=f32)

def norm(v):
    d = v.shape[0]
    off = v - jnp.sum(v, axis=0, keepdims=True) * (1.0 / d)
    r = lax.rsqrt(jnp.sum(off * off, axis=0, keepdims=True) * (1.0 / d) + EPS)
    return off * r, r

def norm_back(dy, gain, n, r):
    d = dy.shape[0]
    g = dy * gain
    mg = jnp.sum(g, axis=0, keepdims=True) * (1.0 / d)
    mgn = jnp.sum(g * n, axis=0, keepdims=True) * (1.0 / d)
    return r * (g - mg - n * mgn)

def tokens_kernel(x_in, ct_in, x_ref, n_ref, r_ref, ct_ref):
    count, T, D = x_in.shape
    for w in range(count):
        xT = x_in[w].astype(f32).T
        n, r = norm(xT)
        x_ref[w] = xT
        n_ref[w] = n
        r_ref[w] = jnp.broadcast_to(r, (8, T))
        ct_ref[w] = ct_in[w]


def cotangent_kernel(valid_ref, ct_in, up_ref, mask_ref):
    count, T, D = ct_in.shape
    H = T // 2
    for w in range(count):
        valid = valid_ref[w:w + 1, :]
        live = (lax.broadcasted_iota(jnp.int32, (1, T), 1) < jnp.concatenate([valid, valid], 1)).astype(f32)
        up_ref[w] = ct_in[w].astype(f32).T * live
        j = lax.broadcasted_iota(jnp.int32, (H, H), 0)
        tri = j <= lax.broadcasted_iota(jnp.int32, (H, H), 1)
        for k, seen in enumerate((tri & (j < valid), j < valid, tri & (j + H < valid))):
            mask_ref[w, H * k:H * k + H] = jnp.where(seen, 0.0, NEG_FILL).astype(bf16)


def layer_kernel(mine, others, x_ref, n_ref, r_ref, up_ref, mask_ref,
                 keep_ref, send_ref, act_ref, mid_ref, midg_ref, dn_ref, wdT, gain_ref, bias_ref,
                 wqkv, wqkvT, wo, woT, wup, wupT, wd, cols,
                 aqkv, ao, aup, ad, alng, *, wps, group, skew, spread_out):
    me, core = place() if spread_out else (jnp.int32(0), jnp.int32(0))
    D, T = x_ref.shape[1], x_ref.shape[2]
    H = T // 2
    E = D // HEADS
    FF = wup.shape[1]
    scale = E ** -0.5

    def start():
        vec = jnp.zeros((16, D), f32)
        places = [(slot_of(half, k), ref, PIECE_ROWS * k) for half, ref in ((core, mine), (1 - core, others)) for k in range(PIECES // 2)]
        for slot, ref, at in places:
            o = jnp.bitwise_xor(me, slot)
            r16 = pl.ds(pl.multiple_of(o * 16, 16), 16)
            get = lambda first, last: ref[at + first:at + last, :]
            for b in range(3):
                wqkv[r16, D * b:D * b + D] = get(16 * b, 16 * b + 16)
            wo[r16, :] = get(48, 64)
            for b in range(4):
                wup[r16, D * b:D * b + D] = get(64 + 16 * b, 80 + 16 * b)
            wd[pl.ds(pl.multiple_of(o * 64, 64), 64), :] = get(128, 192)
            vec = vec + get(192, 208).astype(f32)
        vecT = jnp.concatenate([vec, jnp.zeros((D - 16, D), f32)], 0).T
        lane = lax.broadcasted_iota(jnp.int32, (D, 16), 1)
        def col(k):
            return jnp.where(lane == k, vecT[:, 0:16], 0.0).astype(bf16)
        def full(k):
            return jnp.broadcast_to(vecT[:, k:k + 1], (D, T))
        for b in range(3):
            wqkvT[D * b:D * b + D, 0:D] = wqkv[:, D * b:D * b + D].T
        wqkvT[0:D, D:D + 16] = col(2)
        wqkvT[D:2 * D, D:D + 16] = jnp.zeros((D, 16), bf16)
        wqkvT[2 * D:3 * D, D:D + 16] = col(3)
        woT[:, 0:D] = wo[...].T
        woT[:, D:D + 16] = col(4)
        for b in range(4):
            wupT[D * b:D * b + D, 0:D] = wup[:, D * b:D * b + D].T
            wupT[D * b:D * b + D, D:D + 16] = col(8 + b)
            wdT[:, D * b:D * b + D] = wd[D * b:D * b + D, :].T
        bias_ref[...] = jnp.broadcast_to(vec[7:8, :], (8, D))
        gain_ref[...] = full(0)
        cols[0] = full(0)
        cols[1] = full(1)
        cols[2] = full(5)
        cols[3] = full(6)
        for ref in (aqkv, ao, aup, ad, alng):
            ref[...] = jnp.zeros(ref.shape, f32)

    start()
    ones = jnp.ones((16, T), bf16)
    eye2 = (lax.broadcasted_iota(jnp.int32, (H, T), 0) == jnp.bitwise_and(lax.broadcasted_iota(jnp.int32, (H, T), 1), H - 1)).astype(f32).astype(bf16)

    def spread(m, h):
        parts = []
        if h > 0:
            parts.append(jnp.zeros((E * h, m.shape[1]), bf16))
        parts.append(m)
        if h < HEADS - 1:
            parts.append(jnp.zeros((E * (HEADS - 1 - h), m.shape[1]), bf16))
        return jnp.concatenate(parts, 0)

    none = jnp.zeros((16, H), bf16)
    blank = jnp.zeros((E, H), bf16)

    def beside(m, g, first, put):
        part = m[E * g:E * g + E, H * first:H * first + H]
        return jnp.concatenate([part, blank] if put == 0 else [blank, part], 1)

    def stack_keys(m):
        return jnp.concatenate([beside(m, g, 0, g % 2) for g in EARLY], 0)

    def stack_early(m):
        return jnp.concatenate([beside(m, g, 0, g // 2) for g in EARLY], 0)

    def stack_late(m, p):
        return jnp.concatenate([beside(m, 2 * p, 1, 0), beside(m, 2 * p + 1, 1, 1)], 0)

    def window(w):
        idx = w
        n1, r1 = n_ref[idx], r_ref[idx, 0:1]
        a1 = (n1 * cols[0] + cols[1]).astype(bf16)
        a1g = jnp.concatenate([a1, ones], 0)
        yield
        qT = (nn(wqkvT[0:D, :], a1g) * (scale * LOG2E)).astype(bf16)
        kT = nn(wqkvT[D:2 * D, :], a1g).astype(bf16)
        vT = nn(wqkvT[2 * D:3 * D, :], a1g).astype(bf16)
        yield
        krow, vrow = kT.T, vT.T
        left = (jnp.concatenate([krow[0:H], mask_ref[idx, 0:H]], 1), jnp.concatenate([krow, mask_ref[idx, H:H + T]], 1))
        vrow1 = jnp.concatenate([vrow, jnp.ones((T, 16), bf16)], 1)
        yield
        exps = []
        for k, pair in TILES:
            cut = slice(H * k, H * k + H)
            right = jnp.concatenate([spread(qT[E * g:E * g + E, cut], g) for g in pair], 1)
            S = nn(left[k], jnp.concatenate([right, eye2], 0))
            exps.append(jnp.exp2(S - jnp.max(S, axis=0, keepdims=True)))
            yield
        lows = [exps[0].astype(bf16), exps[1].astype(bf16), jnp.concatenate([exps[2].astype(bf16), exps[3].astype(bf16)], 0)]
        tops = [nn(jnp.concatenate([vT[E * 2 * p:E * 2 * p + 2 * E], ones], 0), lows[p]) for p in (0, 1)]
        yield
        early = nn(jnp.concatenate([stack_keys(vT), jnp.concatenate([ones[:, 0:H], none], 1), jnp.concatenate([none, ones[:, 0:H]], 1)], 0), lows[2])
        att, invs = [], []
        for g in range(HEADS):
            top, low = tops[g // 2], early[4 * E + 16 * (g % 2):4 * E + 16 * (g % 2) + 1]
            cut, at = slice(H * (g % 2), H * (g % 2) + H), slice(H * (g // 2), H * (g // 2) + H)
            inv = 1.0 / jnp.concatenate([low[:, at], top[2 * E:2 * E + 1, cut]], 1)
            invs.append(inv)
            row = E * EARLY.index(g)
            att.append(jnp.concatenate([early[row:row + E, at], top[E * (g % 2):E * (g % 2) + E, cut]], 1) * inv)
        yield
        attT = jnp.concatenate(att, 0)
        attg = jnp.concatenate([attT.astype(bf16), ones], 0)
        mid = x_ref[idx] + nn(woT[...], attg)
        yield
        n2, r2 = norm(mid)
        a2 = (n2 * cols[2] + cols[3]).astype(bf16)
        a2g = jnp.concatenate([a2, ones], 0)
        upT = up_ref[idx]
        upb = upT.astype(bf16)
        yield
        acts, hgs = [], []
        for b in range(FF // D):
            blk = slice(D * b, D * b + D)
            hid = nn(wupT[blk, :], a2g)
            v2 = hid * hid
            s = 0.5 * jnp.tanh(hid * (TANH_SCALE + (TANH_SCALE * CUBIC) * v2)) + 0.5
            act = hid * s
            acts.append(act.astype(bf16))
            gp = s + act * (1.0 - s) * (2 * TANH_SCALE + (6 * TANH_SCALE * CUBIC) * v2)
            hgs.append((nn(wd[blk, :], upb) * gp).astype(bf16))
            yield
        actg = jnp.concatenate(acts + [ones], 0)
        hg = jnp.concatenate(hgs, 0)
        act_ref[w] = actg[0:FF]
        mid_ref[w] = mid
        yield
        yield (3, actg, upb)
        dn2 = nn(wup[...], hg)
        yield (2, a2g, hg)
        alng[0] += dn2 * n2
        midg = upT + norm_back(dn2, cols[2], n2, r2)
        midg_ref[w] = midg
        bg = midg.astype(bf16)
        yield
        yield (1, attg, bg)
        daT = nn(wo[...], bg)
        yield
        dq, dk, dv = [], [], []
        das, rows = [], []
        for h in range(HEADS):
            blk = slice(E * h, E * h + E)
            da = (daT[blk] * invs[h]).astype(bf16)
            inner = -jnp.sum(da.astype(f32) * att[h], axis=0, keepdims=True)
            hi = inner.astype(bf16).astype(f32)
            mi = (inner - hi).astype(bf16).astype(f32)
            lo = inner - hi - mi
            das.append(da)
            rows.append(jnp.concatenate([hi, mi, lo, jnp.zeros((13, T), f32)], 0).astype(bf16))
        yield
        daT2 = jnp.concatenate(das, 0)
        tiles = []
        for (k, pair), e in zip(TILES, exps):
            cut = slice(H * k, H * k + H)
            right = jnp.concatenate(
                [jnp.concatenate([spread(das[g][:, cut], g), rows[g][:, cut]], 0) for g in pair], 1)
            dP = nn(vrow1[0:H] if k == 0 else vrow1, right)
            tiles.append((e * dP).astype(bf16))
            yield
        tiles = [tiles[0], tiles[1], jnp.concatenate([tiles[2], tiles[3]], 0)]

        def by_query(m, tiles):
            tops = [nn(m[2 * E * p:2 * E * p + 2 * E], tiles[p]) for p in (0, 1)]
            low = nn(stack_keys(m), tiles[2])
            out = []
            for g in range(HEADS):
                at, cut, row = slice(H * (g // 2), H * (g // 2) + H), slice(H * (g % 2), H * (g % 2) + H), E * EARLY.index(g)
                out.append(jnp.concatenate([low[row:row + E, at], tops[g // 2][E * (g % 2):E * (g % 2) + E, cut]], 1))
            return out

        def by_key(m, tiles):
            tops = [nt(stack_late(m, p), tiles[p]) for p in (0, 1)]
            low = nt(stack_early(m), tiles[2])
            out = []
            for g in range(HEADS):
                at, row = slice(H * (g % 2), H * (g % 2) + H), E * EARLY.index(g)
                top = tops[g // 2][E * (g % 2):E * (g % 2) + E]
                out.append(jnp.concatenate([top[:, 0:H] + low[row:row + E, at], top[:, H:T]], 1))
            return out

        dq = [v * scale for v in by_query(kT, tiles)]
        yield
        dk = [v * (1.0 / LOG2E) for v in by_key(qT, tiles)]
        yield
        dv = by_key(daT2, lows)
        yield
        pg = jnp.concatenate(dq + dk + dv, 0).astype(bf16)
        dn1 = nn(wqkv[...], pg)
        yield (0, a1g, pg)
        alng[1] += dn1 * n1
        dn_ref[w] = dn1

    accs = (aqkv, ao, aup, ad)
    held = [[] for _ in accs]
    live_windows = [(w // group * skew, window(w)) for w in range(wps)]
    tick = 0
    while live_windows:
        still = []
        for start, gen in live_windows:
            if tick < start:
                still.append((start, gen))
                continue
            try:
                item = next(gen)
            except StopIteration:
                continue
            still.append((start, gen))
            if item is not None:
                held[item[0]].append(item[1:])
                if len(held[item[0]]) == group:
                    pairs = held[item[0]]
                    held[item[0]] = []
                    join = lambda k: pairs[0][k] if group == 1 else jnp.concatenate([p[k] for p in pairs], 1)
                    accs[item[0]][...] += nt(join(0), join(1))
        live_windows = still
        tick += 1

    def end():
        def row(k):
            a = alng[k]
            a = a[:, 0:H] + a[:, H:T]
            return jnp.sum(a.T, axis=0, keepdims=True)

        def shift(sums, weight):
            hi = sums.astype(bf16).astype(f32)
            mi = (sums - hi).astype(bf16).astype(f32)
            parts = jnp.concatenate([hi, mi, sums - hi - mi, jnp.zeros((13, sums.shape[1]), f32)], 0)
            return jnp.sum(nt(parts.astype(bf16), weight), axis=0, keepdims=True)

        vec = jnp.concatenate(
            [row(1), shift(aqkv[D:D + 1, :], wqkv[...]), aqkv[D:D + 1, 0:D], aqkv[D:D + 1, 2 * D:3 * D], ao[D:D + 1, :],
             row(0), shift(aup[D:D + 1, :], wup[...]), ad[FF:FF + 1, :]]
            + [aup[D:D + 1, D * b:D * b + D] for b in range(4)] + [jnp.zeros((4, D), f32)], 0)
        high = vec.astype(bf16)
        low = (vec - high.astype(f32)).astype(bf16)
        for k in range(PIECES // 2):
            for ref, half in ((keep_ref, core), (send_ref, 1 - core)):
                o = jnp.bitwise_xor(me, slot_of(half, k, BACK))
                r16 = pl.ds(pl.multiple_of(o * 16, 16), 16)
                for b in range(3):
                    ref[k, 16 * b:16 * b + 16, :] = aqkv[r16, D * b:D * b + D].astype(bf16)
                ref[k, 48:64, :] = ao[r16, :].astype(bf16)
                for b in range(4):
                    ref[k, 64 + 16 * b:80 + 16 * b, :] = aup[r16, D * b:D * b + D].astype(bf16)
                ref[k, 128:192, :] = ad[pl.ds(pl.multiple_of(o * 64, 64), 64), :].astype(bf16)
                ref[k, 192:208, :] = high
                ref[k, 208:224, :] = low

    end()

def prepare_tokens(x, ct):
    count, T, D = x.shape
    vmem = pl.BlockSpec(memory_space=pltpu.VMEM)
    turned = jax.ShapeDtypeStruct((count, D, T), f32)
    return pl.pallas_call(
        tokens_kernel,
        in_specs=[vmem] * 2,
        out_specs=[vmem] * 4,
        out_shape=[turned, turned, jax.ShapeDtypeStruct((count, 8, T), f32), jax.ShapeDtypeStruct(ct.shape, bf16)],
        compiler_params=pltpu.CompilerParams(vmem_limit_bytes=16 << 20),
        cost_estimate=pl.CostEstimate(flops=0, bytes_accessed=count * T * D * 40, transcendentals=0),
        name="prepare_tokens",
    )(x, ct)


def prepare_cotangent(valid, ct):
    count, T, D = ct.shape
    vmem = pl.BlockSpec(memory_space=pltpu.VMEM)
    return pl.pallas_call(
        cotangent_kernel,
        in_specs=[vmem] * 2,
        out_specs=[vmem] * 2,
        out_shape=[jax.ShapeDtypeStruct((count, D, T), f32), jax.ShapeDtypeStruct((count, T + T // 2, T // 2), bf16)],
        compiler_params=pltpu.CompilerParams(vmem_limit_bytes=16 << 20),
        cost_estimate=pl.CostEstimate(flops=0, bytes_accessed=count * T * D * 20, transcendentals=0),
        name="prepare_cotangent",
    )(valid, ct)


def results_kernel(act_ref, mid_ref, midg_ref, dn_ref, wdT, gain_ref, bias_ref, n_ref, r_ref, lo_ref, tg_ref, lo_buf, tg_buf, sems):
    copies = []
    for w in range(act_ref.shape[0]):
        lo_buf[w] = (mid_ref[w] + nn(wdT[...], act_ref[w])).T + bias_ref[0:1, :]
        tg_buf[w] = (midg_ref[w] + norm_back(dn_ref[w], gain_ref[...], n_ref[w], r_ref[w, 0:1])).T
        for k, (buf, ref) in enumerate(((lo_buf, lo_ref), (tg_buf, tg_ref))):
            copies.append(pltpu.make_async_copy(buf.at[w], ref.at[w], sems.at[k, w]))
            copies[-1].start()
    for copy in copies:
        copy.wait()


def layer(slots, ready, wps=8, group=4, skew=13, spread_out=True):
    count, D, T = ready[0].shape
    FF = 512
    vm = lambda s, d: pltpu.VMEM(s, d)
    vmem = pl.BlockSpec(memory_space=pltpu.VMEM)
    half = jax.ShapeDtypeStruct((PIECES // 2, GRAD_ROWS, D), bf16)
    turned = jax.ShapeDtypeStruct((count, D, T), f32)
    return pl.pallas_call(
        functools.partial(layer_kernel, wps=wps, group=group, skew=skew, spread_out=spread_out),
        in_specs=[vmem] * 7,
        out_specs=[vmem] * 9,
        out_shape=[half, half, jax.ShapeDtypeStruct((count, FF, T), bf16), turned, turned, turned,
                   jax.ShapeDtypeStruct((D, FF), bf16), jax.ShapeDtypeStruct((D, T), f32), jax.ShapeDtypeStruct((8, D), f32)],
        scratch_shapes=[
            vm((D, 3 * D), bf16), vm((3 * D, D + 16), bf16), vm((D, D), bf16), vm((D, D + 16), bf16),
            vm((D, FF), bf16), vm((FF, D + 16), bf16), vm((FF, D), bf16),
            vm((4, D, T), f32),
            vm((D + 16, 3 * D), f32), vm((D + 16, D), f32), vm((D + 16, FF), f32), vm((FF + 16, D), f32),
            vm((2, D, T), f32)],
        compiler_params=pltpu.CompilerParams(vmem_limit_bytes=20 << 20),
        name="layer",
    )(*slots, *ready)


def results(parts, ready):
    n, r = ready[1:3]
    count, D, T = n.shape
    vmem = pl.BlockSpec(memory_space=pltpu.VMEM)
    rows = jax.ShapeDtypeStruct((count, T, D), f32)
    return pl.pallas_call(
        results_kernel,
        in_specs=[vmem] * 9,
        out_specs=[pl.BlockSpec(memory_space=pl.ANY)] * 2,
        out_shape=[rows] * 2,
        scratch_shapes=[pltpu.VMEM((count, T, D), f32)] * 2 + [pltpu.SemaphoreType.DMA((2, count))],
        compiler_params=pltpu.CompilerParams(vmem_limit_bytes=16 << 20),
        cost_estimate=pl.CostEstimate(flops=2 * count * T * D * 512, bytes_accessed=count * T * D * 40, transcendentals=0),
        name="results",
    )(*parts, n, r)


VMEM = pl.BlockSpec(memory_space=pltpu.VMEM)
SMEM = pl.BlockSpec(memory_space=pltpu.SMEM)
HBM = pl.BlockSpec(memory_space=pltpu.HBM)
SMALL = pltpu.CompilerParams(vmem_limit_bytes=16 << 20)
ALONE = pltpu.CompilerParams(vmem_limit_bytes=60 << 20)


def pack_kernel(*refs, span):
    hbm, out_ref, valid_ref, held, sems = refs[:15], refs[15], refs[16], refs[17:32], refs[32]
    copies = [pltpu.make_async_copy(src, dst, sems.at[k]) for k, (src, dst) in enumerate(zip(hbm, held))]
    for copy in copies:
        copy.start()
    gain_a, shift_a, qkv, query, value, outw, outb, gain_m, shift_m, upw, upb, downw, downb, lens, starts = held
    me, core = place()
    D = out_ref.shape[1]
    row = lax.broadcasted_iota(jnp.int32, (16, D), 0)
    lane16 = lax.broadcasted_iota(jnp.int32, (16, D), 1)
    spot16 = (lane16 == row + 16 * me).astype(bf16)
    r64 = lax.broadcasted_iota(jnp.int32, (64, D), 0)
    l64 = lax.broadcasted_iota(jnp.int32, (64, D), 1)
    spot64 = (l64 == r64 + 64 * jnp.bitwise_and(me, 1)).astype(bf16)
    for copy in copies:
        copy.wait()
    for b in range(3):
        out_ref[16 * b:16 * b + 16, :] = qkv[:, D * b:D * b + D]
    out_ref[48:64, :] = outw[...]
    for b in range(4):
        out_ref[64 + 16 * b:80 + 16 * b, :] = upw[:, D * b:D * b + D]
    out_ref[128:192, :] = downw[...]
    total = jnp.zeros((16, D), f32)
    for k, ref in enumerate((gain_a, shift_a, query, value, outb, gain_m, shift_m, downb)):
        v = jnp.broadcast_to(ref[...].astype(f32).reshape(1, 16), (16, 16)).astype(bf16)
        total = total + jnp.where(row == k, nn(v, spot16), 0.0)
    v = jnp.broadcast_to(upb[...].astype(f32).reshape(1, 64), (16, 64)).astype(bf16)
    total = total + jnp.where(row == 8 + lax.shift_right_logical(me, 1), nn(v, spot64), 0.0)
    out_ref[192:208, :] = total.astype(bf16)
    for w in range(valid_ref.shape[0]):
        valid_ref[w:w + 1, :] = jnp.full((1, D), jnp.clip(lens[w] - starts[w], 1, span), jnp.int32)


def split_add(parts):
    total = parts[0].astype(f32)
    for p in parts[1:]:
        total = total + p.astype(f32)
    vec = total[192:208] + total[208:224]
    high = vec.astype(bf16)
    low = (vec - high.astype(f32)).astype(bf16)
    return total[0:192], vec, high, low


def pair_kernel(keep_ref, got_ref, *out_refs):
    for k, ref in enumerate(out_refs):
        main, vec, high, low = split_add([keep_ref[k], got_ref[k]])
        ref[0:192, :] = main.astype(bf16)
        ref[192:208, :] = high
        ref[208:224, :] = low


def merge_kernel(own_ref, r0, r1, r2, r3, out_ref):
    first = jnp.where(place()[1] == 0, own_ref[...].astype(f32), r0[...].astype(f32))
    main, vec, high, low = split_add([first, r1[...], r2[...], r3[...]])
    out_ref[0:192, :] = main.astype(bf16)
    out_ref[192:208, :] = high
    out_ref[208:224, :] = low


def chip_kernel(own_ref, got_ref, out_ref):
    main, vec, high, low = split_add([own_ref[...], got_ref[...]])
    out_ref[0:192, :] = main.astype(bf16)
    out_ref[192:208, :] = high
    out_ref[208:224, :] = low


def finish_kernel(m0, m1, gain_a, shift_a, qkv, query, value, outw, outb, gain_m, shift_m, upw, upb, downw, downb):
    me, core = place()
    D = m0.shape[1]
    main, vec, high, low = split_add([m0[...], m1[...]])
    for b in range(3):
        qkv[:, D * b:D * b + D] = main[16 * b:16 * b + 16]
    outw[...] = main[48:64]
    for b in range(4):
        upw[:, D * b:D * b + D] = main[64 + 16 * b:80 + 16 * b]
    downw[...] = main[128:192]
    turned = pltpu.roll(vec, jnp.bitwise_and(D - 16 * me, D - 1), 1)
    for k, ref in enumerate((gain_a, shift_a, query, value, outb, gain_m, shift_m, downb)):
        ref[...] = turned[k:k + 1, 0:16].reshape(16)
    row = lax.broadcasted_iota(jnp.int32, (16, D), 0)
    half = jnp.sum(jnp.where(row == 8 + lax.shift_right_logical(me, 1), vec, 0.0), axis=0, keepdims=True)
    half = jnp.where(jnp.bitwise_and(me, 1) == 0, half[:, 0:64], half[:, 64:128])
    upb[...] = half.reshape(64)


def per_device(tokens, episode_length, window_start, *rest):
    params, cotangent = rest[:13], rest[13]
    D = tokens.shape[2]
    grp, wide = lax.axis_size("grp"), lax.axis_size("wide")
    axes = ("grp", "wide")

    def across(core_slots, keep_own=False):
        pairs = []
        for g in range(grp):
            s = core_slots[g % 2]
            if s or keep_own:
                pairs += [(g * wide + i, g * wide + (i ^ s)) for i in range(wide)]
        return pairs

    swap = [(g * wide + i, (g ^ 1) * wide + i) for g in range(grp) for i in range(wide)]
    count = tokens.shape[0]
    piece, valid = pl.pallas_call(
        functools.partial(pack_kernel, span=tokens.shape[1]), in_specs=[HBM] * 15, out_specs=[VMEM] * 2,
        out_shape=[jax.ShapeDtypeStruct((PIECE_ROWS, D), bf16), jax.ShapeDtypeStruct((count, D), jnp.int32)],
        compiler_params=ALONE, name="pack",
        cost_estimate=pl.CostEstimate(flops=0, bytes_accessed=40 << 20, transcendentals=0),
        scratch_shapes=[pltpu.VMEM(p.shape, bf16) for p in params] + [pltpu.SMEM((count,), jnp.int32)] * 2
        + [pltpu.SemaphoreType.DMA((15,))],
    )(*params, episode_length, window_start)
    hops = [across((SLOTS[0][k], SLOTS[1][k]), True) for k in range(4)]
    direct = [lax.ppermute(piece, axes, hops[k]) for k in range(4)]
    *ready, ct_here = prepare_tokens(tokens, cotangent)
    joined, ready, ct_here = lax.optimization_barrier((jnp.concatenate(direct, 0), ready, ct_here))
    others = lax.ppermute(joined, axes, swap)
    ready = [*ready, *prepare_cotangent(valid, ct_here)]
    keep, send, *parts = layer([joined, others], ready)
    got = lax.ppermute(send, axes, swap)
    shape = jax.ShapeDtypeStruct((GRAD_ROWS, D), bf16)
    pairs = pl.pallas_call(
        pair_kernel, in_specs=[VMEM] * 2, out_specs=[VMEM] * 4, out_shape=[shape] * 4, compiler_params=SMALL, name="pair",
    )(keep, got)
    pairs, parts = lax.optimization_barrier((pairs, parts))
    layer_out, tokens_grad = results(parts, ready)
    back = [across((BACK[0][k], BACK[1][k])) for k in range(4)]
    came = [lax.ppermute(pairs[k], axes, back[k]) for k in range(4)]
    merged = pl.pallas_call(
        merge_kernel, in_specs=[VMEM] * 5, out_specs=VMEM, out_shape=shape, compiler_params=SMALL, name="merge",
    )(pairs[0], *came)
    beside = lax.ppermute(merged, axes, swap)
    chip = pl.pallas_call(
        chip_kernel, in_specs=[VMEM] * 2, out_specs=VMEM, out_shape=shape, compiler_params=SMALL, name="chip",
    )(merged, beside)
    over = [(g * wide + i, (g ^ 2) * wide + i) for g in range(grp) for i in range(wide)]
    every = [chip, lax.ppermute(chip, axes, over)]
    grads = pl.pallas_call(
        finish_kernel, in_specs=[VMEM] * 2, out_specs=[VMEM] * 13,
        out_shape=[jax.ShapeDtypeStruct(p.shape, f32) for p in params], compiler_params=SMALL, name="finish",
    )(*every)
    return (layer_out, tokens_grad, *grads)


def gathered(tokens, episode_length, window_start, *rest):
    params, cotangent = rest[:13], rest[13]
    D = tokens.shape[2]
    full = [lax.all_gather(p, "wide", axis=0, tiled=True) for p in params]
    gain_a, shift_a, qkv, query, value, outw, outb, gain_m, shift_m, upw, upb, downw, downb = full
    FF = upw.shape[1]
    lanes = jnp.arange(D) // (D // PIECES)
    spots = (lanes[None, :] == jnp.arange(PIECES)[:, None]).astype(bf16)
    vectors = jnp.stack([gain_a, shift_a, query, value, outb, gain_m, shift_m, downb])[None] * spots[:, None, :]
    where_up = (jnp.arange(FF) // (FF // PIECES))[None, :] == jnp.arange(PIECES)[:, None]
    ups = (upb[None] * where_up.astype(bf16)).reshape(PIECES, FF // D, D)

    def blocks(weight):
        cut = weight.reshape(PIECES, weight.shape[0] // PIECES, weight.shape[1] // D, D)
        return cut.transpose(0, 2, 1, 3).reshape(PIECES, -1, D)

    slots = jnp.concatenate(
        [blocks(qkv), blocks(outw), blocks(upw), blocks(downw), vectors, ups, jnp.zeros((PIECES, 4, D), bf16)], 1
    )
    mine, others = [jnp.concatenate([slots[s] for s in half], 0) for half in SLOTS]
    count, span = tokens.shape[:2]
    valid = jnp.broadcast_to(jnp.clip(episode_length - window_start, 1, span)[:, None], (count, D))
    *ready, ct_here = prepare_tokens(tokens, cotangent)
    ready = [*ready, *prepare_cotangent(valid, ct_here)]
    keep, send, *parts = layer([mine, others], ready, spread_out=False)
    layer_out, tokens_grad = results(parts, ready)
    order = [0] * PIECES
    for half in (0, 1):
        for k in range(4):
            order[BACK[half][k]] = 4 * half + k
    pieces = jnp.concatenate([keep, send], 0)[jnp.array(order)].astype(f32)
    vec = pieces[0, 192:208] + pieces[0, 208:224]

    def rebuilt(first, last, weight):
        cut = pieces[:, first:last].reshape(PIECES, weight.shape[1] // D, weight.shape[0] // PIECES, D)
        return cut.transpose(0, 2, 1, 3).reshape(weight.shape)

    grads = (
        vec[0], vec[1], rebuilt(0, 48, qkv), vec[2], vec[3], rebuilt(48, 64, outw), vec[4], vec[5], vec[6],
        rebuilt(64, 128, upw), vec[8:12].reshape(FF), rebuilt(128, 192, downw), vec[7],
    )
    grads = [lax.psum_scatter(g, "wide", scatter_dimension=0, tiled=True) for g in grads]
    return (layer_out, tokens_grad, *lax.psum(grads, "grp"))


def solution(mesh):
    rows = P(("grp", "wide"), None, None)
    flat = P(("grp", "wide"))
    one, two = P("wide"), P("wide", None)
    params = (one, one, two, one, one, two, one, one, one, two, one, two, one)
    fits = mesh.shape["wide"] == PIECES and mesh.shape["grp"] == 4
    return jax.shard_map(
        per_device if fits else gathered, mesh=mesh, in_specs=(rows, flat, flat, *params, rows), out_specs=(rows, rows, *params), check_vma=False
    )
```

```python
import math
import functools

import jax
import jax.numpy as jnp
from jax import lax
from jax.experimental import pallas as pl
from jax.experimental.pallas import tpu as pltpu
from jax.sharding import PartitionSpec as P

HEADS = 4
EPS = 1e-05
CUBIC = 0.044715
TANH_SCALE = math.sqrt(2.0 / math.pi)
NEG_FILL = -1e30
LOG2E = math.log2(math.e)
f32, bf16 = jnp.float32, jnp.bfloat16
PIECES = 8
PIECE_ROWS = 208
GRAD_ROWS = 224
SLOTS = ((0, 4, 5, 6), (1, 2, 3, 7))
BACK = ((0, 6, 5, 4), (1, 7, 3, 2))

TURNED = (0, 1, 2, 3)
TILES = ((1, (0, 1)), (1, (2, 3)), (0, (0, 2)), (0, (1, 3)))
EARLY = (0, 2, 1, 3)


def place():
    return lax.axis_index("wide").astype(jnp.int32), jnp.bitwise_and(lax.axis_index("grp").astype(jnp.int32), 1)


def slot_of(core, k, table=SLOTS):
    return jnp.where(core == 0, table[0][k], table[1][k])


def nn(a, b):
    return lax.dot_general(a, b, (((1,), (0,)), ((), ())), preferred_element_type=f32)

def nt(a, b):
    return lax.dot_general(a, b, (((1,), (1,)), ((), ())), preferred_element_type=f32)

def norm(v):
    d = v.shape[0]
    off = v - jnp.sum(v, axis=0, keepdims=True) * (1.0 / d)
    r = lax.rsqrt(jnp.sum(off * off, axis=0, keepdims=True) * (1.0 / d) + EPS)
    return off * r, r

def norm_back(dy, gain, n, r):
    d = dy.shape[0]
    g = dy * gain
    mg = jnp.sum(g, axis=0, keepdims=True) * (1.0 / d)
    mgn = jnp.sum(g * n, axis=0, keepdims=True) * (1.0 / d)
    return r * (g - mg - n * mgn)

def tokens_kernel(x_in, ct_in, x_ref, n_ref, r_ref, ct_ref):
    count, T, D = x_in.shape
    for w in range(count):
        xT = x_in[w].astype(f32).T
        n, r = norm(xT)
        x_ref[w] = xT
        n_ref[w] = n
        r_ref[w] = jnp.broadcast_to(r, (8, T))
        ct_ref[w] = ct_in[w]


def cotangent_kernel(valid_ref, ct_in, up_ref, mask_ref):
    count, T, D = ct_in.shape
    H = T // 2
    for w in range(count):
        valid = valid_ref[w:w + 1, :]
        live = (lax.broadcasted_iota(jnp.int32, (1, T), 1) < jnp.concatenate([valid, valid], 1)).astype(f32)
        up_ref[w] = ct_in[w].astype(f32).T * live
        j = lax.broadcasted_iota(jnp.int32, (H, H), 0)
        tri = j <= lax.broadcasted_iota(jnp.int32, (H, H), 1)
        for k, seen in enumerate((tri & (j < valid), j < valid, tri & (j + H < valid))):
            mask_ref[w, H * k:H * k + H] = jnp.where(seen, 0.0, NEG_FILL).astype(bf16)


def layer_kernel(mine, others, x_ref, n_ref, r_ref, up_ref, mask_ref,
                 keep_ref, send_ref, act_ref, mid_ref, midg_ref, dn_ref, wdT, gain_ref, bias_ref,
                 wqkv, wqkvT, wo, woT, wup, wupT, wd, cols,
                 aqkv, ao, aup, ad, alng, turn, t0, t1, t2, t3, *, wps, group, skew, spread_out):
    me, core = place() if spread_out else (jnp.int32(0), jnp.int32(0))
    D, T = x_ref.shape[1], x_ref.shape[2]
    H = T // 2
    E = D // HEADS
    FF = wup.shape[1]
    scale = E ** -0.5

    def start():
        vec = jnp.zeros((16, D), f32)
        places = [(slot_of(half, k), ref, PIECE_ROWS * k) for half, ref in ((core, mine), (1 - core, others)) for k in range(PIECES // 2)]
        for slot, ref, at in places:
            o = jnp.bitwise_xor(me, slot)
            r16 = pl.ds(pl.multiple_of(o * 16, 16), 16)
            get = lambda first, last: ref[at + first:at + last, :]
            for b in range(3):
                wqkv[r16, D * b:D * b + D] = get(16 * b, 16 * b + 16)
            wo[r16, :] = get(48, 64)
            for b in range(4):
                wup[r16, D * b:D * b + D] = get(64 + 16 * b, 80 + 16 * b)
            wd[pl.ds(pl.multiple_of(o * 64, 64), 64), :] = get(128, 192)
            vec = vec + get(192, 208).astype(f32)
        vecT = jnp.concatenate([vec, jnp.zeros((D - 16, D), f32)], 0).T
        lane = lax.broadcasted_iota(jnp.int32, (D, 16), 1)
        def col(k):
            return jnp.where(lane == k, vecT[:, 0:16], 0.0).astype(bf16)
        def full(k):
            return jnp.broadcast_to(vecT[:, k:k + 1], (D, T))
        for b in range(3):
            wqkvT[D * b:D * b + D, 0:D] = wqkv[:, D * b:D * b + D].T
        wqkvT[0:D, D:D + 16] = col(2)
        wqkvT[D:2 * D, D:D + 16] = jnp.zeros((D, 16), bf16)
        wqkvT[2 * D:3 * D, D:D + 16] = col(3)
        woT[:, 0:D] = wo[...].T
        woT[:, D:D + 16] = col(4)
        for b in range(4):
            wupT[D * b:D * b + D, 0:D] = wup[:, D * b:D * b + D].T
            wupT[D * b:D * b + D, D:D + 16] = col(8 + b)
            wdT[:, D * b:D * b + D] = wd[D * b:D * b + D, :].T
        bias_ref[...] = jnp.broadcast_to(vec[7:8, :], (8, D))
        gain_ref[...] = full(0)
        cols[0] = full(0)
        cols[1] = full(1)
        cols[2] = full(5)
        cols[3] = full(6)
        for ref in (aqkv, ao, aup, ad, alng):
            ref[...] = jnp.zeros(ref.shape, f32)

    start()
    ones = jnp.ones((16, T), bf16)
    eye2 = (lax.broadcasted_iota(jnp.int32, (H, T), 0) == jnp.bitwise_and(lax.broadcasted_iota(jnp.int32, (H, T), 1), H - 1)).astype(f32).astype(bf16)

    def spread(m, h):
        parts = []
        if h > 0:
            parts.append(jnp.zeros((E * h, m.shape[1]), bf16))
        parts.append(m)
        if h < HEADS - 1:
            parts.append(jnp.zeros((E * (HEADS - 1 - h), m.shape[1]), bf16))
        return jnp.concatenate(parts, 0)

    none = jnp.zeros((16, H), bf16)
    blank = jnp.zeros((E, H), bf16)

    def beside(m, g, first, put):
        part = m[E * g:E * g + E, H * first:H * first + H]
        return jnp.concatenate([part, blank] if put == 0 else [blank, part], 1)

    def stack_keys(m):
        return jnp.concatenate([beside(m, g, 0, g % 2) for g in EARLY], 0)

    def stack_early(m):
        return jnp.concatenate([beside(m, g, 0, g // 2) for g in EARLY], 0)

    def stack_late(m, p):
        return jnp.concatenate([beside(m, 2 * p, 1, 0), beside(m, 2 * p + 1, 1, 1)], 0)

    def window(w):
        idx = w
        n1, r1 = n_ref[idx], r_ref[idx, 0:1]
        a1 = (n1 * cols[0] + cols[1]).astype(bf16)
        a1g = jnp.concatenate([a1, ones], 0)
        yield
        qT = (nn(wqkvT[0:D, :], a1g) * (scale * LOG2E)).astype(bf16)
        kT = nn(wqkvT[D:2 * D, :], a1g).astype(bf16)
        vT = nn(wqkvT[2 * D:3 * D, :], a1g).astype(bf16)
        yield
        krow, vrow = kT.T, vT.T
        left = (jnp.concatenate([krow[0:H], mask_ref[idx, 0:H]], 1), jnp.concatenate([krow, mask_ref[idx, H:H + T]], 1))
        vrow1 = jnp.concatenate([vrow, jnp.ones((T, 16), bf16)], 1)
        yield
        exps = []
        for k, pair in TILES:
            cut = slice(H * k, H * k + H)
            right = jnp.concatenate([spread(qT[E * g:E * g + E, cut], g) for g in pair], 1)
            S = nn(left[k], jnp.concatenate([right, eye2], 0))
            exps.append(jnp.exp2(S - jnp.max(S, axis=0, keepdims=True)))
            yield
        lows = [exps[0].astype(bf16), exps[1].astype(bf16), jnp.concatenate([exps[2].astype(bf16), exps[3].astype(bf16)], 0)]
        tops = [nn(jnp.concatenate([vT[E * 2 * p:E * 2 * p + 2 * E], ones], 0), lows[p]) for p in (0, 1)]
        yield
        early = nn(jnp.concatenate([stack_keys(vT), jnp.concatenate([ones[:, 0:H], none], 1), jnp.concatenate([none, ones[:, 0:H]], 1)], 0), lows[2])
        att, invs = [], []
        for g in range(HEADS):
            top, low = tops[g // 2], early[4 * E + 16 * (g % 2):4 * E + 16 * (g % 2) + 1]
            cut, at = slice(H * (g % 2), H * (g % 2) + H), slice(H * (g // 2), H * (g // 2) + H)
            inv = 1.0 / jnp.concatenate([low[:, at], top[2 * E:2 * E + 1, cut]], 1)
            invs.append(inv)
            row = E * EARLY.index(g)
            att.append(jnp.concatenate([early[row:row + E, at], top[E * (g % 2):E * (g % 2) + E, cut]], 1) * inv)
        yield
        attT = jnp.concatenate(att, 0)
        attg = jnp.concatenate([attT.astype(bf16), ones], 0)
        mid = x_ref[idx] + nn(woT[...], attg)
        yield
        n2, r2 = norm(mid)
        a2 = (n2 * cols[2] + cols[3]).astype(bf16)
        a2g = jnp.concatenate([a2, ones], 0)
        upT = up_ref[idx]
        upb = upT.astype(bf16)
        yield
        acts, hgs = [], []
        for b in range(FF // D):
            blk = slice(D * b, D * b + D)
            hid = nn(wupT[blk, :], a2g)
            v2 = hid * hid
            s = 0.5 * jnp.tanh(hid * (TANH_SCALE + (TANH_SCALE * CUBIC) * v2)) + 0.5
            act = hid * s
            acts.append(act.astype(bf16))
            gp = s + act * (1.0 - s) * (2 * TANH_SCALE + (6 * TANH_SCALE * CUBIC) * v2)
            hgs.append((nn(wd[blk, :], upb) * gp).astype(bf16))
            yield
        actg = jnp.concatenate(acts + [ones], 0)
        hg = jnp.concatenate(hgs, 0)
        act_ref[w] = actg[0:FF]
        mid_ref[w] = mid
        yield
        yield (3, actg, upb)
        dn2 = nn(wup[...], hg)
        yield (2, a2g, hg)
        alng[0] += dn2 * n2
        midg = upT + norm_back(dn2, cols[2], n2, r2)
        midg_ref[w] = midg
        bg = midg.astype(bf16)
        yield
        yield (1, attg, bg)
        daT = nn(wo[...], bg)
        yield
        dq, dk, dv = [], [], []
        das, rows = [], []
        for h in range(HEADS):
            blk = slice(E * h, E * h + E)
            da = (daT[blk] * invs[h]).astype(bf16)
            inner = -jnp.sum(da.astype(f32) * att[h], axis=0, keepdims=True)
            hi = inner.astype(bf16).astype(f32)
            mi = (inner - hi).astype(bf16).astype(f32)
            lo = inner - hi - mi
            das.append(da)
            rows.append(jnp.concatenate([hi, mi, lo, jnp.zeros((13, T), f32)], 0).astype(bf16))
        yield
        daT2 = jnp.concatenate(das, 0)
        tiles = []
        for (k, pair), e in zip(TILES, exps):
            cut = slice(H * k, H * k + H)
            right = jnp.concatenate(
                [jnp.concatenate([spread(das[g][:, cut], g), rows[g][:, cut]], 0) for g in pair], 1)
            dP = nn(vrow1[0:H] if k == 0 else vrow1, right)
            tiles.append((e * dP).astype(bf16))
            yield
        tiles = [tiles[0], tiles[1], jnp.concatenate([tiles[2], tiles[3]], 0)]

        def by_query(m, tiles):
            tops = [nn(m[2 * E * p:2 * E * p + 2 * E], tiles[p]) for p in (0, 1)]
            low = nn(stack_keys(m), tiles[2])
            out = []
            for g in range(HEADS):
                at, cut, row = slice(H * (g // 2), H * (g // 2) + H), slice(H * (g % 2), H * (g % 2) + H), E * EARLY.index(g)
                out.append(jnp.concatenate([low[row:row + E, at], tops[g // 2][E * (g % 2):E * (g % 2) + E, cut]], 1))
            return out

        def by_key(m, tiles, which):
            for p in range(3):
                turn[w, 3 * which + p] = tiles[p].T
            tops = [nn(stack_late(m, p), turn[w, 3 * which + p]) for p in (0, 1)]
            low = nn(stack_early(m), turn[w, 3 * which + 2])
            out = []
            for g in range(HEADS):
                at, row = slice(H * (g % 2), H * (g % 2) + H), E * EARLY.index(g)
                top = tops[g // 2][E * (g % 2):E * (g % 2) + E]
                out.append(jnp.concatenate([top[:, 0:H] + low[row:row + E, at], top[:, H:T]], 1))
            return out

        dq = [v * scale for v in by_query(kT, tiles)]
        yield
        dk = [v * (1.0 / LOG2E) for v in by_key(qT, tiles, 0)]
        yield
        dv = by_key(daT2, lows, 1)
        yield
        pg = jnp.concatenate(dq + dk + dv, 0).astype(bf16)
        dn1 = nn(wqkv[...], pg)
        yield (0, a1g, pg)
        alng[1] += dn1 * n1
        dn_ref[w] = dn1

    accs = (aqkv, ao, aup, ad)
    turns = (t0, t1, t2, t3)
    held = [[] for _ in accs]
    live_windows = [(w // group * skew, window(w)) for w in range(wps)]
    tick = 0
    while live_windows:
        still = []
        for start, gen in live_windows:
            if tick < start:
                still.append((start, gen))
                continue
            try:
                item = next(gen)
            except StopIteration:
                continue
            still.append((start, gen))
            if item is not None:
                k, left, right = item
                at = len(held[k])
                if k in TURNED:
                    turns[k][at] = right.T
                held[k].append((left, right))
                if at + 1 == group:
                    join = lambda m: jnp.concatenate([p[m] for p in held[k]], 1) if group > 1 else held[k][0][m]
                    if k in TURNED:
                        accs[k][...] += nn(join(0), turns[k][...].reshape(group * T, right.shape[0]))
                    else:
                        accs[k][...] += nt(join(0), join(1))
                    held[k] = []
        live_windows = still
        tick += 1

    def end():
        def row(k):
            a = alng[k]
            a = a[:, 0:H] + a[:, H:T]
            return jnp.sum(a.T, axis=0, keepdims=True)

        def shift(sums, weight):
            hi = sums.astype(bf16).astype(f32)
            mi = (sums - hi).astype(bf16).astype(f32)
            parts = jnp.concatenate([hi, mi, sums - hi - mi, jnp.zeros((13, sums.shape[1]), f32)], 0)
            return jnp.sum(nt(parts.astype(bf16), weight), axis=0, keepdims=True)

        vec = jnp.concatenate(
            [row(1), shift(aqkv[D:D + 1, :], wqkv[...]), aqkv[D:D + 1, 0:D], aqkv[D:D + 1, 2 * D:3 * D], ao[D:D + 1, :],
             row(0), shift(aup[D:D + 1, :], wup[...]), ad[FF:FF + 1, :]]
            + [aup[D:D + 1, D * b:D * b + D] for b in range(4)] + [jnp.zeros((4, D), f32)], 0)
        high = vec.astype(bf16)
        low = (vec - high.astype(f32)).astype(bf16)
        for k in range(PIECES // 2):
            for ref, half in ((keep_ref, core), (send_ref, 1 - core)):
                o = jnp.bitwise_xor(me, slot_of(half, k, BACK))
                r16 = pl.ds(pl.multiple_of(o * 16, 16), 16)
                for b in range(3):
                    ref[k, 16 * b:16 * b + 16, :] = aqkv[r16, D * b:D * b + D].astype(bf16)
                ref[k, 48:64, :] = ao[r16, :].astype(bf16)
                for b in range(4):
                    ref[k, 64 + 16 * b:80 + 16 * b, :] = aup[r16, D * b:D * b + D].astype(bf16)
                ref[k, 128:192, :] = ad[pl.ds(pl.multiple_of(o * 64, 64), 64), :].astype(bf16)
                ref[k, 192:208, :] = high
                ref[k, 208:224, :] = low

    end()

def prepare_tokens(x, ct):
    count, T, D = x.shape
    vmem = pl.BlockSpec(memory_space=pltpu.VMEM)
    turned = jax.ShapeDtypeStruct((count, D, T), f32)
    return pl.pallas_call(
        tokens_kernel,
        in_specs=[vmem] * 2,
        out_specs=[vmem] * 4,
        out_shape=[turned, turned, jax.ShapeDtypeStruct((count, 8, T), f32), jax.ShapeDtypeStruct(ct.shape, bf16)],
        compiler_params=pltpu.CompilerParams(vmem_limit_bytes=16 << 20),
        cost_estimate=pl.CostEstimate(flops=0, bytes_accessed=count * T * D * 40, transcendentals=0),
        name="prepare_tokens",
    )(x, ct)


def prepare_cotangent(valid, ct):
    count, T, D = ct.shape
    vmem = pl.BlockSpec(memory_space=pltpu.VMEM)
    return pl.pallas_call(
        cotangent_kernel,
        in_specs=[vmem] * 2,
        out_specs=[vmem] * 2,
        out_shape=[jax.ShapeDtypeStruct((count, D, T), f32), jax.ShapeDtypeStruct((count, T + T // 2, T // 2), bf16)],
        compiler_params=pltpu.CompilerParams(vmem_limit_bytes=16 << 20),
        cost_estimate=pl.CostEstimate(flops=0, bytes_accessed=count * T * D * 20, transcendentals=0),
        name="prepare_cotangent",
    )(valid, ct)


def results_kernel(act_ref, mid_ref, midg_ref, dn_ref, wdT, gain_ref, bias_ref, n_ref, r_ref, lo_ref, tg_ref, lo_buf, tg_buf, sems):
    copies = []
    for w in range(act_ref.shape[0]):
        lo_buf[w] = (mid_ref[w] + nn(wdT[...], act_ref[w])).T + bias_ref[0:1, :]
        tg_buf[w] = (midg_ref[w] + norm_back(dn_ref[w], gain_ref[...], n_ref[w], r_ref[w, 0:1])).T
        for k, (buf, ref) in enumerate(((lo_buf, lo_ref), (tg_buf, tg_ref))):
            copies.append(pltpu.make_async_copy(buf.at[w], ref.at[w], sems.at[k, w]))
            copies[-1].start()
    for copy in copies:
        copy.wait()


def layer(slots, ready, wps=8, group=4, skew=13, spread_out=True):
    count, D, T = ready[0].shape
    FF = 512
    vm = lambda s, d: pltpu.VMEM(s, d)
    vmem = pl.BlockSpec(memory_space=pltpu.VMEM)
    half = jax.ShapeDtypeStruct((PIECES // 2, GRAD_ROWS, D), bf16)
    turned = jax.ShapeDtypeStruct((count, D, T), f32)
    return pl.pallas_call(
        functools.partial(layer_kernel, wps=wps, group=group, skew=skew, spread_out=spread_out),
        in_specs=[vmem] * 7,
        out_specs=[vmem] * 9,
        out_shape=[half, half, jax.ShapeDtypeStruct((count, FF, T), bf16), turned, turned, turned,
                   jax.ShapeDtypeStruct((D, FF), bf16), jax.ShapeDtypeStruct((D, T), f32), jax.ShapeDtypeStruct((8, D), f32)],
        scratch_shapes=[
            vm((D, 3 * D), bf16), vm((3 * D, D + 16), bf16), vm((D, D), bf16), vm((D, D + 16), bf16),
            vm((D, FF), bf16), vm((FF, D + 16), bf16), vm((FF, D), bf16),
            vm((4, D, T), f32),
            vm((D + 16, 3 * D), f32), vm((D + 16, D), f32), vm((D + 16, FF), f32), vm((FF + 16, D), f32),
            vm((2, D, T), f32), vm((count, 6, T, T), bf16),
            vm((group, T, 3 * D), bf16), vm((group, T, D), bf16), vm((group, T, FF), bf16), vm((group, T, D), bf16)],
        compiler_params=pltpu.CompilerParams(vmem_limit_bytes=32 << 20),
        name="layer",
    )(*slots, *ready)


def results(parts, ready):
    n, r = ready[1:3]
    count, D, T = n.shape
    vmem = pl.BlockSpec(memory_space=pltpu.VMEM)
    rows = jax.ShapeDtypeStruct((count, T, D), f32)
    return pl.pallas_call(
        results_kernel,
        in_specs=[vmem] * 9,
        out_specs=[pl.BlockSpec(memory_space=pl.ANY)] * 2,
        out_shape=[rows] * 2,
        scratch_shapes=[pltpu.VMEM((count, T, D), f32)] * 2 + [pltpu.SemaphoreType.DMA((2, count))],
        compiler_params=pltpu.CompilerParams(vmem_limit_bytes=16 << 20),
        cost_estimate=pl.CostEstimate(flops=2 * count * T * D * 512, bytes_accessed=count * T * D * 40, transcendentals=0),
        name="results",
    )(*parts, n, r)


VMEM = pl.BlockSpec(memory_space=pltpu.VMEM)
SMEM = pl.BlockSpec(memory_space=pltpu.SMEM)
HBM = pl.BlockSpec(memory_space=pltpu.HBM)
SMALL = pltpu.CompilerParams(vmem_limit_bytes=16 << 20)
ALONE = pltpu.CompilerParams(vmem_limit_bytes=60 << 20)


def pack_kernel(*refs, span):
    hbm, out_ref, valid_ref, held, sems = refs[:15], refs[15], refs[16], refs[17:32], refs[32]
    copies = [pltpu.make_async_copy(src, dst, sems.at[k]) for k, (src, dst) in enumerate(zip(hbm, held))]
    for copy in copies:
        copy.start()
    gain_a, shift_a, qkv, query, value, outw, outb, gain_m, shift_m, upw, upb, downw, downb, lens, starts = held
    me, core = place()
    D = out_ref.shape[1]
    row = lax.broadcasted_iota(jnp.int32, (16, D), 0)
    lane16 = lax.broadcasted_iota(jnp.int32, (16, D), 1)
    spot16 = (lane16 == row + 16 * me).astype(bf16)
    r64 = lax.broadcasted_iota(jnp.int32, (64, D), 0)
    l64 = lax.broadcasted_iota(jnp.int32, (64, D), 1)
    spot64 = (l64 == r64 + 64 * jnp.bitwise_and(me, 1)).astype(bf16)
    for copy in copies:
        copy.wait()
    for b in range(3):
        out_ref[16 * b:16 * b + 16, :] = qkv[:, D * b:D * b + D]
    out_ref[48:64, :] = outw[...]
    for b in range(4):
        out_ref[64 + 16 * b:80 + 16 * b, :] = upw[:, D * b:D * b + D]
    out_ref[128:192, :] = downw[...]
    total = jnp.zeros((16, D), f32)
    for k, ref in enumerate((gain_a, shift_a, query, value, outb, gain_m, shift_m, downb)):
        v = jnp.broadcast_to(ref[...].astype(f32).reshape(1, 16), (16, 16)).astype(bf16)
        total = total + jnp.where(row == k, nn(v, spot16), 0.0)
    v = jnp.broadcast_to(upb[...].astype(f32).reshape(1, 64), (16, 64)).astype(bf16)
    total = total + jnp.where(row == 8 + lax.shift_right_logical(me, 1), nn(v, spot64), 0.0)
    out_ref[192:208, :] = total.astype(bf16)
    for w in range(valid_ref.shape[0]):
        valid_ref[w:w + 1, :] = jnp.full((1, D), jnp.clip(lens[w] - starts[w], 1, span), jnp.int32)


def split_add(parts):
    total = parts[0].astype(f32)
    for p in parts[1:]:
        total = total + p.astype(f32)
    vec = total[192:208] + total[208:224]
    high = vec.astype(bf16)
    low = (vec - high.astype(f32)).astype(bf16)
    return total[0:192], vec, high, low


def pair_kernel(keep_ref, got_ref, *out_refs):
    for k, ref in enumerate(out_refs):
        main, vec, high, low = split_add([keep_ref[k], got_ref[k]])
        ref[0:192, :] = main.astype(bf16)
        ref[192:208, :] = high
        ref[208:224, :] = low


def merge_kernel(own_ref, r0, r1, r2, r3, out_ref):
    first = jnp.where(place()[1] == 0, own_ref[...].astype(f32), r0[...].astype(f32))
    main, vec, high, low = split_add([first, r1[...], r2[...], r3[...]])
    out_ref[0:192, :] = main.astype(bf16)
    out_ref[192:208, :] = high
    out_ref[208:224, :] = low


def chip_kernel(own_ref, got_ref, out_ref):
    main, vec, high, low = split_add([own_ref[...], got_ref[...]])
    out_ref[0:192, :] = main.astype(bf16)
    out_ref[192:208, :] = high
    out_ref[208:224, :] = low


def finish_kernel(m0, m1, gain_a, shift_a, qkv, query, value, outw, outb, gain_m, shift_m, upw, upb, downw, downb):
    me, core = place()
    D = m0.shape[1]
    main, vec, high, low = split_add([m0[...], m1[...]])
    for b in range(3):
        qkv[:, D * b:D * b + D] = main[16 * b:16 * b + 16]
    outw[...] = main[48:64]
    for b in range(4):
        upw[:, D * b:D * b + D] = main[64 + 16 * b:80 + 16 * b]
    downw[...] = main[128:192]
    turned = pltpu.roll(vec, jnp.bitwise_and(D - 16 * me, D - 1), 1)
    for k, ref in enumerate((gain_a, shift_a, query, value, outb, gain_m, shift_m, downb)):
        ref[...] = turned[k:k + 1, 0:16].reshape(16)
    row = lax.broadcasted_iota(jnp.int32, (16, D), 0)
    half = jnp.sum(jnp.where(row == 8 + lax.shift_right_logical(me, 1), vec, 0.0), axis=0, keepdims=True)
    half = jnp.where(jnp.bitwise_and(me, 1) == 0, half[:, 0:64], half[:, 64:128])
    upb[...] = half.reshape(64)


def per_device(tokens, episode_length, window_start, *rest):
    params, cotangent = rest[:13], rest[13]
    D = tokens.shape[2]
    grp, wide = lax.axis_size("grp"), lax.axis_size("wide")
    axes = ("grp", "wide")

    def across(core_slots, keep_own=False):
        pairs = []
        for g in range(grp):
            s = core_slots[g % 2]
            if s or keep_own:
                pairs += [(g * wide + i, g * wide + (i ^ s)) for i in range(wide)]
        return pairs

    swap = [(g * wide + i, (g ^ 1) * wide + i) for g in range(grp) for i in range(wide)]
    count = tokens.shape[0]
    piece, valid = pl.pallas_call(
        functools.partial(pack_kernel, span=tokens.shape[1]), in_specs=[HBM] * 15, out_specs=[VMEM] * 2,
        out_shape=[jax.ShapeDtypeStruct((PIECE_ROWS, D), bf16), jax.ShapeDtypeStruct((count, D), jnp.int32)],
        compiler_params=ALONE, name="pack",
        cost_estimate=pl.CostEstimate(flops=0, bytes_accessed=40 << 20, transcendentals=0),
        scratch_shapes=[pltpu.VMEM(p.shape, bf16) for p in params] + [pltpu.SMEM((count,), jnp.int32)] * 2
        + [pltpu.SemaphoreType.DMA((15,))],
    )(*params, episode_length, window_start)
    hops = [across((SLOTS[0][k], SLOTS[1][k]), True) for k in range(4)]
    direct = [lax.ppermute(piece, axes, hops[k]) for k in range(4)]
    *ready, ct_here = prepare_tokens(tokens, cotangent)
    joined, ready, ct_here = lax.optimization_barrier((jnp.concatenate(direct, 0), ready, ct_here))
    others = lax.ppermute(joined, axes, swap)
    ready = [*ready, *prepare_cotangent(valid, ct_here)]
    keep, send, *parts = layer([joined, others], ready)
    got = lax.ppermute(send, axes, swap)
    shape = jax.ShapeDtypeStruct((GRAD_ROWS, D), bf16)
    pairs = pl.pallas_call(
        pair_kernel, in_specs=[VMEM] * 2, out_specs=[VMEM] * 4, out_shape=[shape] * 4, compiler_params=SMALL, name="pair",
    )(keep, got)
    pairs, parts = lax.optimization_barrier((pairs, parts))
    layer_out, tokens_grad = results(parts, ready)
    back = [across((BACK[0][k], BACK[1][k])) for k in range(4)]
    came = [lax.ppermute(pairs[k], axes, back[k]) for k in range(4)]
    merged = pl.pallas_call(
        merge_kernel, in_specs=[VMEM] * 5, out_specs=VMEM, out_shape=shape, compiler_params=SMALL, name="merge",
    )(pairs[0], *came)
    beside = lax.ppermute(merged, axes, swap)
    chip = pl.pallas_call(
        chip_kernel, in_specs=[VMEM] * 2, out_specs=VMEM, out_shape=shape, compiler_params=SMALL, name="chip",
    )(merged, beside)
    over = [(g * wide + i, (g ^ 2) * wide + i) for g in range(grp) for i in range(wide)]
    every = [chip, lax.ppermute(chip, axes, over)]
    grads = pl.pallas_call(
        finish_kernel, in_specs=[VMEM] * 2, out_specs=[VMEM] * 13,
        out_shape=[jax.ShapeDtypeStruct(p.shape, f32) for p in params], compiler_params=SMALL, name="finish",
    )(*every)
    return (layer_out, tokens_grad, *grads)


def gathered(tokens, episode_length, window_start, *rest):
    params, cotangent = rest[:13], rest[13]
    D = tokens.shape[2]
    full = [lax.all_gather(p, "wide", axis=0, tiled=True) for p in params]
    gain_a, shift_a, qkv, query, value, outw, outb, gain_m, shift_m, upw, upb, downw, downb = full
    FF = upw.shape[1]
    lanes = jnp.arange(D) // (D // PIECES)
    spots = (lanes[None, :] == jnp.arange(PIECES)[:, None]).astype(bf16)
    vectors = jnp.stack([gain_a, shift_a, query, value, outb, gain_m, shift_m, downb])[None] * spots[:, None, :]
    where_up = (jnp.arange(FF) // (FF // PIECES))[None, :] == jnp.arange(PIECES)[:, None]
    ups = (upb[None] * where_up.astype(bf16)).reshape(PIECES, FF // D, D)

    def blocks(weight):
        cut = weight.reshape(PIECES, weight.shape[0] // PIECES, weight.shape[1] // D, D)
        return cut.transpose(0, 2, 1, 3).reshape(PIECES, -1, D)

    slots = jnp.concatenate(
        [blocks(qkv), blocks(outw), blocks(upw), blocks(downw), vectors, ups, jnp.zeros((PIECES, 4, D), bf16)], 1
    )
    mine, others = [jnp.concatenate([slots[s] for s in half], 0) for half in SLOTS]
    count, span = tokens.shape[:2]
    valid = jnp.broadcast_to(jnp.clip(episode_length - window_start, 1, span)[:, None], (count, D))
    *ready, ct_here = prepare_tokens(tokens, cotangent)
    ready = [*ready, *prepare_cotangent(valid, ct_here)]
    keep, send, *parts = layer([mine, others], ready, spread_out=False)
    layer_out, tokens_grad = results(parts, ready)
    order = [0] * PIECES
    for half in (0, 1):
        for k in range(4):
            order[BACK[half][k]] = 4 * half + k
    pieces = jnp.concatenate([keep, send], 0)[jnp.array(order)].astype(f32)
    vec = pieces[0, 192:208] + pieces[0, 208:224]

    def rebuilt(first, last, weight):
        cut = pieces[:, first:last].reshape(PIECES, weight.shape[1] // D, weight.shape[0] // PIECES, D)
        return cut.transpose(0, 2, 1, 3).reshape(weight.shape)

    grads = (
        vec[0], vec[1], rebuilt(0, 48, qkv), vec[2], vec[3], rebuilt(48, 64, outw), vec[4], vec[5], vec[6],
        rebuilt(64, 128, upw), vec[8:12].reshape(FF), rebuilt(128, 192, downw), vec[7],
    )
    grads = [lax.psum_scatter(g, "wide", scatter_dimension=0, tiled=True) for g in grads]
    return (layer_out, tokens_grad, *lax.psum(grads, "grp"))


def solution(mesh):
    rows = P(("grp", "wide"), None, None)
    flat = P(("grp", "wide"))
    one, two = P("wide"), P("wide", None)
    params = (one, one, two, one, one, two, one, one, one, two, one, two, one)
    fits = mesh.shape["wide"] == PIECES and mesh.shape["grp"] == 4
    return jax.shard_map(
        per_device if fits else gathered, mesh=mesh, in_specs=(rows, flat, flat, *params, rows), out_specs=(rows, rows, *params), check_vma=False
    )
```

```python
import math
import functools

import jax
import jax.numpy as jnp
from jax import lax
from jax.experimental import pallas as pl
from jax.experimental.pallas import tpu as pltpu
from jax.sharding import PartitionSpec as P

HEADS = 4
EPS = 1e-05
CUBIC = 0.044715
TANH_SCALE = math.sqrt(2.0 / math.pi)
NEG_FILL = -1e30
LOG2E = math.log2(math.e)
f32, bf16 = jnp.float32, jnp.bfloat16
PIECES = 8
PIECE_ROWS = 208
GRAD_ROWS = 224
SLOTS = ((0, 4, 5, 6), (1, 2, 3, 7))
BACK = ((0, 6, 5, 4), (1, 7, 3, 2))

TILES = ((1, (0, 1)), (1, (2, 3)), (0, (0, 2)), (0, (1, 3)))
EARLY = (0, 2, 1, 3)


def place():
    return lax.axis_index("wide").astype(jnp.int32), jnp.bitwise_and(lax.axis_index("grp").astype(jnp.int32), 1)


def slot_of(core, k, table=SLOTS):
    return jnp.where(core == 0, table[0][k], table[1][k])


def nn(a, b):
    return lax.dot_general(a, b, (((1,), (0,)), ((), ())), preferred_element_type=f32)

def nt(a, b):
    return lax.dot_general(a, b, (((1,), (1,)), ((), ())), preferred_element_type=f32)

def norm(v):
    d = v.shape[0]
    off = v - jnp.sum(v, axis=0, keepdims=True) * (1.0 / d)
    r = lax.rsqrt(jnp.sum(off * off, axis=0, keepdims=True) * (1.0 / d) + EPS)
    return off * r, r

def norm_back(dy, gain, n, r):
    d = dy.shape[0]
    g = dy * gain
    mg = jnp.sum(g, axis=0, keepdims=True) * (1.0 / d)
    mgn = jnp.sum(g * n, axis=0, keepdims=True) * (1.0 / d)
    return r * (g - mg - n * mgn)

def tokens_kernel(x_in, ct_in, x_ref, n_ref, r_ref, ct_ref):
    count, T, D = x_in.shape
    for w in range(count):
        xT = x_in[w].astype(f32).T
        n, r = norm(xT)
        x_ref[w] = xT
        n_ref[w] = n
        r_ref[w] = jnp.broadcast_to(r, (8, T))
        ct_ref[w] = ct_in[w]


def cotangent_kernel(valid_ref, ct_in, up_ref, mask_ref):
    count, T, D = ct_in.shape
    H = T // 2
    for w in range(count):
        valid = valid_ref[w:w + 1, :]
        live = (lax.broadcasted_iota(jnp.int32, (1, T), 1) < jnp.concatenate([valid, valid], 1)).astype(f32)
        up_ref[w] = ct_in[w].astype(f32).T * live
        j = lax.broadcasted_iota(jnp.int32, (H, H), 0)
        tri = j <= lax.broadcasted_iota(jnp.int32, (H, H), 1)
        for k, seen in enumerate((tri & (j < valid), j < valid, tri & (j + H < valid))):
            mask_ref[w, H * k:H * k + H] = jnp.where(seen, 0.0, NEG_FILL).astype(bf16)


def layer_kernel(mine, others, x_ref, n_ref, r_ref, up_ref, mask_ref,
                 keep_ref, send_ref, act_ref, mid_ref, midg_ref, dn_ref, wdT, gain_ref, bias_ref,
                 wqkv, wqkvT, wo, woT, wup, wupT, wd, cols,
                 aqkv, ao, aup, ad, alng, turn, t0, t1, t2, t3, *, batches, spread_out):
    me, core = place() if spread_out else (jnp.int32(0), jnp.int32(0))
    D, T = x_ref.shape[1], x_ref.shape[2]
    H = T // 2
    E = D // HEADS
    FF = wup.shape[1]
    scale = E ** -0.5

    def start():
        vec = jnp.zeros((16, D), f32)
        places = [(slot_of(half, k), ref, PIECE_ROWS * k) for half, ref in ((core, mine), (1 - core, others)) for k in range(PIECES // 2)]
        for slot, ref, at in places:
            o = jnp.bitwise_xor(me, slot)
            r16 = pl.ds(pl.multiple_of(o * 16, 16), 16)
            get = lambda first, last: ref[at + first:at + last, :]
            for b in range(3):
                wqkv[r16, D * b:D * b + D] = get(16 * b, 16 * b + 16)
            wo[r16, :] = get(48, 64)
            for b in range(4):
                wup[r16, D * b:D * b + D] = get(64 + 16 * b, 80 + 16 * b)
            wd[pl.ds(pl.multiple_of(o * 64, 64), 64), :] = get(128, 192)
            vec = vec + get(192, 208).astype(f32)
        vecT = jnp.concatenate([vec, jnp.zeros((D - 16, D), f32)], 0).T
        lane = lax.broadcasted_iota(jnp.int32, (D, 16), 1)
        def col(k):
            return jnp.where(lane == k, vecT[:, 0:16], 0.0).astype(bf16)
        def full(k):
            return jnp.broadcast_to(vecT[:, k:k + 1], (D, T))
        for b in range(3):
            wqkvT[D * b:D * b + D, 0:D] = wqkv[:, D * b:D * b + D].T
        wqkvT[0:D, D:D + 16] = col(2)
        wqkvT[D:2 * D, D:D + 16] = jnp.zeros((D, 16), bf16)
        wqkvT[2 * D:3 * D, D:D + 16] = col(3)
        woT[:, 0:D] = wo[...].T
        woT[:, D:D + 16] = col(4)
        for b in range(4):
            wupT[D * b:D * b + D, 0:D] = wup[:, D * b:D * b + D].T
            wupT[D * b:D * b + D, D:D + 16] = col(8 + b)
            wdT[:, D * b:D * b + D] = wd[D * b:D * b + D, :].T
        bias_ref[...] = jnp.broadcast_to(vec[7:8, :], (8, D))
        gain_ref[...] = full(0)
        cols[0] = full(0)
        cols[1] = full(1)
        cols[2] = full(5)
        cols[3] = full(6)
        for ref in (aqkv, ao, aup, ad, alng):
            ref[...] = jnp.zeros(ref.shape, f32)

    start()
    ones = jnp.ones((16, T), bf16)
    eye2 = (lax.broadcasted_iota(jnp.int32, (H, T), 0) == jnp.bitwise_and(lax.broadcasted_iota(jnp.int32, (H, T), 1), H - 1)).astype(f32).astype(bf16)

    def spread(m, h):
        parts = []
        if h > 0:
            parts.append(jnp.zeros((E * h, m.shape[1]), bf16))
        parts.append(m)
        if h < HEADS - 1:
            parts.append(jnp.zeros((E * (HEADS - 1 - h), m.shape[1]), bf16))
        return jnp.concatenate(parts, 0)

    none = jnp.zeros((16, H), bf16)
    blank = jnp.zeros((E, H), bf16)

    def beside(m, g, first, put):
        part = m[E * g:E * g + E, H * first:H * first + H]
        return jnp.concatenate([part, blank] if put == 0 else [blank, part], 1)

    def stack_keys(m):
        return jnp.concatenate([beside(m, g, 0, g % 2) for g in EARLY], 0)

    def stack_early(m):
        return jnp.concatenate([beside(m, g, 0, g // 2) for g in EARLY], 0)

    def stack_late(m, p):
        return jnp.concatenate([beside(m, 2 * p, 1, 0), beside(m, 2 * p + 1, 1, 1)], 0)

    def window(w):
        idx = w
        n1, r1 = n_ref[idx], r_ref[idx, 0:1]
        a1 = (n1 * cols[0] + cols[1]).astype(bf16)
        a1g = jnp.concatenate([a1, ones], 0)
        yield
        qT = nn(wqkvT[0:D, :], a1g).astype(bf16)
        kT = nn(wqkvT[D:2 * D, :], a1g).astype(bf16)
        vT = nn(wqkvT[2 * D:3 * D, :], a1g).astype(bf16)
        yield
        krow, vrow = kT.T, vT.T
        left = (jnp.concatenate([krow[0:H], mask_ref[idx, 0:H]], 1), jnp.concatenate([krow, mask_ref[idx, H:H + T]], 1))
        vrow1 = jnp.concatenate([vrow, jnp.ones((T, 16), bf16)], 1)
        yield
        exps = []
        for k, pair in TILES:
            cut = slice(H * k, H * k + H)
            right = jnp.concatenate([spread(qT[E * g:E * g + E, cut], g) for g in pair], 1)
            S = nn(left[k], jnp.concatenate([right, eye2], 0))
            exps.append(jnp.exp2((S - jnp.max(S, axis=0, keepdims=True)) * (scale * LOG2E)))
            yield
        lows = [exps[0].astype(bf16), exps[1].astype(bf16), jnp.concatenate([exps[2].astype(bf16), exps[3].astype(bf16)], 0)]
        tops = [nn(jnp.concatenate([vT[E * 2 * p:E * 2 * p + 2 * E], ones], 0), lows[p]) for p in (0, 1)]
        yield
        early = nn(jnp.concatenate([stack_keys(vT), jnp.concatenate([ones[:, 0:H], none], 1), jnp.concatenate([none, ones[:, 0:H]], 1)], 0), lows[2])
        att, invs = [], []
        for g in range(HEADS):
            top, low = tops[g // 2], early[4 * E + 16 * (g % 2):4 * E + 16 * (g % 2) + 1]
            cut, at = slice(H * (g % 2), H * (g % 2) + H), slice(H * (g // 2), H * (g // 2) + H)
            inv = 1.0 / jnp.concatenate([low[:, at], top[2 * E:2 * E + 1, cut]], 1)
            invs.append(inv)
            row = E * EARLY.index(g)
            att.append(jnp.concatenate([early[row:row + E, at], top[E * (g % 2):E * (g % 2) + E, cut]], 1) * inv)
        yield
        attT = jnp.concatenate(att, 0)
        attg = jnp.concatenate([attT.astype(bf16), ones], 0)
        mid = x_ref[idx] + nn(woT[...], attg)
        yield
        n2, r2 = norm(mid)
        a2 = (n2 * cols[2] + cols[3]).astype(bf16)
        a2g = jnp.concatenate([a2, ones], 0)
        upT = up_ref[idx]
        upb = upT.astype(bf16)
        yield
        acts, hgs = [], []
        for b in range(FF // D):
            blk = slice(D * b, D * b + D)
            hid = nn(wupT[blk, :], a2g)
            v2 = hid * hid
            s = 0.5 * jnp.tanh(hid * (TANH_SCALE + (TANH_SCALE * CUBIC) * v2)) + 0.5
            act = hid * s
            acts.append(act.astype(bf16))
            gp = s + act * (1.0 - s) * (2 * TANH_SCALE + (6 * TANH_SCALE * CUBIC) * v2)
            hgs.append((nn(wd[blk, :], upb) * gp).astype(bf16))
            yield
        actg = jnp.concatenate(acts + [ones], 0)
        hg = jnp.concatenate(hgs, 0)
        act_ref[w] = actg[0:FF]
        mid_ref[w] = mid
        yield
        yield (3, actg, upb)
        dn2 = nn(wup[...], hg)
        yield (2, a2g, hg)
        alng[0] += dn2 * n2
        midg = upT + norm_back(dn2, cols[2], n2, r2)
        midg_ref[w] = midg
        bg = midg.astype(bf16)
        yield
        yield (1, attg, bg)
        daT = nn(wo[...], bg)
        yield
        dq, dk, dv = [], [], []
        das, rows = [], []
        for h in range(HEADS):
            blk = slice(E * h, E * h + E)
            da = (daT[blk] * invs[h]).astype(bf16)
            inner = -jnp.sum(da.astype(f32) * att[h], axis=0, keepdims=True)
            hi = inner.astype(bf16).astype(f32)
            mi = (inner - hi).astype(bf16).astype(f32)
            lo = inner - hi - mi
            das.append(da)
            rows.append(jnp.concatenate([hi, mi, lo, jnp.zeros((13, T), f32)], 0).astype(bf16))
        yield
        daT2 = jnp.concatenate(das, 0)
        tiles = []
        for (k, pair), e in zip(TILES, exps):
            cut = slice(H * k, H * k + H)
            right = jnp.concatenate(
                [jnp.concatenate([spread(das[g][:, cut], g), rows[g][:, cut]], 0) for g in pair], 1)
            dP = nn(vrow1[0:H] if k == 0 else vrow1, right)
            tiles.append((e * dP).astype(bf16))
            yield
        tiles = [tiles[0], tiles[1], jnp.concatenate([tiles[2], tiles[3]], 0)]

        def by_query(m, tiles):
            tops = [nn(m[2 * E * p:2 * E * p + 2 * E], tiles[p]) for p in (0, 1)]
            low = nn(stack_keys(m), tiles[2])
            out = []
            for g in range(HEADS):
                at, cut, row = slice(H * (g // 2), H * (g // 2) + H), slice(H * (g % 2), H * (g % 2) + H), E * EARLY.index(g)
                out.append(jnp.concatenate([low[row:row + E, at], tops[g // 2][E * (g % 2):E * (g % 2) + E, cut]], 1))
            return out

        def by_key(m, tiles, which):
            for p in range(3):
                turn[w, 3 * which + p] = tiles[p].T
            tops = [nn(stack_late(m, p), turn[w, 3 * which + p]) for p in (0, 1)]
            low = nn(stack_early(m), turn[w, 3 * which + 2])
            out = []
            for g in range(HEADS):
                at, row = slice(H * (g % 2), H * (g % 2) + H), E * EARLY.index(g)
                top = tops[g // 2][E * (g % 2):E * (g % 2) + E]
                out.append(jnp.concatenate([top[:, 0:H] + low[row:row + E, at], top[:, H:T]], 1))
            return out

        dq = [v * scale for v in by_query(kT, tiles)]
        yield
        dk = [v * scale for v in by_key(qT, tiles, 0)]
        yield
        dv = by_key(daT2, lows, 1)
        yield
        pg = jnp.concatenate(dq + dk + dv, 0).astype(bf16)
        dn1 = nn(wqkv[...], pg)
        yield (0, a1g, pg)
        alng[1] += dn1 * n1
        dn_ref[w] = dn1

    accs = (aqkv, ao, aup, ad)
    turns = (t0, t1, t2, t3)
    held = [[[] for _ in accs] for _ in batches]
    live_windows, w = [], 0
    for at, (size, begin) in enumerate(batches):
        for _ in range(size):
            live_windows.append((begin, window(w), at))
            w += 1
    tick = 0
    while live_windows:
        still = []
        for begin, gen, batch in live_windows:
            if tick < begin:
                still.append((begin, gen, batch))
                continue
            try:
                item = next(gen)
            except StopIteration:
                continue
            still.append((begin, gen, batch))
            if item is not None:
                k, left, right = item
                pairs, size = held[batch][k], batches[batch][0]
                turns[k][len(pairs)] = right.T
                pairs.append(left)
                if len(pairs) == size:
                    accs[k][...] += nn(jnp.concatenate(pairs, 1), turns[k][0:size].reshape(size * T, right.shape[0]))
        live_windows = still
        tick += 1

    def end():
        def row(k):
            a = alng[k]
            a = a[:, 0:H] + a[:, H:T]
            return jnp.sum(a.T, axis=0, keepdims=True)

        def shift(sums, weight):
            hi = sums.astype(bf16).astype(f32)
            mi = (sums - hi).astype(bf16).astype(f32)
            parts = jnp.concatenate([hi, mi, sums - hi - mi, jnp.zeros((13, sums.shape[1]), f32)], 0)
            return jnp.sum(nt(parts.astype(bf16), weight), axis=0, keepdims=True)

        vec = jnp.concatenate(
            [row(1), shift(aqkv[D:D + 1, :], wqkv[...]), aqkv[D:D + 1, 0:D], aqkv[D:D + 1, 2 * D:3 * D], ao[D:D + 1, :],
             row(0), shift(aup[D:D + 1, :], wup[...]), ad[FF:FF + 1, :]]
            + [aup[D:D + 1, D * b:D * b + D] for b in range(4)] + [jnp.zeros((4, D), f32)], 0)
        high = vec.astype(bf16)
        low = (vec - high.astype(f32)).astype(bf16)
        for k in range(PIECES // 2):
            for ref, half in ((keep_ref, core), (send_ref, 1 - core)):
                o = jnp.bitwise_xor(me, slot_of(half, k, BACK))
                r16 = pl.ds(pl.multiple_of(o * 16, 16), 16)
                for b in range(3):
                    ref[k, 16 * b:16 * b + 16, :] = aqkv[r16, D * b:D * b + D].astype(bf16)
                ref[k, 48:64, :] = ao[r16, :].astype(bf16)
                for b in range(4):
                    ref[k, 64 + 16 * b:80 + 16 * b, :] = aup[r16, D * b:D * b + D].astype(bf16)
                ref[k, 128:192, :] = ad[pl.ds(pl.multiple_of(o * 64, 64), 64), :].astype(bf16)
                ref[k, 192:208, :] = high
                ref[k, 208:224, :] = low

    end()

def prepare_tokens(x, ct):
    count, T, D = x.shape
    vmem = pl.BlockSpec(memory_space=pltpu.VMEM)
    turned = jax.ShapeDtypeStruct((count, D, T), f32)
    return pl.pallas_call(
        tokens_kernel,
        in_specs=[vmem] * 2,
        out_specs=[vmem] * 4,
        out_shape=[turned, turned, jax.ShapeDtypeStruct((count, 8, T), f32), jax.ShapeDtypeStruct(ct.shape, bf16)],
        compiler_params=pltpu.CompilerParams(vmem_limit_bytes=16 << 20),
        cost_estimate=pl.CostEstimate(flops=0, bytes_accessed=count * T * D * 40, transcendentals=0),
        name="prepare_tokens",
    )(x, ct)


def prepare_cotangent(valid, ct):
    count, T, D = ct.shape
    vmem = pl.BlockSpec(memory_space=pltpu.VMEM)
    return pl.pallas_call(
        cotangent_kernel,
        in_specs=[vmem] * 2,
        out_specs=[vmem] * 2,
        out_shape=[jax.ShapeDtypeStruct((count, D, T), f32), jax.ShapeDtypeStruct((count, T + T // 2, T // 2), bf16)],
        compiler_params=pltpu.CompilerParams(vmem_limit_bytes=16 << 20),
        cost_estimate=pl.CostEstimate(flops=0, bytes_accessed=count * T * D * 20, transcendentals=0),
        name="prepare_cotangent",
    )(valid, ct)


def results_kernel(act_ref, mid_ref, midg_ref, dn_ref, wdT, gain_ref, bias_ref, n_ref, r_ref, lo_ref, tg_ref, lo_buf, tg_buf, sems):
    copies = []
    for w in range(act_ref.shape[0]):
        lo_buf[w] = (mid_ref[w] + nn(wdT[...], act_ref[w])).T + bias_ref[0:1, :]
        tg_buf[w] = (midg_ref[w] + norm_back(dn_ref[w], gain_ref[...], n_ref[w], r_ref[w, 0:1])).T
        for k, (buf, ref) in enumerate(((lo_buf, lo_ref), (tg_buf, tg_ref))):
            copies.append(pltpu.make_async_copy(buf.at[w], ref.at[w], sems.at[k, w]))
            copies[-1].start()
    for copy in copies:
        copy.wait()


def layer(slots, ready, batches=None, spread_out=True):
    count, D, T = ready[0].shape
    FF = 512
    batches = batches or ((count // 2, 0), (count - count // 2, 13))
    group = max(size for size, _ in batches)
    vm = lambda s, d: pltpu.VMEM(s, d)
    vmem = pl.BlockSpec(memory_space=pltpu.VMEM)
    half = jax.ShapeDtypeStruct((PIECES // 2, GRAD_ROWS, D), bf16)
    turned = jax.ShapeDtypeStruct((count, D, T), f32)
    return pl.pallas_call(
        functools.partial(layer_kernel, batches=batches, spread_out=spread_out),
        in_specs=[vmem] * 7,
        out_specs=[vmem] * 9,
        out_shape=[half, half, jax.ShapeDtypeStruct((count, FF, T), bf16), turned, turned, turned,
                   jax.ShapeDtypeStruct((D, FF), bf16), jax.ShapeDtypeStruct((D, T), f32), jax.ShapeDtypeStruct((8, D), f32)],
        scratch_shapes=[
            vm((D, 3 * D), bf16), vm((3 * D, D + 16), bf16), vm((D, D), bf16), vm((D, D + 16), bf16),
            vm((D, FF), bf16), vm((FF, D + 16), bf16), vm((FF, D), bf16),
            vm((4, D, T), f32),
            vm((D + 16, 3 * D), f32), vm((D + 16, D), f32), vm((D + 16, FF), f32), vm((FF + 16, D), f32),
            vm((2, D, T), f32), vm((count, 6, T, T), bf16),
            vm((group, T, 3 * D), bf16), vm((group, T, D), bf16), vm((group, T, FF), bf16), vm((group, T, D), bf16)],
        compiler_params=pltpu.CompilerParams(vmem_limit_bytes=32 << 20),
        name="layer",
    )(*slots, *ready)


def results(parts, ready):
    n, r = ready[1:3]
    count, D, T = n.shape
    vmem = pl.BlockSpec(memory_space=pltpu.VMEM)
    rows = jax.ShapeDtypeStruct((count, T, D), f32)
    return pl.pallas_call(
        results_kernel,
        in_specs=[vmem] * 9,
        out_specs=[pl.BlockSpec(memory_space=pl.ANY)] * 2,
        out_shape=[rows] * 2,
        scratch_shapes=[pltpu.VMEM((count, T, D), f32)] * 2 + [pltpu.SemaphoreType.DMA((2, count))],
        compiler_params=pltpu.CompilerParams(vmem_limit_bytes=16 << 20),
        cost_estimate=pl.CostEstimate(flops=2 * count * T * D * 512, bytes_accessed=count * T * D * 40, transcendentals=0),
        name="results",
    )(*parts, n, r)


VMEM = pl.BlockSpec(memory_space=pltpu.VMEM)
SMEM = pl.BlockSpec(memory_space=pltpu.SMEM)
HBM = pl.BlockSpec(memory_space=pltpu.HBM)
SMALL = pltpu.CompilerParams(vmem_limit_bytes=16 << 20)
ALONE = pltpu.CompilerParams(vmem_limit_bytes=60 << 20)


def pack_kernel(*refs, span):
    hbm, out_ref, valid_ref, held, sems = refs[:15], refs[15], refs[16], refs[17:32], refs[32]
    copies = [pltpu.make_async_copy(src, dst, sems.at[k]) for k, (src, dst) in enumerate(zip(hbm, held))]
    for copy in copies:
        copy.start()
    gain_a, shift_a, qkv, query, value, outw, outb, gain_m, shift_m, upw, upb, downw, downb, lens, starts = held
    me, core = place()
    D = out_ref.shape[1]
    row = lax.broadcasted_iota(jnp.int32, (16, D), 0)
    lane16 = lax.broadcasted_iota(jnp.int32, (16, D), 1)
    spot16 = (lane16 == row + 16 * me).astype(bf16)
    r64 = lax.broadcasted_iota(jnp.int32, (64, D), 0)
    l64 = lax.broadcasted_iota(jnp.int32, (64, D), 1)
    spot64 = (l64 == r64 + 64 * jnp.bitwise_and(me, 1)).astype(bf16)
    for copy in copies:
        copy.wait()
    for b in range(3):
        out_ref[16 * b:16 * b + 16, :] = qkv[:, D * b:D * b + D]
    out_ref[48:64, :] = outw[...]
    for b in range(4):
        out_ref[64 + 16 * b:80 + 16 * b, :] = upw[:, D * b:D * b + D]
    out_ref[128:192, :] = downw[...]
    total = jnp.zeros((16, D), f32)
    for k, ref in enumerate((gain_a, shift_a, query, value, outb, gain_m, shift_m, downb)):
        v = jnp.broadcast_to(ref[...].astype(f32).reshape(1, 16), (16, 16)).astype(bf16)
        total = total + jnp.where(row == k, nn(v, spot16), 0.0)
    v = jnp.broadcast_to(upb[...].astype(f32).reshape(1, 64), (16, 64)).astype(bf16)
    total = total + jnp.where(row == 8 + lax.shift_right_logical(me, 1), nn(v, spot64), 0.0)
    out_ref[192:208, :] = total.astype(bf16)
    for w in range(valid_ref.shape[0]):
        valid_ref[w:w + 1, :] = jnp.full((1, D), jnp.clip(lens[w] - starts[w], 1, span), jnp.int32)


def split_add(parts):
    total = parts[0].astype(f32)
    for p in parts[1:]:
        total = total + p.astype(f32)
    vec = total[192:208] + total[208:224]
    high = vec.astype(bf16)
    low = (vec - high.astype(f32)).astype(bf16)
    return total[0:192], vec, high, low


def pair_kernel(keep_ref, got_ref, *out_refs):
    for k, ref in enumerate(out_refs):
        main, vec, high, low = split_add([keep_ref[k], got_ref[k]])
        ref[0:192, :] = main.astype(bf16)
        ref[192:208, :] = high
        ref[208:224, :] = low


def merge_kernel(own_ref, r0, r1, r2, r3, out_ref):
    first = jnp.where(place()[1] == 0, own_ref[...].astype(f32), r0[...].astype(f32))
    main, vec, high, low = split_add([first, r1[...], r2[...], r3[...]])
    out_ref[0:192, :] = main.astype(bf16)
    out_ref[192:208, :] = high
    out_ref[208:224, :] = low


def chip_kernel(own_ref, got_ref, out_ref):
    main, vec, high, low = split_add([own_ref[...], got_ref[...]])
    out_ref[0:192, :] = main.astype(bf16)
    out_ref[192:208, :] = high
    out_ref[208:224, :] = low


def finish_kernel(m0, m1, gain_a, shift_a, qkv, query, value, outw, outb, gain_m, shift_m, upw, upb, downw, downb):
    me, core = place()
    D = m0.shape[1]
    main, vec, high, low = split_add([m0[...], m1[...]])
    for b in range(3):
        qkv[:, D * b:D * b + D] = main[16 * b:16 * b + 16]
    outw[...] = main[48:64]
    for b in range(4):
        upw[:, D * b:D * b + D] = main[64 + 16 * b:80 + 16 * b]
    downw[...] = main[128:192]
    turned = pltpu.roll(vec, jnp.bitwise_and(D - 16 * me, D - 1), 1)
    for k, ref in enumerate((gain_a, shift_a, query, value, outb, gain_m, shift_m, downb)):
        ref[...] = turned[k:k + 1, 0:16].reshape(16)
    row = lax.broadcasted_iota(jnp.int32, (16, D), 0)
    half = jnp.sum(jnp.where(row == 8 + lax.shift_right_logical(me, 1), vec, 0.0), axis=0, keepdims=True)
    half = jnp.where(jnp.bitwise_and(me, 1) == 0, half[:, 0:64], half[:, 64:128])
    upb[...] = half.reshape(64)


def per_device(tokens, episode_length, window_start, *rest):
    params, cotangent = rest[:13], rest[13]
    D = tokens.shape[2]
    grp, wide = lax.axis_size("grp"), lax.axis_size("wide")
    axes = ("grp", "wide")

    def across(core_slots, keep_own=False):
        pairs = []
        for g in range(grp):
            s = core_slots[g % 2]
            if s or keep_own:
                pairs += [(g * wide + i, g * wide + (i ^ s)) for i in range(wide)]
        return pairs

    swap = [(g * wide + i, (g ^ 1) * wide + i) for g in range(grp) for i in range(wide)]
    count = tokens.shape[0]
    piece, valid = pl.pallas_call(
        functools.partial(pack_kernel, span=tokens.shape[1]), in_specs=[HBM] * 15, out_specs=[VMEM] * 2,
        out_shape=[jax.ShapeDtypeStruct((PIECE_ROWS, D), bf16), jax.ShapeDtypeStruct((count, D), jnp.int32)],
        compiler_params=ALONE, name="pack",
        cost_estimate=pl.CostEstimate(flops=0, bytes_accessed=40 << 20, transcendentals=0),
        scratch_shapes=[pltpu.VMEM(p.shape, bf16) for p in params] + [pltpu.SMEM((count,), jnp.int32)] * 2
        + [pltpu.SemaphoreType.DMA((15,))],
    )(*params, episode_length, window_start)
    hops = [across((SLOTS[0][k], SLOTS[1][k]), True) for k in range(4)]
    direct = [lax.ppermute(piece, axes, hops[k]) for k in range(4)]
    *ready, ct_here = prepare_tokens(tokens, cotangent)
    joined, ready, ct_here = lax.optimization_barrier((jnp.concatenate(direct, 0), ready, ct_here))
    others = lax.ppermute(joined, axes, swap)
    ready = [*ready, *prepare_cotangent(valid, ct_here)]
    keep, send, *parts = layer([joined, others], ready)
    got = lax.ppermute(send, axes, swap)
    shape = jax.ShapeDtypeStruct((GRAD_ROWS, D), bf16)
    pairs = pl.pallas_call(
        pair_kernel, in_specs=[VMEM] * 2, out_specs=[VMEM] * 4, out_shape=[shape] * 4, compiler_params=SMALL, name="pair",
    )(keep, got)
    pairs, parts = lax.optimization_barrier((pairs, parts))
    layer_out, tokens_grad = results(parts, ready)
    back = [across((BACK[0][k], BACK[1][k])) for k in range(4)]
    came = [lax.ppermute(pairs[k], axes, back[k]) for k in range(4)]
    merged = pl.pallas_call(
        merge_kernel, in_specs=[VMEM] * 5, out_specs=VMEM, out_shape=shape, compiler_params=SMALL, name="merge",
    )(pairs[0], *came)
    beside = lax.ppermute(merged, axes, swap)
    chip = pl.pallas_call(
        chip_kernel, in_specs=[VMEM] * 2, out_specs=VMEM, out_shape=shape, compiler_params=SMALL, name="chip",
    )(merged, beside)
    over = [(g * wide + i, (g ^ 2) * wide + i) for g in range(grp) for i in range(wide)]
    every = [chip, lax.ppermute(chip, axes, over)]
    grads = pl.pallas_call(
        finish_kernel, in_specs=[VMEM] * 2, out_specs=[VMEM] * 13,
        out_shape=[jax.ShapeDtypeStruct(p.shape, f32) for p in params], compiler_params=SMALL, name="finish",
    )(*every)
    return (layer_out, tokens_grad, *grads)


def gathered(tokens, episode_length, window_start, *rest):
    params, cotangent = rest[:13], rest[13]
    D = tokens.shape[2]
    full = [lax.all_gather(p, "wide", axis=0, tiled=True) for p in params]
    gain_a, shift_a, qkv, query, value, outw, outb, gain_m, shift_m, upw, upb, downw, downb = full
    FF = upw.shape[1]
    lanes = jnp.arange(D) // (D // PIECES)
    spots = (lanes[None, :] == jnp.arange(PIECES)[:, None]).astype(bf16)
    vectors = jnp.stack([gain_a, shift_a, query, value, outb, gain_m, shift_m, downb])[None] * spots[:, None, :]
    where_up = (jnp.arange(FF) // (FF // PIECES))[None, :] == jnp.arange(PIECES)[:, None]
    ups = (upb[None] * where_up.astype(bf16)).reshape(PIECES, FF // D, D)

    def blocks(weight):
        cut = weight.reshape(PIECES, weight.shape[0] // PIECES, weight.shape[1] // D, D)
        return cut.transpose(0, 2, 1, 3).reshape(PIECES, -1, D)

    slots = jnp.concatenate(
        [blocks(qkv), blocks(outw), blocks(upw), blocks(downw), vectors, ups, jnp.zeros((PIECES, 4, D), bf16)], 1
    )
    mine, others = [jnp.concatenate([slots[s] for s in half], 0) for half in SLOTS]
    count, span = tokens.shape[:2]
    valid = jnp.broadcast_to(jnp.clip(episode_length - window_start, 1, span)[:, None], (count, D))
    *ready, ct_here = prepare_tokens(tokens, cotangent)
    ready = [*ready, *prepare_cotangent(valid, ct_here)]
    keep, send, *parts = layer([mine, others], ready, spread_out=False)
    layer_out, tokens_grad = results(parts, ready)
    order = [0] * PIECES
    for half in (0, 1):
        for k in range(4):
            order[BACK[half][k]] = 4 * half + k
    pieces = jnp.concatenate([keep, send], 0)[jnp.array(order)].astype(f32)
    vec = pieces[0, 192:208] + pieces[0, 208:224]

    def rebuilt(first, last, weight):
        cut = pieces[:, first:last].reshape(PIECES, weight.shape[1] // D, weight.shape[0] // PIECES, D)
        return cut.transpose(0, 2, 1, 3).reshape(weight.shape)

    grads = (
        vec[0], vec[1], rebuilt(0, 48, qkv), vec[2], vec[3], rebuilt(48, 64, outw), vec[4], vec[5], vec[6],
        rebuilt(64, 128, upw), vec[8:12].reshape(FF), rebuilt(128, 192, downw), vec[7],
    )
    grads = [lax.psum_scatter(g, "wide", scatter_dimension=0, tiled=True) for g in grads]
    return (layer_out, tokens_grad, *lax.psum(grads, "grp"))


def solution(mesh):
    rows = P(("grp", "wide"), None, None)
    flat = P(("grp", "wide"))
    one, two = P("wide"), P("wide", None)
    params = (one, one, two, one, one, two, one, one, one, two, one, two, one)
    fits = mesh.shape["wide"] == PIECES and mesh.shape["grp"] == 4
    return jax.shard_map(
        per_device if fits else gathered, mesh=mesh, in_specs=(rows, flat, flat, *params, rows), out_specs=(rows, rows, *params), check_vma=False
    )
```

```python
import math
import functools

import jax
import jax.numpy as jnp
from jax import lax
from jax.experimental import pallas as pl
from jax.experimental.pallas import tpu as pltpu
from jax.sharding import PartitionSpec as P

HEADS = 4
EPS = 1e-05
CUBIC = 0.044715
TANH_SCALE = math.sqrt(2.0 / math.pi)
NEG_FILL = -1e30
LOG2E = math.log2(math.e)
f32, bf16 = jnp.float32, jnp.bfloat16
PIECES = 8
PIECE_ROWS = 208
GRAD_ROWS = 208
SLOTS = ((0, 4, 5, 6), (1, 2, 3, 7))
BACK = ((0, 6, 5, 4), (1, 7, 3, 2))

TILES = ((1, (0, 1)), (1, (2, 3)), (0, (0, 2)), (0, (1, 3)))
EARLY = (0, 2, 1, 3)


def place():
    return lax.axis_index("wide").astype(jnp.int32), jnp.bitwise_and(lax.axis_index("grp").astype(jnp.int32), 1)


def slot_of(core, k, table=SLOTS):
    return jnp.where(core == 0, table[0][k], table[1][k])


def nn(a, b):
    return lax.dot_general(a, b, (((1,), (0,)), ((), ())), preferred_element_type=f32)

def nt(a, b):
    return lax.dot_general(a, b, (((1,), (1,)), ((), ())), preferred_element_type=f32)

def norm(v):
    d = v.shape[0]
    off = v - jnp.sum(v, axis=0, keepdims=True) * (1.0 / d)
    r = lax.rsqrt(jnp.sum(off * off, axis=0, keepdims=True) * (1.0 / d) + EPS)
    return off * r, r

def norm_back(dy, gain, n, r):
    d = dy.shape[0]
    g = dy * gain
    mg = jnp.sum(g, axis=0, keepdims=True) * (1.0 / d)
    mgn = jnp.sum(g * n, axis=0, keepdims=True) * (1.0 / d)
    return r * (g - mg - n * mgn)

def tokens_kernel(x_in, ct_in, x_ref, n_ref, r_ref, ct_ref):
    count, T, D = x_in.shape
    for w in range(count):
        xT = x_in[w].astype(f32).T
        n, r = norm(xT)
        x_ref[w] = xT
        n_ref[w] = n
        r_ref[w] = jnp.broadcast_to(r, (8, T))
        ct_ref[w] = ct_in[w]


def cotangent_kernel(valid_ref, ct_in, up_ref, mask_ref):
    count, T, D = ct_in.shape
    H = T // 2
    for w in range(count):
        valid = valid_ref[w:w + 1, :]
        live = (lax.broadcasted_iota(jnp.int32, (1, T), 1) < jnp.concatenate([valid, valid], 1)).astype(f32)
        up_ref[w] = ct_in[w].astype(f32).T * live
        j = lax.broadcasted_iota(jnp.int32, (H, H), 0)
        tri = j <= lax.broadcasted_iota(jnp.int32, (H, H), 1)
        for k, seen in enumerate((tri & (j < valid), j < valid, tri & (j + H < valid))):
            mask_ref[w, H * k:H * k + H] = jnp.where(seen, 0.0, NEG_FILL).astype(bf16)


def layer_kernel(mine, others, x_ref, n_ref, r_ref, up_ref, mask_ref,
                 keep_ref, send_ref, act_ref, mid_ref, midg_ref, dn_ref, wdT, gain_ref, bias_ref,
                 wqkv, wqkvT, wo, woT, wup, wupT, wd, cols,
                 aqkv, ao, aup, ad, alng, turn, t0, t1, t2, t3, *, batches, spread_out):
    me, core = place() if spread_out else (jnp.int32(0), jnp.int32(0))
    D, T = x_ref.shape[1], x_ref.shape[2]
    H = T // 2
    E = D // HEADS
    FF = wup.shape[1]
    scale = E ** -0.5

    def start():
        vec = jnp.zeros((16, D), f32)
        places = [(slot_of(half, k), ref, PIECE_ROWS * k) for half, ref in ((core, mine), (1 - core, others)) for k in range(PIECES // 2)]
        for slot, ref, at in places:
            o = jnp.bitwise_xor(me, slot)
            r16 = pl.ds(pl.multiple_of(o * 16, 16), 16)
            get = lambda first, last: ref[at + first:at + last, :]
            for b in range(3):
                wqkv[r16, D * b:D * b + D] = get(16 * b, 16 * b + 16)
            wo[r16, :] = get(48, 64)
            for b in range(4):
                wup[r16, D * b:D * b + D] = get(64 + 16 * b, 80 + 16 * b)
            wd[pl.ds(pl.multiple_of(o * 64, 64), 64), :] = get(128, 192)
            vec = vec + get(192, 208).astype(f32)
        vecT = jnp.concatenate([vec, jnp.zeros((D - 16, D), f32)], 0).T
        lane = lax.broadcasted_iota(jnp.int32, (D, 16), 1)
        def col(k):
            return jnp.where(lane == k, vecT[:, 0:16], 0.0).astype(bf16)
        def full(k):
            return jnp.broadcast_to(vecT[:, k:k + 1], (D, T))
        for b in range(3):
            wqkvT[D * b:D * b + D, 0:D] = wqkv[:, D * b:D * b + D].T
        wqkvT[0:D, D:D + 16] = col(2)
        wqkvT[D:2 * D, D:D + 16] = jnp.zeros((D, 16), bf16)
        wqkvT[2 * D:3 * D, D:D + 16] = col(3)
        woT[:, 0:D] = wo[...].T
        woT[:, D:D + 16] = col(4)
        for b in range(4):
            wupT[D * b:D * b + D, 0:D] = wup[:, D * b:D * b + D].T
            wupT[D * b:D * b + D, D:D + 16] = col(8 + b)
            wdT[:, D * b:D * b + D] = wd[D * b:D * b + D, :].T
        bias_ref[...] = jnp.broadcast_to(vec[7:8, :], (8, D))
        gain_ref[...] = full(0)
        cols[0] = full(0)
        cols[1] = full(1)
        cols[2] = full(5)
        cols[3] = full(6)
        for ref in (aqkv, ao, aup, ad, alng):
            ref[...] = jnp.zeros(ref.shape, f32)

    start()
    ones = jnp.ones((16, T), bf16)
    eye2 = (lax.broadcasted_iota(jnp.int32, (H, T), 0) == jnp.bitwise_and(lax.broadcasted_iota(jnp.int32, (H, T), 1), H - 1)).astype(f32).astype(bf16)

    def spread(m, h):
        parts = []
        if h > 0:
            parts.append(jnp.zeros((E * h, m.shape[1]), bf16))
        parts.append(m)
        if h < HEADS - 1:
            parts.append(jnp.zeros((E * (HEADS - 1 - h), m.shape[1]), bf16))
        return jnp.concatenate(parts, 0)

    none = jnp.zeros((16, H), bf16)
    blank = jnp.zeros((E, H), bf16)

    def beside(m, g, first, put):
        part = m[E * g:E * g + E, H * first:H * first + H]
        return jnp.concatenate([part, blank] if put == 0 else [blank, part], 1)

    def stack_keys(m):
        return jnp.concatenate([beside(m, g, 0, g % 2) for g in EARLY], 0)

    def stack_early(m):
        return jnp.concatenate([beside(m, g, 0, g // 2) for g in EARLY], 0)

    def stack_late(m, p):
        return jnp.concatenate([beside(m, 2 * p, 1, 0), beside(m, 2 * p + 1, 1, 1)], 0)

    def window(w):
        idx = w
        n1, r1 = n_ref[idx], r_ref[idx, 0:1]
        a1 = (n1 * cols[0] + cols[1]).astype(bf16)
        a1g = jnp.concatenate([a1, ones], 0)
        yield
        qT = nn(wqkvT[0:D, :], a1g).astype(bf16)
        kT = nn(wqkvT[D:2 * D, :], a1g).astype(bf16)
        vT = nn(wqkvT[2 * D:3 * D, :], a1g).astype(bf16)
        yield
        krow, vrow = kT.T, vT.T
        left = (jnp.concatenate([krow[0:H], mask_ref[idx, 0:H]], 1), jnp.concatenate([krow, mask_ref[idx, H:H + T]], 1))
        vrow1 = jnp.concatenate([vrow, jnp.ones((T, 16), bf16)], 1)
        yield
        exps = []
        for k, pair in TILES:
            cut = slice(H * k, H * k + H)
            right = jnp.concatenate([spread(qT[E * g:E * g + E, cut], g) for g in pair], 1)
            S = nn(left[k], jnp.concatenate([right, eye2], 0))
            exps.append(jnp.exp2((S - jnp.max(S, axis=0, keepdims=True)) * (scale * LOG2E)))
            yield
        lows = [exps[0].astype(bf16), exps[1].astype(bf16), jnp.concatenate([exps[2].astype(bf16), exps[3].astype(bf16)], 0)]
        tops = [nn(jnp.concatenate([vT[E * 2 * p:E * 2 * p + 2 * E], ones], 0), lows[p]) for p in (0, 1)]
        yield
        early = nn(jnp.concatenate([stack_keys(vT), jnp.concatenate([ones[:, 0:H], none], 1), jnp.concatenate([none, ones[:, 0:H]], 1)], 0), lows[2])
        att, invs = [], []
        for g in range(HEADS):
            top, low = tops[g // 2], early[4 * E + 16 * (g % 2):4 * E + 16 * (g % 2) + 1]
            cut, at = slice(H * (g % 2), H * (g % 2) + H), slice(H * (g // 2), H * (g // 2) + H)
            inv = 1.0 / jnp.concatenate([low[:, at], top[2 * E:2 * E + 1, cut]], 1)
            invs.append(inv)
            row = E * EARLY.index(g)
            att.append(jnp.concatenate([early[row:row + E, at], top[E * (g % 2):E * (g % 2) + E, cut]], 1) * inv)
        yield
        attT = jnp.concatenate(att, 0)
        attg = jnp.concatenate([attT.astype(bf16), ones], 0)
        mid = x_ref[idx] + nn(woT[...], attg)
        yield
        n2, r2 = norm(mid)
        a2 = (n2 * cols[2] + cols[3]).astype(bf16)
        a2g = jnp.concatenate([a2, ones], 0)
        upT = up_ref[idx]
        upb = upT.astype(bf16)
        yield
        acts, hgs = [], []
        for b in range(FF // D):
            blk = slice(D * b, D * b + D)
            hid = nn(wupT[blk, :], a2g)
            v2 = hid * hid
            s = 0.5 * jnp.tanh(hid * (TANH_SCALE + (TANH_SCALE * CUBIC) * v2)) + 0.5
            act = hid * s
            acts.append(act.astype(bf16))
            gp = s + act * (1.0 - s) * (2 * TANH_SCALE + (6 * TANH_SCALE * CUBIC) * v2)
            hgs.append((nn(wd[blk, :], upb) * gp).astype(bf16))
            yield
        actg = jnp.concatenate(acts + [ones], 0)
        hg = jnp.concatenate(hgs, 0)
        act_ref[w] = actg[0:FF]
        mid_ref[w] = mid
        yield
        yield (3, actg, upb)
        dn2 = nn(wup[...], hg)
        yield (2, a2g, hg)
        alng[0] += dn2 * n2
        midg = upT + norm_back(dn2, cols[2], n2, r2)
        midg_ref[w] = midg
        bg = midg.astype(bf16)
        yield
        yield (1, attg, bg)
        daT = nn(wo[...], bg)
        yield
        dq, dk, dv = [], [], []
        das, rows = [], []
        for h in range(HEADS):
            blk = slice(E * h, E * h + E)
            da = (daT[blk] * invs[h]).astype(bf16)
            inner = -jnp.sum(da.astype(f32) * att[h], axis=0, keepdims=True)
            hi = inner.astype(bf16).astype(f32)
            mi = (inner - hi).astype(bf16).astype(f32)
            lo = inner - hi - mi
            das.append(da)
            rows.append(jnp.concatenate([hi, mi, lo, jnp.zeros((13, T), f32)], 0).astype(bf16))
        yield
        daT2 = jnp.concatenate(das, 0)
        tiles = []
        for (k, pair), e in zip(TILES, exps):
            cut = slice(H * k, H * k + H)
            right = jnp.concatenate(
                [jnp.concatenate([spread(das[g][:, cut], g), rows[g][:, cut]], 0) for g in pair], 1)
            dP = nn(vrow1[0:H] if k == 0 else vrow1, right)
            tiles.append((e * dP).astype(bf16))
            yield
        tiles = [tiles[0], tiles[1], jnp.concatenate([tiles[2], tiles[3]], 0)]

        def by_query(m, tiles):
            tops = [nn(m[2 * E * p:2 * E * p + 2 * E], tiles[p]) for p in (0, 1)]
            low = nn(stack_keys(m), tiles[2])
            out = []
            for g in range(HEADS):
                at, cut, row = slice(H * (g // 2), H * (g // 2) + H), slice(H * (g % 2), H * (g % 2) + H), E * EARLY.index(g)
                out.append(jnp.concatenate([low[row:row + E, at], tops[g // 2][E * (g % 2):E * (g % 2) + E, cut]], 1))
            return out

        def by_key(m, tiles, which):
            for p in range(3):
                turn[w, 3 * which + p] = tiles[p].T
            tops = [nn(stack_late(m, p), turn[w, 3 * which + p]) for p in (0, 1)]
            low = nn(stack_early(m), turn[w, 3 * which + 2])
            out = []
            for g in range(HEADS):
                at, row = slice(H * (g % 2), H * (g % 2) + H), E * EARLY.index(g)
                top = tops[g // 2][E * (g % 2):E * (g % 2) + E]
                out.append(jnp.concatenate([top[:, 0:H] + low[row:row + E, at], top[:, H:T]], 1))
            return out

        dq = [v * scale for v in by_query(kT, tiles)]
        yield
        dk = [v * scale for v in by_key(qT, tiles, 0)]
        yield
        dv = by_key(daT2, lows, 1)
        yield
        pg = jnp.concatenate(dq + dk + dv, 0).astype(bf16)
        dn1 = nn(wqkv[...], pg)
        yield (0, a1g, pg)
        alng[1] += dn1 * n1
        dn_ref[w] = dn1

    accs = (aqkv, ao, aup, ad)
    turns = (t0, t1, t2, t3)
    held = [[[] for _ in accs] for _ in batches]
    live_windows, w = [], 0
    for at, (size, begin) in enumerate(batches):
        for _ in range(size):
            live_windows.append((begin, window(w), at))
            w += 1
    tick = 0
    while live_windows:
        still = []
        for begin, gen, batch in live_windows:
            if tick < begin:
                still.append((begin, gen, batch))
                continue
            try:
                item = next(gen)
            except StopIteration:
                continue
            still.append((begin, gen, batch))
            if item is not None:
                k, left, right = item
                pairs, size = held[batch][k], batches[batch][0]
                turns[k][len(pairs)] = right.T
                pairs.append(left)
                if len(pairs) == size:
                    accs[k][...] += nn(jnp.concatenate(pairs, 1), turns[k][0:size].reshape(size * T, right.shape[0]))
        live_windows = still
        tick += 1

    def end():
        def row(k):
            a = alng[k]
            a = a[:, 0:H] + a[:, H:T]
            return jnp.sum(a.T, axis=0, keepdims=True)

        def shift(sums, weight):
            hi = sums.astype(bf16).astype(f32)
            mi = (sums - hi).astype(bf16).astype(f32)
            parts = jnp.concatenate([hi, mi, sums - hi - mi, jnp.zeros((13, sums.shape[1]), f32)], 0)
            return jnp.sum(nt(parts.astype(bf16), weight), axis=0, keepdims=True)

        vec = jnp.concatenate(
            [row(1), shift(aqkv[D:D + 1, :], wqkv[...]), aqkv[D:D + 1, 0:D], aqkv[D:D + 1, 2 * D:3 * D], ao[D:D + 1, :],
             row(0), shift(aup[D:D + 1, :], wup[...]), ad[FF:FF + 1, :]]
            + [aup[D:D + 1, D * b:D * b + D] for b in range(4)] + [jnp.zeros((4, D), f32)], 0)
        for k in range(PIECES // 2):
            for ref, half in ((keep_ref, core), (send_ref, 1 - core)):
                o = jnp.bitwise_xor(me, slot_of(half, k, BACK))
                r16 = pl.ds(pl.multiple_of(o * 16, 16), 16)
                for b in range(3):
                    ref[k, 16 * b:16 * b + 16, :] = aqkv[r16, D * b:D * b + D].astype(bf16)
                ref[k, 48:64, :] = ao[r16, :].astype(bf16)
                for b in range(4):
                    ref[k, 64 + 16 * b:80 + 16 * b, :] = aup[r16, D * b:D * b + D].astype(bf16)
                ref[k, 128:192, :] = ad[pl.ds(pl.multiple_of(o * 64, 64), 64), :].astype(bf16)
                ref[k, 192:208, :] = vec.astype(bf16)

    end()

def prepare_tokens(x, ct):
    count, T, D = x.shape
    vmem = pl.BlockSpec(memory_space=pltpu.VMEM)
    turned = jax.ShapeDtypeStruct((count, D, T), f32)
    return pl.pallas_call(
        tokens_kernel,
        in_specs=[vmem] * 2,
        out_specs=[vmem] * 4,
        out_shape=[turned, turned, jax.ShapeDtypeStruct((count, 8, T), f32), jax.ShapeDtypeStruct(ct.shape, bf16)],
        compiler_params=pltpu.CompilerParams(vmem_limit_bytes=16 << 20),
        cost_estimate=pl.CostEstimate(flops=0, bytes_accessed=count * T * D * 40, transcendentals=0),
        name="prepare_tokens",
    )(x, ct)


def prepare_cotangent(valid, ct):
    count, T, D = ct.shape
    vmem = pl.BlockSpec(memory_space=pltpu.VMEM)
    return pl.pallas_call(
        cotangent_kernel,
        in_specs=[vmem] * 2,
        out_specs=[vmem] * 2,
        out_shape=[jax.ShapeDtypeStruct((count, D, T), f32), jax.ShapeDtypeStruct((count, T + T // 2, T // 2), bf16)],
        compiler_params=pltpu.CompilerParams(vmem_limit_bytes=16 << 20),
        cost_estimate=pl.CostEstimate(flops=0, bytes_accessed=count * T * D * 20, transcendentals=0),
        name="prepare_cotangent",
    )(valid, ct)


def results_kernel(act_ref, mid_ref, midg_ref, dn_ref, wdT, gain_ref, bias_ref, n_ref, r_ref, lo_ref, tg_ref, lo_buf, tg_buf, sems):
    copies = []
    for w in range(act_ref.shape[0]):
        lo_buf[w] = (mid_ref[w] + nn(wdT[...], act_ref[w])).T + bias_ref[0:1, :]
        tg_buf[w] = (midg_ref[w] + norm_back(dn_ref[w], gain_ref[...], n_ref[w], r_ref[w, 0:1])).T
        for k, (buf, ref) in enumerate(((lo_buf, lo_ref), (tg_buf, tg_ref))):
            copies.append(pltpu.make_async_copy(buf.at[w], ref.at[w], sems.at[k, w]))
            copies[-1].start()
    for copy in copies:
        copy.wait()


def layer(slots, ready, batches=None, spread_out=True):
    count, D, T = ready[0].shape
    FF = 512
    batches = batches or ((count // 2, 0), (count - count // 2, 13))
    group = max(size for size, _ in batches)
    vm = lambda s, d: pltpu.VMEM(s, d)
    vmem = pl.BlockSpec(memory_space=pltpu.VMEM)
    half = jax.ShapeDtypeStruct((PIECES // 2, GRAD_ROWS, D), bf16)
    turned = jax.ShapeDtypeStruct((count, D, T), f32)
    return pl.pallas_call(
        functools.partial(layer_kernel, batches=batches, spread_out=spread_out),
        in_specs=[vmem] * 7,
        out_specs=[vmem] * 9,
        out_shape=[half, half, jax.ShapeDtypeStruct((count, FF, T), bf16), turned, turned, turned,
                   jax.ShapeDtypeStruct((D, FF), bf16), jax.ShapeDtypeStruct((D, T), f32), jax.ShapeDtypeStruct((8, D), f32)],
        scratch_shapes=[
            vm((D, 3 * D), bf16), vm((3 * D, D + 16), bf16), vm((D, D), bf16), vm((D, D + 16), bf16),
            vm((D, FF), bf16), vm((FF, D + 16), bf16), vm((FF, D), bf16),
            vm((4, D, T), f32),
            vm((D + 16, 3 * D), f32), vm((D + 16, D), f32), vm((D + 16, FF), f32), vm((FF + 16, D), f32),
            vm((2, D, T), f32), vm((count, 6, T, T), bf16),
            vm((group, T, 3 * D), bf16), vm((group, T, D), bf16), vm((group, T, FF), bf16), vm((group, T, D), bf16)],
        compiler_params=pltpu.CompilerParams(vmem_limit_bytes=32 << 20),
        name="layer",
    )(*slots, *ready)


def results(parts, ready):
    n, r = ready[1:3]
    count, D, T = n.shape
    vmem = pl.BlockSpec(memory_space=pltpu.VMEM)
    rows = jax.ShapeDtypeStruct((count, T, D), f32)
    return pl.pallas_call(
        results_kernel,
        in_specs=[vmem] * 9,
        out_specs=[pl.BlockSpec(memory_space=pl.ANY)] * 2,
        out_shape=[rows] * 2,
        scratch_shapes=[pltpu.VMEM((count, T, D), f32)] * 2 + [pltpu.SemaphoreType.DMA((2, count))],
        compiler_params=pltpu.CompilerParams(vmem_limit_bytes=16 << 20),
        cost_estimate=pl.CostEstimate(flops=2 * count * T * D * 512, bytes_accessed=count * T * D * 40, transcendentals=0),
        name="results",
    )(*parts, n, r)


VMEM = pl.BlockSpec(memory_space=pltpu.VMEM)
SMEM = pl.BlockSpec(memory_space=pltpu.SMEM)
HBM = pl.BlockSpec(memory_space=pltpu.HBM)
SMALL = pltpu.CompilerParams(vmem_limit_bytes=16 << 20)
ALONE = pltpu.CompilerParams(vmem_limit_bytes=60 << 20)


def pack_kernel(*refs, span):
    hbm, out_ref, valid_ref, held, sems = refs[:15], refs[15], refs[16], refs[17:32], refs[32]
    copies = [pltpu.make_async_copy(src, dst, sems.at[k]) for k, (src, dst) in enumerate(zip(hbm, held))]
    for copy in copies:
        copy.start()
    gain_a, shift_a, qkv, query, value, outw, outb, gain_m, shift_m, upw, upb, downw, downb, lens, starts = held
    me, core = place()
    D = out_ref.shape[1]
    row = lax.broadcasted_iota(jnp.int32, (16, D), 0)
    lane16 = lax.broadcasted_iota(jnp.int32, (16, D), 1)
    spot16 = (lane16 == row + 16 * me).astype(bf16)
    r64 = lax.broadcasted_iota(jnp.int32, (64, D), 0)
    l64 = lax.broadcasted_iota(jnp.int32, (64, D), 1)
    spot64 = (l64 == r64 + 64 * jnp.bitwise_and(me, 1)).astype(bf16)
    for copy in copies:
        copy.wait()
    for b in range(3):
        out_ref[16 * b:16 * b + 16, :] = qkv[:, D * b:D * b + D]
    out_ref[48:64, :] = outw[...]
    for b in range(4):
        out_ref[64 + 16 * b:80 + 16 * b, :] = upw[:, D * b:D * b + D]
    out_ref[128:192, :] = downw[...]
    total = jnp.zeros((16, D), f32)
    for k, ref in enumerate((gain_a, shift_a, query, value, outb, gain_m, shift_m, downb)):
        v = jnp.broadcast_to(ref[...].astype(f32).reshape(1, 16), (16, 16)).astype(bf16)
        total = total + jnp.where(row == k, nn(v, spot16), 0.0)
    v = jnp.broadcast_to(upb[...].astype(f32).reshape(1, 64), (16, 64)).astype(bf16)
    total = total + jnp.where(row == 8 + lax.shift_right_logical(me, 1), nn(v, spot64), 0.0)
    out_ref[192:208, :] = total.astype(bf16)
    for w in range(valid_ref.shape[0]):
        valid_ref[w:w + 1, :] = jnp.full((1, D), jnp.clip(lens[w] - starts[w], 1, span), jnp.int32)


def added(parts):
    total = parts[0].astype(f32)
    for p in parts[1:]:
        total = total + p.astype(f32)
    return total


def pair_kernel(keep_ref, got_ref, *out_refs):
    for k, ref in enumerate(out_refs):
        ref[...] = added([keep_ref[k], got_ref[k]]).astype(bf16)


def merge_kernel(own_ref, r0, r1, r2, r3, out_ref):
    first = jnp.where(place()[1] == 0, own_ref[...].astype(f32), r0[...].astype(f32))
    out_ref[...] = added([first, r1[...], r2[...], r3[...]]).astype(bf16)


def chip_kernel(own_ref, got_ref, out_ref):
    out_ref[...] = added([own_ref[...], got_ref[...]]).astype(bf16)


def finish_kernel(m0, m1, gain_a, shift_a, qkv, query, value, outw, outb, gain_m, shift_m, upw, upb, downw, downb):
    me, core = place()
    D = m0.shape[1]
    total = added([m0[...], m1[...]])
    main, vec = total[0:192], total[192:208]
    for b in range(3):
        qkv[:, D * b:D * b + D] = main[16 * b:16 * b + 16]
    outw[...] = main[48:64]
    for b in range(4):
        upw[:, D * b:D * b + D] = main[64 + 16 * b:80 + 16 * b]
    downw[...] = main[128:192]
    turned = pltpu.roll(vec, jnp.bitwise_and(D - 16 * me, D - 1), 1)
    for k, ref in enumerate((gain_a, shift_a, query, value, outb, gain_m, shift_m, downb)):
        ref[...] = turned[k:k + 1, 0:16].reshape(16)
    row = lax.broadcasted_iota(jnp.int32, (16, D), 0)
    half = jnp.sum(jnp.where(row == 8 + lax.shift_right_logical(me, 1), vec, 0.0), axis=0, keepdims=True)
    half = jnp.where(jnp.bitwise_and(me, 1) == 0, half[:, 0:64], half[:, 64:128])
    upb[...] = half.reshape(64)


def per_device(tokens, episode_length, window_start, *rest):
    params, cotangent = rest[:13], rest[13]
    D = tokens.shape[2]
    grp, wide = lax.axis_size("grp"), lax.axis_size("wide")
    axes = ("grp", "wide")

    def across(core_slots, keep_own=False):
        pairs = []
        for g in range(grp):
            s = core_slots[g % 2]
            if s or keep_own:
                pairs += [(g * wide + i, g * wide + (i ^ s)) for i in range(wide)]
        return pairs

    swap = [(g * wide + i, (g ^ 1) * wide + i) for g in range(grp) for i in range(wide)]
    count = tokens.shape[0]
    piece, valid = pl.pallas_call(
        functools.partial(pack_kernel, span=tokens.shape[1]), in_specs=[HBM] * 15, out_specs=[VMEM] * 2,
        out_shape=[jax.ShapeDtypeStruct((PIECE_ROWS, D), bf16), jax.ShapeDtypeStruct((count, D), jnp.int32)],
        compiler_params=ALONE, name="pack",
        cost_estimate=pl.CostEstimate(flops=0, bytes_accessed=40 << 20, transcendentals=0),
        scratch_shapes=[pltpu.VMEM(p.shape, bf16) for p in params] + [pltpu.SMEM((count,), jnp.int32)] * 2
        + [pltpu.SemaphoreType.DMA((15,))],
    )(*params, episode_length, window_start)
    hops = [across((SLOTS[0][k], SLOTS[1][k]), True) for k in range(4)]
    direct = [lax.ppermute(piece, axes, hops[k]) for k in range(4)]
    *ready, ct_here = prepare_tokens(tokens, cotangent)
    joined, ready, ct_here = lax.optimization_barrier((jnp.concatenate(direct, 0), ready, ct_here))
    others = lax.ppermute(joined, axes, swap)
    ready = [*ready, *prepare_cotangent(valid, ct_here)]
    keep, send, *parts = layer([joined, others], ready)
    got = lax.ppermute(send, axes, swap)
    shape = jax.ShapeDtypeStruct((GRAD_ROWS, D), bf16)
    pairs = pl.pallas_call(
        pair_kernel, in_specs=[VMEM] * 2, out_specs=[VMEM] * 4, out_shape=[shape] * 4, compiler_params=SMALL, name="pair",
    )(keep, got)
    pairs, parts = lax.optimization_barrier((pairs, parts))
    layer_out, tokens_grad = results(parts, ready)
    back = [across((BACK[0][k], BACK[1][k])) for k in range(4)]
    came = [lax.ppermute(pairs[k], axes, back[k]) for k in range(4)]
    merged = pl.pallas_call(
        merge_kernel, in_specs=[VMEM] * 5, out_specs=VMEM, out_shape=shape, compiler_params=SMALL, name="merge",
    )(pairs[0], *came)
    beside = lax.ppermute(merged, axes, swap)
    chip = pl.pallas_call(
        chip_kernel, in_specs=[VMEM] * 2, out_specs=VMEM, out_shape=shape, compiler_params=SMALL, name="chip",
    )(merged, beside)
    over = [(g * wide + i, (g ^ 2) * wide + i) for g in range(grp) for i in range(wide)]
    every = [chip, lax.ppermute(chip, axes, over)]
    grads = pl.pallas_call(
        finish_kernel, in_specs=[VMEM] * 2, out_specs=[VMEM] * 13,
        out_shape=[jax.ShapeDtypeStruct(p.shape, f32) for p in params], compiler_params=SMALL, name="finish",
    )(*every)
    return (layer_out, tokens_grad, *grads)


def gathered(tokens, episode_length, window_start, *rest):
    params, cotangent = rest[:13], rest[13]
    D = tokens.shape[2]
    full = [lax.all_gather(p, "wide", axis=0, tiled=True) for p in params]
    gain_a, shift_a, qkv, query, value, outw, outb, gain_m, shift_m, upw, upb, downw, downb = full
    FF = upw.shape[1]
    lanes = jnp.arange(D) // (D // PIECES)
    spots = (lanes[None, :] == jnp.arange(PIECES)[:, None]).astype(bf16)
    vectors = jnp.stack([gain_a, shift_a, query, value, outb, gain_m, shift_m, downb])[None] * spots[:, None, :]
    where_up = (jnp.arange(FF) // (FF // PIECES))[None, :] == jnp.arange(PIECES)[:, None]
    ups = (upb[None] * where_up.astype(bf16)).reshape(PIECES, FF // D, D)

    def blocks(weight):
        cut = weight.reshape(PIECES, weight.shape[0] // PIECES, weight.shape[1] // D, D)
        return cut.transpose(0, 2, 1, 3).reshape(PIECES, -1, D)

    slots = jnp.concatenate(
        [blocks(qkv), blocks(outw), blocks(upw), blocks(downw), vectors, ups, jnp.zeros((PIECES, 4, D), bf16)], 1
    )
    mine, others = [jnp.concatenate([slots[s] for s in half], 0) for half in SLOTS]
    count, span = tokens.shape[:2]
    valid = jnp.broadcast_to(jnp.clip(episode_length - window_start, 1, span)[:, None], (count, D))
    *ready, ct_here = prepare_tokens(tokens, cotangent)
    ready = [*ready, *prepare_cotangent(valid, ct_here)]
    keep, send, *parts = layer([mine, others], ready, spread_out=False)
    layer_out, tokens_grad = results(parts, ready)
    order = [0] * PIECES
    for half in (0, 1):
        for k in range(4):
            order[BACK[half][k]] = 4 * half + k
    pieces = jnp.concatenate([keep, send], 0)[jnp.array(order)].astype(f32)
    vec = pieces[0, 192:208]

    def rebuilt(first, last, weight):
        cut = pieces[:, first:last].reshape(PIECES, weight.shape[1] // D, weight.shape[0] // PIECES, D)
        return cut.transpose(0, 2, 1, 3).reshape(weight.shape)

    grads = (
        vec[0], vec[1], rebuilt(0, 48, qkv), vec[2], vec[3], rebuilt(48, 64, outw), vec[4], vec[5], vec[6],
        rebuilt(64, 128, upw), vec[8:12].reshape(FF), rebuilt(128, 192, downw), vec[7],
    )
    grads = [lax.psum_scatter(g, "wide", scatter_dimension=0, tiled=True) for g in grads]
    return (layer_out, tokens_grad, *lax.psum(grads, "grp"))


def solution(mesh):
    rows = P(("grp", "wide"), None, None)
    flat = P(("grp", "wide"))
    one, two = P("wide"), P("wide", None)
    params = (one, one, two, one, one, two, one, one, one, two, one, two, one)
    fits = mesh.shape["wide"] == PIECES and mesh.shape["grp"] == 4
    return jax.shard_map(
        per_device if fits else gathered, mesh=mesh, in_specs=(rows, flat, flat, *params, rows), out_specs=(rows, rows, *params), check_vma=False
    )
```

```python
import math
import functools

import jax
import jax.numpy as jnp
from jax import lax
from jax.experimental import pallas as pl
from jax.experimental.pallas import tpu as pltpu
from jax.sharding import PartitionSpec as P

HEADS = 4
EPS = 1e-05
CUBIC = 0.044715
TANH_SCALE = math.sqrt(2.0 / math.pi)
NEG_FILL = -1e30
LOG2E = math.log2(math.e)
f32, bf16 = jnp.float32, jnp.bfloat16
PIECES = 8
PIECE_ROWS = 208
GRAD_ROWS = 208
SLOTS = ((0, 4, 5, 6), (1, 2, 3, 7))
BACK = ((0, 6, 5, 4), (1, 7, 3, 2))

TILES = ((1, (0, 1)), (1, (2, 3)), (0, (0, 2)), (0, (1, 3)))
EARLY = (0, 2, 1, 3)


def place():
    return lax.axis_index("wide").astype(jnp.int32), jnp.bitwise_and(lax.axis_index("grp").astype(jnp.int32), 1)


def slot_of(core, k, table=SLOTS):
    return jnp.where(core == 0, table[0][k], table[1][k])


def nn(a, b):
    return lax.dot_general(a, b, (((1,), (0,)), ((), ())), preferred_element_type=f32)

def nt(a, b):
    return lax.dot_general(a, b, (((1,), (1,)), ((), ())), preferred_element_type=f32)

def norm(v):
    d = v.shape[0]
    off = v - jnp.sum(v, axis=0, keepdims=True) * (1.0 / d)
    r = lax.rsqrt(jnp.sum(off * off, axis=0, keepdims=True) * (1.0 / d) + EPS)
    return off * r, r

def norm_back(dy, gain, n, r):
    d = dy.shape[0]
    g = dy * gain
    mg = jnp.sum(g, axis=0, keepdims=True) * (1.0 / d)
    mgn = jnp.sum(g * n, axis=0, keepdims=True) * (1.0 / d)
    return r * (g - mg - n * mgn)

def tokens_kernel(x_in, ct_in, x_ref, n_ref, r_ref, ct_ref):
    count, T, D = x_in.shape
    for w in range(count):
        xT = x_in[w].astype(f32).T
        n, r = norm(xT)
        x_ref[w] = xT
        n_ref[w] = n
        r_ref[w] = jnp.broadcast_to(r, (8, T))
        ct_ref[w] = ct_in[w]


def cotangent_kernel(valid_ref, ct_in, up_ref, mask_ref):
    count, T, D = ct_in.shape
    H = T // 2
    for w in range(count):
        valid = valid_ref[w:w + 1, :]
        live = (lax.broadcasted_iota(jnp.int32, (1, T), 1) < jnp.concatenate([valid, valid], 1)).astype(f32)
        up_ref[w] = ct_in[w].astype(f32).T * live
        j = lax.broadcasted_iota(jnp.int32, (H, H), 0)
        tri = j <= lax.broadcasted_iota(jnp.int32, (H, H), 1)
        for k, seen in enumerate((tri & (j < valid), j < valid, tri & (j + H < valid))):
            mask_ref[w, H * k:H * k + H] = jnp.where(seen, 0.0, NEG_FILL).astype(bf16)


def layer_kernel(mine, others, x_ref, n_ref, r_ref, up_ref, mask_ref,
                 keep_ref, send_ref, act_ref, mid_ref, midg_ref, dn_ref, wdT, gain_ref, bias_ref,
                 wqkv, wqkvT, wo, woT, wup, wupT, wd, cols,
                 aqkv, ao, aup, ad, alng, turn, t0, t1, t2, t3, *, batches, spread_out):
    me, core = place() if spread_out else (jnp.int32(0), jnp.int32(0))
    D, T = x_ref.shape[1], x_ref.shape[2]
    H = T // 2
    E = D // HEADS
    FF = wup.shape[1]
    scale = E ** -0.5

    def start():
        vec = jnp.zeros((16, D), f32)
        places = [(slot_of(half, k), ref, PIECE_ROWS * k) for half, ref in ((core, mine), (1 - core, others)) for k in range(PIECES // 2)]
        for slot, ref, at in places:
            o = jnp.bitwise_xor(me, slot)
            r16 = pl.ds(pl.multiple_of(o * 16, 16), 16)
            get = lambda first, last: ref[at + first:at + last, :]
            for b in range(3):
                wqkv[r16, D * b:D * b + D] = get(16 * b, 16 * b + 16)
            wo[r16, :] = get(48, 64)
            for b in range(4):
                wup[r16, D * b:D * b + D] = get(64 + 16 * b, 80 + 16 * b)
            wd[pl.ds(pl.multiple_of(o * 64, 64), 64), :] = get(128, 192)
            vec = vec + get(192, 208).astype(f32)
        vecT = jnp.concatenate([vec, jnp.zeros((D - 16, D), f32)], 0).T
        lane = lax.broadcasted_iota(jnp.int32, (D, 16), 1)
        def col(k):
            return jnp.where(lane == k, vecT[:, 0:16], 0.0).astype(bf16)
        def full(k):
            return jnp.broadcast_to(vecT[:, k:k + 1], (D, T))
        for b in range(3):
            wqkvT[D * b:D * b + D, 0:D] = wqkv[:, D * b:D * b + D].T
        wqkvT[0:D, D:D + 16] = col(2)
        wqkvT[D:2 * D, D:D + 16] = jnp.zeros((D, 16), bf16)
        wqkvT[2 * D:3 * D, D:D + 16] = col(3)
        woT[:, 0:D] = wo[...].T
        woT[:, D:D + 16] = col(4)
        for b in range(4):
            wupT[D * b:D * b + D, 0:D] = wup[:, D * b:D * b + D].T
            wupT[D * b:D * b + D, D:D + 16] = col(8 + b)
            wdT[:, D * b:D * b + D] = wd[D * b:D * b + D, :].T
        bias_ref[...] = jnp.broadcast_to(vec[7:8, :], (8, D))
        gain_ref[...] = full(0)
        cols[0] = full(0)
        cols[1] = full(1)
        cols[2] = full(5)
        cols[3] = full(6)
        for ref in (aqkv, ao, aup, ad, alng):
            ref[...] = jnp.zeros(ref.shape, f32)

    start()
    ones = jnp.ones((16, T), bf16)
    eye2 = (lax.broadcasted_iota(jnp.int32, (H, T), 0) == jnp.bitwise_and(lax.broadcasted_iota(jnp.int32, (H, T), 1), H - 1)).astype(f32).astype(bf16)

    def spread(m, h):
        parts = []
        if h > 0:
            parts.append(jnp.zeros((E * h, m.shape[1]), bf16))
        parts.append(m)
        if h < HEADS - 1:
            parts.append(jnp.zeros((E * (HEADS - 1 - h), m.shape[1]), bf16))
        return jnp.concatenate(parts, 0)

    none = jnp.zeros((16, H), bf16)
    blank = jnp.zeros((E, H), bf16)

    def beside(m, g, first, put):
        part = m[E * g:E * g + E, H * first:H * first + H]
        return jnp.concatenate([part, blank] if put == 0 else [blank, part], 1)

    def stack_keys(m):
        return jnp.concatenate([beside(m, g, 0, g % 2) for g in EARLY], 0)

    def stack_early(m):
        return jnp.concatenate([beside(m, g, 0, g // 2) for g in EARLY], 0)

    def stack_late(m, p):
        return jnp.concatenate([beside(m, 2 * p, 1, 0), beside(m, 2 * p + 1, 1, 1)], 0)

    def window(w):
        idx = w
        n1, r1 = n_ref[idx], r_ref[idx, 0:1]
        a1 = (n1 * cols[0] + cols[1]).astype(bf16)
        a1g = jnp.concatenate([a1, ones], 0)
        yield
        qT = nn(wqkvT[0:D, :], a1g).astype(bf16)
        kT = nn(wqkvT[D:2 * D, :], a1g).astype(bf16)
        vT = nn(wqkvT[2 * D:3 * D, :], a1g).astype(bf16)
        yield
        krow, vrow = kT.T, vT.T
        left = (jnp.concatenate([krow[0:H], mask_ref[idx, 0:H]], 1), jnp.concatenate([krow, mask_ref[idx, H:H + T]], 1))
        vrow1 = jnp.concatenate([vrow, jnp.ones((T, 16), bf16)], 1)
        yield
        exps = []
        for k, pair in TILES:
            cut = slice(H * k, H * k + H)
            right = jnp.concatenate([spread(qT[E * g:E * g + E, cut], g) for g in pair], 1)
            S = nn(left[k], jnp.concatenate([right, eye2], 0))
            exps.append(jnp.exp2((S - jnp.max(S, axis=0, keepdims=True)) * (scale * LOG2E)))
            yield
        lows = [exps[0].astype(bf16), exps[1].astype(bf16), jnp.concatenate([exps[2].astype(bf16), exps[3].astype(bf16)], 0)]
        tops = [nn(jnp.concatenate([vT[E * 2 * p:E * 2 * p + 2 * E], ones], 0), lows[p]) for p in (0, 1)]
        yield
        early = nn(jnp.concatenate([stack_keys(vT), jnp.concatenate([ones[:, 0:H], none], 1), jnp.concatenate([none, ones[:, 0:H]], 1)], 0), lows[2])
        att, invs = [], []
        for g in range(HEADS):
            top, low = tops[g // 2], early[4 * E + 16 * (g % 2):4 * E + 16 * (g % 2) + 1]
            cut, at = slice(H * (g % 2), H * (g % 2) + H), slice(H * (g // 2), H * (g // 2) + H)
            inv = 1.0 / jnp.concatenate([low[:, at], top[2 * E:2 * E + 1, cut]], 1)
            invs.append(inv)
            row = E * EARLY.index(g)
            att.append(jnp.concatenate([early[row:row + E, at], top[E * (g % 2):E * (g % 2) + E, cut]], 1) * inv)
        yield
        attT = jnp.concatenate(att, 0)
        attg = jnp.concatenate([attT.astype(bf16), ones], 0)
        mid = x_ref[idx] + nn(woT[...], attg)
        yield
        n2, r2 = norm(mid)
        a2 = (n2 * cols[2] + cols[3]).astype(bf16)
        a2g = jnp.concatenate([a2, ones], 0)
        upT = up_ref[idx]
        upb = upT.astype(bf16)
        yield
        acts, hgs = [], []
        for b in range(FF // D):
            blk = slice(D * b, D * b + D)
            hid = nn(wupT[blk, :], a2g)
            v2 = hid * hid
            s = 0.5 * jnp.tanh(hid * (TANH_SCALE + (TANH_SCALE * CUBIC) * v2)) + 0.5
            act = hid * s
            acts.append(act.astype(bf16))
            gp = s + act * (1.0 - s) * (2 * TANH_SCALE + (6 * TANH_SCALE * CUBIC) * v2)
            hgs.append((nn(wd[blk, :], upb) * gp).astype(bf16))
            yield
        actg = jnp.concatenate(acts + [ones], 0)
        hg = jnp.concatenate(hgs, 0)
        act_ref[w] = actg[0:FF]
        mid_ref[w] = mid
        yield
        yield (3, actg, upb)
        dn2 = nn(wup[...], hg)
        yield (2, a2g, hg)
        alng[0] += dn2 * n2
        midg = upT + norm_back(dn2, cols[2], n2, r2)
        midg_ref[w] = midg
        bg = midg.astype(bf16)
        yield
        yield (1, attg, bg)
        daT = nn(wo[...], bg)
        yield
        dq, dk, dv = [], [], []
        das, rows = [], []
        for h in range(HEADS):
            blk = slice(E * h, E * h + E)
            da = (daT[blk] * invs[h]).astype(bf16)
            inner = -jnp.sum(da.astype(f32) * att[h], axis=0, keepdims=True)
            hi = inner.astype(bf16).astype(f32)
            mi = (inner - hi).astype(bf16).astype(f32)
            lo = inner - hi - mi
            das.append(da)
            rows.append(jnp.concatenate([hi, mi, lo, jnp.zeros((13, T), f32)], 0).astype(bf16))
        yield
        daT2 = jnp.concatenate(das, 0)
        tiles = []
        for (k, pair), e in zip(TILES, exps):
            cut = slice(H * k, H * k + H)
            right = jnp.concatenate(
                [jnp.concatenate([spread(das[g][:, cut], g), rows[g][:, cut]], 0) for g in pair], 1)
            dP = nn(vrow1[0:H] if k == 0 else vrow1, right)
            tiles.append((e * dP).astype(bf16))
            yield
        tiles = [tiles[0], tiles[1], jnp.concatenate([tiles[2], tiles[3]], 0)]

        def by_query(m, tiles):
            tops = [nn(m[2 * E * p:2 * E * p + 2 * E], tiles[p]) for p in (0, 1)]
            low = nn(stack_keys(m), tiles[2])
            out = []
            for g in range(HEADS):
                at, cut, row = slice(H * (g // 2), H * (g // 2) + H), slice(H * (g % 2), H * (g % 2) + H), E * EARLY.index(g)
                out.append(jnp.concatenate([low[row:row + E, at], tops[g // 2][E * (g % 2):E * (g % 2) + E, cut]], 1))
            return out

        def by_key(m, tiles, which):
            for p in range(3):
                turn[w, 3 * which + p] = tiles[p].T
            tops = [nn(stack_late(m, p), turn[w, 3 * which + p]) for p in (0, 1)]
            low = nn(stack_early(m), turn[w, 3 * which + 2])
            out = []
            for g in range(HEADS):
                at, row = slice(H * (g % 2), H * (g % 2) + H), E * EARLY.index(g)
                top = tops[g // 2][E * (g % 2):E * (g % 2) + E]
                out.append(jnp.concatenate([top[:, 0:H] + low[row:row + E, at], top[:, H:T]], 1))
            return out

        dq = [v * scale for v in by_query(kT, tiles)]
        yield
        dk = [v * scale for v in by_key(qT, tiles, 0)]
        yield
        dv = by_key(daT2, lows, 1)
        yield
        pg = jnp.concatenate(dq + dk + dv, 0).astype(bf16)
        dn1 = nn(wqkv[...], pg)
        yield (0, a1g, pg)
        alng[1] += dn1 * n1
        dn_ref[w] = dn1

    accs = (aqkv, ao, aup, ad)
    turns = (t0, t1, t2, t3)
    held = [[[] for _ in accs] for _ in batches]
    live_windows, w = [], 0
    for at, (size, begin) in enumerate(batches):
        for _ in range(size):
            live_windows.append((begin, window(w), at))
            w += 1
    tick = 0
    while live_windows:
        still = []
        for begin, gen, batch in live_windows:
            if tick < begin:
                still.append((begin, gen, batch))
                continue
            try:
                item = next(gen)
            except StopIteration:
                continue
            still.append((begin, gen, batch))
            if item is not None:
                k, left, right = item
                pairs, size = held[batch][k], batches[batch][0]
                turns[k][len(pairs)] = right.T
                pairs.append(left)
                if len(pairs) == size:
                    accs[k][...] += nn(jnp.concatenate(pairs, 1), turns[k][0:size].reshape(size * T, right.shape[0]))
        live_windows = still
        tick += 1

    def end():
        def row(k):
            a = alng[k]
            a = a[:, 0:H] + a[:, H:T]
            return jnp.sum(a.T, axis=0, keepdims=True)

        def shift(sums, weight):
            hi = sums.astype(bf16).astype(f32)
            mi = (sums - hi).astype(bf16).astype(f32)
            parts = jnp.concatenate([hi, mi, sums - hi - mi, jnp.zeros((13, sums.shape[1]), f32)], 0)
            return jnp.sum(nt(parts.astype(bf16), weight), axis=0, keepdims=True)

        vec = jnp.concatenate(
            [row(1), shift(aqkv[D:D + 1, :], wqkv[...]), aqkv[D:D + 1, 0:D], aqkv[D:D + 1, 2 * D:3 * D], ao[D:D + 1, :],
             row(0), shift(aup[D:D + 1, :], wup[...]), ad[FF:FF + 1, :]]
            + [aup[D:D + 1, D * b:D * b + D] for b in range(4)] + [jnp.zeros((4, D), f32)], 0)
        for k in range(PIECES // 2):
            for ref, half in ((keep_ref, core), (send_ref, 1 - core)):
                o = jnp.bitwise_xor(me, slot_of(half, k, BACK))
                r16 = pl.ds(pl.multiple_of(o * 16, 16), 16)
                for b in range(3):
                    ref[k, 16 * b:16 * b + 16, :] = aqkv[r16, D * b:D * b + D].astype(bf16)
                ref[k, 48:64, :] = ao[r16, :].astype(bf16)
                for b in range(4):
                    ref[k, 64 + 16 * b:80 + 16 * b, :] = aup[r16, D * b:D * b + D].astype(bf16)
                ref[k, 128:192, :] = ad[pl.ds(pl.multiple_of(o * 64, 64), 64), :].astype(bf16)
                ref[k, 192:208, :] = vec.astype(bf16)

    end()

def prepare_tokens(x, ct):
    count, T, D = x.shape
    vmem = pl.BlockSpec(memory_space=pltpu.VMEM)
    turned = jax.ShapeDtypeStruct((count, D, T), f32)
    return pl.pallas_call(
        tokens_kernel,
        in_specs=[vmem] * 2,
        out_specs=[vmem] * 4,
        out_shape=[turned, turned, jax.ShapeDtypeStruct((count, 8, T), f32), jax.ShapeDtypeStruct(ct.shape, bf16)],
        compiler_params=pltpu.CompilerParams(vmem_limit_bytes=16 << 20),
        cost_estimate=pl.CostEstimate(flops=0, bytes_accessed=count * T * D * 40, transcendentals=0),
        name="prepare_tokens",
    )(x, ct)


def prepare_cotangent(valid, ct):
    count, T, D = ct.shape
    vmem = pl.BlockSpec(memory_space=pltpu.VMEM)
    return pl.pallas_call(
        cotangent_kernel,
        in_specs=[vmem] * 2,
        out_specs=[vmem] * 2,
        out_shape=[jax.ShapeDtypeStruct((count, D, T), f32), jax.ShapeDtypeStruct((count, T + T // 2, T // 2), bf16)],
        compiler_params=pltpu.CompilerParams(vmem_limit_bytes=16 << 20),
        cost_estimate=pl.CostEstimate(flops=0, bytes_accessed=count * T * D * 20, transcendentals=0),
        name="prepare_cotangent",
    )(valid, ct)


def results_kernel(act_ref, mid_ref, midg_ref, dn_ref, wdT, gain_ref, bias_ref, n_ref, r_ref, lo_ref, tg_ref, lo_buf, tg_buf, sems):
    copies = []
    for w in range(act_ref.shape[0]):
        lo_buf[w] = (mid_ref[w] + nn(wdT[...], act_ref[w])).T + bias_ref[0:1, :]
        tg_buf[w] = (midg_ref[w] + norm_back(dn_ref[w], gain_ref[...], n_ref[w], r_ref[w, 0:1])).T
        for k, (buf, ref) in enumerate(((lo_buf, lo_ref), (tg_buf, tg_ref))):
            copies.append(pltpu.make_async_copy(buf.at[w], ref.at[w], sems.at[k, w]))
            copies[-1].start()
    for copy in copies:
        copy.wait()


def layer(slots, ready, batches=None, spread_out=True):
    count, D, T = ready[0].shape
    FF = 512
    batches = batches or ((count // 2, 0), (count - count // 2, 13))
    group = max(size for size, _ in batches)
    vm = lambda s, d: pltpu.VMEM(s, d)
    vmem = pl.BlockSpec(memory_space=pltpu.VMEM)
    half = jax.ShapeDtypeStruct((PIECES // 2, GRAD_ROWS, D), bf16)
    turned = jax.ShapeDtypeStruct((count, D, T), f32)
    return pl.pallas_call(
        functools.partial(layer_kernel, batches=batches, spread_out=spread_out),
        in_specs=[vmem] * 7,
        out_specs=[vmem] * 9,
        out_shape=[half, half, jax.ShapeDtypeStruct((count, FF, T), bf16), turned, turned, turned,
                   jax.ShapeDtypeStruct((D, FF), bf16), jax.ShapeDtypeStruct((D, T), f32), jax.ShapeDtypeStruct((8, D), f32)],
        scratch_shapes=[
            vm((D, 3 * D), bf16), vm((3 * D, D + 16), bf16), vm((D, D), bf16), vm((D, D + 16), bf16),
            vm((D, FF), bf16), vm((FF, D + 16), bf16), vm((FF, D), bf16),
            vm((4, D, T), f32),
            vm((D + 16, 3 * D), f32), vm((D + 16, D), f32), vm((D + 16, FF), f32), vm((FF + 16, D), f32),
            vm((2, D, T), f32), vm((count, 6, T, T), bf16),
            vm((group, T, 3 * D), bf16), vm((group, T, D), bf16), vm((group, T, FF), bf16), vm((group, T, D), bf16)],
        compiler_params=pltpu.CompilerParams(vmem_limit_bytes=32 << 20),
        name="layer",
    )(*slots, *ready)


def results(parts, ready):
    n, r = ready[1:3]
    count, D, T = n.shape
    vmem = pl.BlockSpec(memory_space=pltpu.VMEM)
    rows = jax.ShapeDtypeStruct((count, T, D), f32)
    return pl.pallas_call(
        results_kernel,
        in_specs=[vmem] * 9,
        out_specs=[pl.BlockSpec(memory_space=pl.ANY)] * 2,
        out_shape=[rows] * 2,
        scratch_shapes=[pltpu.VMEM((count, T, D), f32)] * 2 + [pltpu.SemaphoreType.DMA((2, count))],
        compiler_params=pltpu.CompilerParams(vmem_limit_bytes=16 << 20),
        cost_estimate=pl.CostEstimate(flops=2 * count * T * D * 512, bytes_accessed=count * T * D * 40, transcendentals=0),
        name="results",
    )(*parts, n, r)


VMEM = pl.BlockSpec(memory_space=pltpu.VMEM)
SMEM = pl.BlockSpec(memory_space=pltpu.SMEM)
HBM = pl.BlockSpec(memory_space=pltpu.HBM)
SMALL = pltpu.CompilerParams(vmem_limit_bytes=16 << 20)
ALONE = pltpu.CompilerParams(vmem_limit_bytes=60 << 20)


def pack_kernel(*refs, span):
    hbm, out_ref, valid_ref, held, sems = refs[:15], refs[15], refs[16], refs[17:32], refs[32]
    copies = [pltpu.make_async_copy(src, dst, sems.at[k]) for k, (src, dst) in enumerate(zip(hbm, held))]
    for copy in copies:
        copy.start()
    gain_a, shift_a, qkv, query, value, outw, outb, gain_m, shift_m, upw, upb, downw, downb, lens, starts = held
    me, core = place()
    D = out_ref.shape[1]
    row = lax.broadcasted_iota(jnp.int32, (16, D), 0)
    lane16 = lax.broadcasted_iota(jnp.int32, (16, D), 1)
    spot16 = (lane16 == row + 16 * me).astype(bf16)
    r64 = lax.broadcasted_iota(jnp.int32, (64, D), 0)
    l64 = lax.broadcasted_iota(jnp.int32, (64, D), 1)
    spot64 = (l64 == r64 + 64 * jnp.bitwise_and(me, 1)).astype(bf16)
    for copy in copies:
        copy.wait()
    for b in range(3):
        out_ref[16 * b:16 * b + 16, :] = qkv[:, D * b:D * b + D]
    out_ref[48:64, :] = outw[...]
    for b in range(4):
        out_ref[64 + 16 * b:80 + 16 * b, :] = upw[:, D * b:D * b + D]
    out_ref[128:192, :] = downw[...]
    short = [ref[...].astype(f32).reshape(1, 16) for ref in (gain_a, shift_a, query, value, outb, gain_m, shift_m, downb)]
    total = nn(jnp.concatenate(short + [jnp.zeros((8, 16), f32)], 0).astype(bf16), spot16)
    v = jnp.broadcast_to(upb[...].astype(f32).reshape(1, 64), (16, 64)).astype(bf16)
    total = total + jnp.where(row == 8 + lax.shift_right_logical(me, 1), nn(v, spot64), 0.0)
    out_ref[192:208, :] = total.astype(bf16)
    for w in range(valid_ref.shape[0]):
        valid_ref[w:w + 1, :] = jnp.full((1, D), jnp.clip(lens[w] - starts[w], 1, span), jnp.int32)


def added(parts):
    total = parts[0].astype(f32)
    for p in parts[1:]:
        total = total + p.astype(f32)
    return total


def pair_kernel(keep_ref, got_ref, *out_refs):
    for k, ref in enumerate(out_refs):
        ref[...] = added([keep_ref[k], got_ref[k]]).astype(bf16)


def merge_kernel(own_ref, r0, r1, r2, r3, out_ref):
    first = jnp.where(place()[1] == 0, own_ref[...].astype(f32), r0[...].astype(f32))
    out_ref[...] = added([first, r1[...], r2[...], r3[...]]).astype(bf16)


def chip_kernel(own_ref, got_ref, out_ref):
    out_ref[...] = added([own_ref[...], got_ref[...]]).astype(bf16)


def finish_kernel(m0, m1, gain_a, shift_a, qkv, query, value, outw, outb, gain_m, shift_m, upw, upb, downw, downb):
    me, core = place()
    D = m0.shape[1]
    total = added([m0[...], m1[...]])
    main, vec = total[0:192], total[192:208]
    for b in range(3):
        qkv[:, D * b:D * b + D] = main[16 * b:16 * b + 16]
    outw[...] = main[48:64]
    for b in range(4):
        upw[:, D * b:D * b + D] = main[64 + 16 * b:80 + 16 * b]
    downw[...] = main[128:192]
    turned = pltpu.roll(vec, jnp.bitwise_and(D - 16 * me, D - 1), 1)
    for k, ref in enumerate((gain_a, shift_a, query, value, outb, gain_m, shift_m, downb)):
        ref[...] = turned[k:k + 1, 0:16].reshape(16)
    row = lax.broadcasted_iota(jnp.int32, (16, D), 0)
    half = jnp.sum(jnp.where(row == 8 + lax.shift_right_logical(me, 1), vec, 0.0), axis=0, keepdims=True)
    half = jnp.where(jnp.bitwise_and(me, 1) == 0, half[:, 0:64], half[:, 64:128])
    upb[...] = half.reshape(64)


def per_device(tokens, episode_length, window_start, *rest):
    params, cotangent = rest[:13], rest[13]
    D = tokens.shape[2]
    grp, wide = lax.axis_size("grp"), lax.axis_size("wide")
    axes = ("grp", "wide")

    def across(core_slots, keep_own=False):
        pairs = []
        for g in range(grp):
            s = core_slots[g % 2]
            if s or keep_own:
                pairs += [(g * wide + i, g * wide + (i ^ s)) for i in range(wide)]
        return pairs

    swap = [(g * wide + i, (g ^ 1) * wide + i) for g in range(grp) for i in range(wide)]
    count = tokens.shape[0]
    piece, valid = pl.pallas_call(
        functools.partial(pack_kernel, span=tokens.shape[1]), in_specs=[HBM] * 15, out_specs=[VMEM] * 2,
        out_shape=[jax.ShapeDtypeStruct((PIECE_ROWS, D), bf16), jax.ShapeDtypeStruct((count, D), jnp.int32)],
        compiler_params=ALONE, name="pack",
        cost_estimate=pl.CostEstimate(flops=0, bytes_accessed=40 << 20, transcendentals=0),
        scratch_shapes=[pltpu.VMEM(p.shape, bf16) for p in params] + [pltpu.SMEM((count,), jnp.int32)] * 2
        + [pltpu.SemaphoreType.DMA((15,))],
    )(*params, episode_length, window_start)
    hops = [across((SLOTS[0][k], SLOTS[1][k]), True) for k in range(4)]
    direct = [lax.ppermute(piece, axes, hops[k]) for k in range(4)]
    *ready, ct_here = prepare_tokens(tokens, cotangent)
    joined, ready, ct_here = lax.optimization_barrier((jnp.concatenate(direct, 0), ready, ct_here))
    others = lax.ppermute(joined, axes, swap)
    ready = [*ready, *prepare_cotangent(valid, ct_here)]
    keep, send, *parts = layer([joined, others], ready)
    got = lax.ppermute(send, axes, swap)
    shape = jax.ShapeDtypeStruct((GRAD_ROWS, D), bf16)
    pairs = pl.pallas_call(
        pair_kernel, in_specs=[VMEM] * 2, out_specs=[VMEM] * 4, out_shape=[shape] * 4, compiler_params=SMALL, name="pair",
    )(keep, got)
    pairs, parts = lax.optimization_barrier((pairs, parts))
    layer_out, tokens_grad = results(parts, ready)
    back = [across((BACK[0][k], BACK[1][k])) for k in range(4)]
    came = [lax.ppermute(pairs[k], axes, back[k]) for k in range(4)]
    merged = pl.pallas_call(
        merge_kernel, in_specs=[VMEM] * 5, out_specs=VMEM, out_shape=shape, compiler_params=SMALL, name="merge",
    )(pairs[0], *came)
    beside = lax.ppermute(merged, axes, swap)
    chip = pl.pallas_call(
        chip_kernel, in_specs=[VMEM] * 2, out_specs=VMEM, out_shape=shape, compiler_params=SMALL, name="chip",
    )(merged, beside)
    over = [(g * wide + i, (g ^ 2) * wide + i) for g in range(grp) for i in range(wide)]
    every = [chip, lax.ppermute(chip, axes, over)]
    grads = pl.pallas_call(
        finish_kernel, in_specs=[VMEM] * 2, out_specs=[VMEM] * 13,
        out_shape=[jax.ShapeDtypeStruct(p.shape, f32) for p in params], compiler_params=SMALL, name="finish",
    )(*every)
    return (layer_out, tokens_grad, *grads)


def gathered(tokens, episode_length, window_start, *rest):
    params, cotangent = rest[:13], rest[13]
    D = tokens.shape[2]
    full = [lax.all_gather(p, "wide", axis=0, tiled=True) for p in params]
    gain_a, shift_a, qkv, query, value, outw, outb, gain_m, shift_m, upw, upb, downw, downb = full
    FF = upw.shape[1]
    lanes = jnp.arange(D) // (D // PIECES)
    spots = (lanes[None, :] == jnp.arange(PIECES)[:, None]).astype(bf16)
    vectors = jnp.stack([gain_a, shift_a, query, value, outb, gain_m, shift_m, downb])[None] * spots[:, None, :]
    where_up = (jnp.arange(FF) // (FF // PIECES))[None, :] == jnp.arange(PIECES)[:, None]
    ups = (upb[None] * where_up.astype(bf16)).reshape(PIECES, FF // D, D)

    def blocks(weight):
        cut = weight.reshape(PIECES, weight.shape[0] // PIECES, weight.shape[1] // D, D)
        return cut.transpose(0, 2, 1, 3).reshape(PIECES, -1, D)

    slots = jnp.concatenate(
        [blocks(qkv), blocks(outw), blocks(upw), blocks(downw), vectors, ups, jnp.zeros((PIECES, 4, D), bf16)], 1
    )
    mine, others = [jnp.concatenate([slots[s] for s in half], 0) for half in SLOTS]
    count, span = tokens.shape[:2]
    valid = jnp.broadcast_to(jnp.clip(episode_length - window_start, 1, span)[:, None], (count, D))
    *ready, ct_here = prepare_tokens(tokens, cotangent)
    ready = [*ready, *prepare_cotangent(valid, ct_here)]
    keep, send, *parts = layer([mine, others], ready, spread_out=False)
    layer_out, tokens_grad = results(parts, ready)
    order = [0] * PIECES
    for half in (0, 1):
        for k in range(4):
            order[BACK[half][k]] = 4 * half + k
    pieces = jnp.concatenate([keep, send], 0)[jnp.array(order)].astype(f32)
    vec = pieces[0, 192:208]

    def rebuilt(first, last, weight):
        cut = pieces[:, first:last].reshape(PIECES, weight.shape[1] // D, weight.shape[0] // PIECES, D)
        return cut.transpose(0, 2, 1, 3).reshape(weight.shape)

    grads = (
        vec[0], vec[1], rebuilt(0, 48, qkv), vec[2], vec[3], rebuilt(48, 64, outw), vec[4], vec[5], vec[6],
        rebuilt(64, 128, upw), vec[8:12].reshape(FF), rebuilt(128, 192, downw), vec[7],
    )
    grads = [lax.psum_scatter(g, "wide", scatter_dimension=0, tiled=True) for g in grads]
    return (layer_out, tokens_grad, *lax.psum(grads, "grp"))


def solution(mesh):
    rows = P(("grp", "wide"), None, None)
    flat = P(("grp", "wide"))
    one, two = P("wide"), P("wide", None)
    params = (one, one, two, one, one, two, one, one, one, two, one, two, one)
    fits = mesh.shape["wide"] == PIECES and mesh.shape["grp"] == 4
    return jax.shard_map(
        per_device if fits else gathered, mesh=mesh, in_specs=(rows, flat, flat, *params, rows), out_specs=(rows, rows, *params), check_vma=False
    )
```
